256 devices in a mesh: rans: 64 (over z, y, core), pitch: 2 (over x_hi), span: 2 (over x_lo).
Axes of the slice: x: 4 (x_hi: 2, x_lo: 2; x = x_hi * 2 + x_lo), y: 4, z: 8, core: 2. Of those that a mesh axis runs over, the one named last changes fastest.
Arguments:
- solution: bfloat16 [5, 64, 393216], P(None, None, ('rans', 'pitch', 'span')), may hold values from -6 to 6
- volume_ops: bfloat16 [3, 64, 64], replicated, may hold values from -0.4375 to 0.4375
- flux_jacobian: float32 [3, 5, 5], replicated, may hold values from -2.5 to 2.5
- lift_matrix: bfloat16 [64, 96], replicated, may hold values from -1.5 to 1.5
- filter_matrix: bfloat16 [64, 64], replicated
- wall_matrix: bfloat16 [64, 64], replicated, may hold values from -0.75 to 0.75
- pinched_map: int32 [393216], P(('rans', 'pitch', 'span')), may hold values from 0 to 1, as said below
- mode_rows: int32 [2, 2, 16384, 64], P('pitch', 'span', 'rans'), may hold values from 0 to 2047
- mode_seeds: int32 [2, 2, 16384], P('pitch', 'span', 'rans'), may hold values from 0 to 31
- mode_shape: float32 [2, 2, 16384, 64], P('pitch', 'span', 'rans'), may hold values from 0.2 to 1
- mean_inflow: float32 [2, 2, 5, 2048], P('pitch', 'span'), may hold values from -6 to 6
- eddy_amplitude: float32 [2, 2, 5, 2048], P('pitch', 'span'), may hold values from 0.3 to 3
Outputs:
- new_solution: bfloat16 [5, 64, 393216], P(None, None, ('rans', 'pitch', 'span'))
The draws below stay inside these ranges and needn't reach their ends.
Inputs may be any that keep to these rules, and one draw needn't show every extreme that they name: pinched_map is 1 only for elements in the last 4 element layers of the whole domain along span, hence only on devices with the last span index; one device holds at most 192 ones, and some devices hold exactly 192.
All inputs are finite; a program needn't handle non-finite values.
Results may differ from the reference program's by a relative error of at most 0.0042.
The reference program's roundings to bfloat16 on the way count: a program that leaves them out, or rounds other values in their place, can miss the bound.
Values may be sent and summed in bfloat16 or wider, within the bound.
No kernel may reach another device: no remote copies, remote signals or barrier semaphores. Data moves between devices by JAX's collectives and lax.ppermute only.
A program may use at most 128 MiB of HBM per device.

```python
import math
import jax
import jax.numpy as jnp
from jax import lax

FIELDS = 5
NODES = 64
FACE = 16
EX = 12
EY = 4
EZ = 32
TIP = 4
FOOT = 64
ELEMENTS = 393216
PLANE = 2048
MODES = 16384
N_RANS = 64
N_PITCH = 2
N_SPAN = 2


def draw_filter_matrix(key, part):
    key = jax.random.fold_in(key, 11)
    diag_key, off_key = jax.random.split(key)
    row_index = jnp.arange(64)[:, None]
    col_index = jnp.arange(64)[None, :]
    diagonal = jax.random.uniform(diag_key, (64, 64), jnp.float32, 0.7, 1.0)
    spread = 0.04 * jax.random.normal(off_key, (64, 64), jnp.float32)
    return jnp.where(row_index == col_index, diagonal, spread).astype(jnp.bfloat16)


def draw_pinched_map(key, part):
    key = jax.random.fold_in(key, 23)
    band_key, depth_key = jax.random.split(key)
    blade_band = jax.random.randint(band_key, (), 0, N_PITCH)
    pinch_depth = jax.random.randint(depth_key, (EX * N_RANS, EY * N_PITCH), 0, TIP + 1)
    column_pitch = jnp.arange(EY * N_PITCH)[None, :] // EY
    pinch_depth = jnp.where(column_pitch == blade_band, TIP, pinch_depth)
    span_layer = jnp.arange(EZ * N_SPAN)
    pinch_grid = (span_layer[None, None, :] >= EZ * N_SPAN - pinch_depth[:, :, None]).astype(jnp.int32)
    pinch_grid = pinch_grid.reshape(N_RANS, EX, N_PITCH, EY, N_SPAN, EZ).transpose(0, 2, 4, 1, 3, 5)
    return pinch_grid.reshape(-1)


def place_ends(drawn, rng, smallest, largest):
    dims = drawn.shape
    index_at = [jax.random.randint(jax.random.fold_in(rng, axis), (), 0, dims[axis]) for axis in range(len(dims))]
    drawn = drawn.at[tuple(index_at)].set(smallest)
    longest = dims.index(max(dims))
    index_at[longest] = (index_at[longest] + 1) % dims[longest]
    return drawn.at[tuple(index_at)].set(largest)


def block_scale(stream_key, shape, cuts, least, largest):
    def one(dim, shards_of):
        steps = jax.random.uniform(jax.random.fold_in(jax.random.fold_in(stream_key, 6), dim), (shards_of,), jnp.float32, least / len(cuts), largest / len(cuts))
        return jnp.repeat(jnp.exp(steps), shape[dim] // shards_of).reshape((-1,) + (1,) * (len(shape) - dim - 1))

    level = one(*cuts[0])
    for cut in cuts[1:]:
        level = level * one(*cut)
    return level


def bell_draw(stream_key, dims, scale, bound, shards=(), held_as=jnp.bfloat16):
    result = jax.random.normal(stream_key, dims, jnp.float32) * scale
    if len(shards) > 0:
        result = block_scale(stream_key, dims, shards, -0.22, 0.18) * result
    return jnp.clip(result, min=-bound, max=bound).astype(held_as)


def setup_inputs(seed: int = 0) -> dict:
    key_list = jax.random.split(jax.random.key(seed), 13)
    solution = bell_draw(key_list[0], (FIELDS, NODES, ELEMENTS), 1.0, 6.0, ((2, 256),))
    volume_ops = bell_draw(key_list[1], (3, NODES, NODES), (3 * NODES) ** -0.5, 0.4375)
    flux_jacobian = bell_draw(key_list[2], (3, FIELDS, FIELDS), FIELDS ** -0.5, 2.5, (), jnp.float32)
    lift_matrix = bell_draw(key_list[3], (NODES, 6 * FACE), FACE ** -0.5, 1.5)
    filter_matrix = draw_filter_matrix(jax.random.fold_in(key_list[12], 71), 0)
    wall_matrix = bell_draw(key_list[5], (NODES, NODES), NODES ** -0.5, 0.75)
    pinched_map = draw_pinched_map(jax.random.fold_in(key_list[12], 71), 0)
    mode_rows = place_ends(jax.random.randint(key_list[7], (N_PITCH, N_SPAN, MODES, FOOT), 0, PLANE), jax.random.fold_in(key_list[7], 1), 0, PLANE - 1).astype(jnp.int32)
    mode_seeds = place_ends(jax.random.randint(key_list[8], (N_PITCH, N_SPAN, MODES), 0, 32), jax.random.fold_in(key_list[8], 1), 0, 31).astype(jnp.int32)
    mode_shape = jnp.clip(0.2 + 0.8 * jax.random.uniform(key_list[9], (N_PITCH, N_SPAN, MODES, FOOT), jnp.float32) ** block_scale(key_list[9], (N_PITCH, N_SPAN, MODES, FOOT), ((0, 2), (1, 2), (2, 64)), -0.2, 0.2), 0.2, 1.0)
    mean_inflow = bell_draw(key_list[10], (N_PITCH, N_SPAN, FIELDS, PLANE), 1.0, 6.0, ((0, 2), (1, 2)), jnp.float32)
    eddy_amplitude = jnp.clip(jnp.exp(math.log(3.0) - 2.3025851 * jax.random.uniform(key_list[11], (N_PITCH, N_SPAN, FIELDS, PLANE), jnp.float32) ** block_scale(key_list[11], (N_PITCH, N_SPAN, FIELDS, PLANE), ((0, 2), (1, 2)), -0.2, 0.2)), 0.3, 3.0)
    return dict(solution=solution, volume_ops=volume_ops, flux_jacobian=flux_jacobian, lift_matrix=lift_matrix, filter_matrix=filter_matrix, wall_matrix=wall_matrix, pinched_map=pinched_map, mode_rows=mode_rows, mode_seeds=mode_seeds, mode_shape=mode_shape, mean_inflow=mean_inflow, eddy_amplitude=eddy_amplitude)


time_step = 0.4
upwind_speed = 1.0
highest = lax.Precision.HIGHEST


def face_term(flux_jacobian, direction, normal_sign, inner_trace, outer_trace):
    identity = jnp.eye(5, dtype=jnp.float32)
    matrix = 0.5 * normal_sign * flux_jacobian[direction] - 0.5 * upwind_speed * identity
    difference = outer_trace.astype(jnp.float32) - inner_trace.astype(jnp.float32)
    mixed_jump = jnp.einsum("fh,h...->f...", matrix, difference, precision=highest)
    return mixed_jump.reshape(5, 16, -1)


def take_layer(whole_field, layer_index):
    zero_index = jnp.zeros((), jnp.int32)
    starts = (zero_index, zero_index, (layer_index // EX).astype(jnp.int32), zero_index, zero_index,
              (layer_index % EX).astype(jnp.int32), zero_index, zero_index)
    layer_piece = lax.dynamic_slice(whole_field, starts, (5, 64, 1, N_PITCH, N_SPAN, 1, EY, EZ))
    layer_piece = layer_piece.reshape(5, 64, N_PITCH, N_SPAN, EY, EZ).transpose(0, 1, 2, 4, 3, 5)
    return layer_piece.reshape(5, 4, 4, 4, N_PITCH * EY, N_SPAN * EZ)


def put_layer(whole_field, layer_values, layer_index):
    zero_index = jnp.zeros((), jnp.int32)
    layer_piece = layer_values.reshape(5, 64, N_PITCH, EY, N_SPAN, EZ).transpose(0, 1, 2, 4, 3, 5)
    layer_piece = layer_piece.reshape(5, 64, 1, N_PITCH, N_SPAN, 1, EY, EZ)
    starts = (zero_index, zero_index, (layer_index // EX).astype(jnp.int32), zero_index, zero_index,
              (layer_index % EX).astype(jnp.int32), zero_index, zero_index)
    return lax.dynamic_update_slice(whole_field, layer_piece, starts)


def take_pins(pinned, layer_index):
    zero_index = jnp.zeros((), jnp.int32)
    starts = ((layer_index // EX).astype(jnp.int32), zero_index, zero_index,
              (layer_index % EX).astype(jnp.int32), zero_index, zero_index)
    layer_piece = lax.dynamic_slice(pinned, starts, (1, N_PITCH, N_SPAN, 1, EY, EZ))
    return layer_piece.reshape(N_PITCH, N_SPAN, EY, EZ).transpose(0, 2, 1, 3).reshape(-1)


def layer_rate(current, layer_below, layer_above, layer_index, inflow, pinned_layer,
               volume_ops, flux_jacobian, lift_matrix, wall_matrix):
    last_layer = EX * N_RANS - 1
    lower_edge = jnp.where(layer_index == 0, inflow, layer_below[:, 3].astype(jnp.float32))
    upper_edge = jnp.where(layer_index == last_layer, current[:, 3], layer_above[:, 0])
    face_jumps = jnp.concatenate([
        face_term(flux_jacobian, 0, -1.0, current[:, 0], lower_edge),
        face_term(flux_jacobian, 0, 1.0, current[:, 3], upper_edge),
        face_term(flux_jacobian, 1, -1.0, current[:, :, 0], jnp.roll(current[:, :, 3], 1, axis=3)),
        face_term(flux_jacobian, 1, 1.0, current[:, :, 3], jnp.roll(current[:, :, 0], -1, axis=3)),
        face_term(flux_jacobian, 2, -1.0, current[:, :, :, 0],
                  jnp.concatenate([current[:, :, :, 0, :, :1], current[:, :, :, 3, :, :-1]], axis=4)),
        face_term(flux_jacobian, 2, 1.0, current[:, :, :, 3],
                  jnp.concatenate([current[:, :, :, 0, :, 1:], current[:, :, :, 3, :, -1:]], axis=4)),
    ], axis=1).astype(jnp.bfloat16)
    flat_layer = current.reshape(5, 64, -1).astype(jnp.float32)
    fluxes = jnp.einsum("dfg,gne->dfne", flux_jacobian, flat_layer, precision=highest).astype(jnp.bfloat16)
    volume = jnp.einsum("dnm,dfme->fne", volume_ops.astype(jnp.float32), fluxes.astype(jnp.float32), precision=highest)
    surface = jnp.einsum("nq,fqe->fne", lift_matrix.astype(jnp.float32), face_jumps.astype(jnp.float32), precision=highest)
    wall_term = jnp.einsum("nm,fme->fne", wall_matrix.astype(jnp.float32), flat_layer, precision=highest)
    wall_term = wall_term * pinned_layer.astype(jnp.float32)
    return -(volume + surface + wall_term)


def run_phase(source, base_field, inflow, pinned, volume_ops, flux_jacobian, lift_matrix,
              wall_matrix, filter_matrix, averaged):
    last_layer = EX * N_RANS - 1

    def layer_step(buffer, layer_index):
        current = take_layer(source, layer_index)
        layer_below = take_layer(source, jnp.maximum(layer_index - 1, 0))
        layer_above = take_layer(source, jnp.minimum(layer_index + 1, last_layer))
        pinned_layer = take_pins(pinned, layer_index)
        rate_now = layer_rate(current, layer_below, layer_above, layer_index, inflow, pinned_layer,
                              volume_ops, flux_jacobian, lift_matrix, wall_matrix)
        flat_now = current.reshape(5, 64, -1).astype(jnp.float32)
        if averaged:
            base_now = take_layer(base_field, layer_index).reshape(5, 64, -1).astype(jnp.float32)
            trial_layer = (0.5 * (base_now + flat_now + time_step * rate_now)).astype(jnp.bfloat16)
        else:
            trial_layer = (flat_now + time_step * rate_now).astype(jnp.bfloat16)
        filtered = jnp.einsum("nm,fme->fne", filter_matrix.astype(jnp.float32), trial_layer.astype(jnp.float32),
                              precision=highest).astype(jnp.bfloat16)
        return put_layer(buffer, filtered, layer_index), None

    buffer, unused = lax.scan(layer_step, jnp.zeros_like(source), jnp.arange(EX * N_RANS, dtype=jnp.int32))
    return buffer


def reference(solution, volume_ops, flux_jacobian, lift_matrix, filter_matrix, wall_matrix, pinched_map,
              mode_rows, mode_seeds, mode_shape, mean_inflow, eddy_amplitude):
    powers = 2 ** jnp.arange(5, dtype=jnp.int32)
    parity = (mode_seeds[:, :, None, :] // powers[None, None, :, None]) % 2
    mode_signs = (2 * parity - 1).astype(jnp.float32)
    normalizer = (PLANE / (MODES * FOOT)) ** 0.5
    contrib = mode_signs[:, :, :, :, None] * mode_shape[:, :, None, :, :] * normalizer

    def plane_of(values, rows_here):
        return jax.ops.segment_sum(values.reshape(5, -1).T, rows_here.reshape(-1), num_segments=PLANE).T

    fluctuation = jax.vmap(jax.vmap(plane_of))(contrib, mode_rows)
    inflow = mean_inflow + eddy_amplitude * fluctuation
    inflow = inflow.reshape(N_PITCH, N_SPAN, 5, 4, 4, EY, EZ).transpose(2, 3, 4, 0, 5, 1, 6)
    inflow = inflow.reshape(5, 4, 4, N_PITCH * EY, N_SPAN * EZ)
    pinned = pinched_map.reshape(N_RANS, N_PITCH, N_SPAN, EX, EY, EZ)
    source_field = solution.reshape(5, 64, N_RANS, N_PITCH, N_SPAN, EX, EY, EZ)
    phase_one = run_phase(source_field, source_field, inflow, pinned, volume_ops, flux_jacobian,
                          lift_matrix, wall_matrix, filter_matrix, False)
    result_field = run_phase(phase_one, source_field, inflow, pinned, volume_ops, flux_jacobian,
                             lift_matrix, wall_matrix, filter_matrix, True)
    return result_field.reshape(5, 64, -1)
```

```python
import functools

import jax
import jax.numpy as jnp
import numpy as np
from jax import lax
from jax.experimental import pallas as pl
from jax.experimental.pallas import tpu as pltpu
from jax.sharding import PartitionSpec as P

FIELDS = 5
NODES = 64
EX = 12
CELLS = 128
SPAN_CELLS = 32
PAIR = 2 * CELLS
MIXED = 352
TIME_STEP = 0.4
f32 = jnp.float32
bf16 = jnp.bfloat16


def trace_selector():
    pick = np.zeros((64, 64), np.float32)
    for first in range(4):
        for second in range(4):
            w = 4 * first + second
            pick[w, 16 * first + second] = 1
            pick[16 + w, 16 * first + 12 + second] = 1
            pick[32 + w, 16 * first + 4 * second] = 1
            pick[48 + w, 16 * first + 4 * second + 3] = 1
    return jnp.asarray(pick, bf16)


def dot(a, b):
    return jnp.dot(a, b, preferred_element_type=f32)


def lanes():
    return lax.broadcasted_iota(jnp.int32, (16, CELLS), 1)


def plane_kernel(rows_ref, seeds_ref, shape_ref, plane_ref, rows_t, shape_t, *, normalizer):
    rows_t[...] = rows_ref[...].T
    shape_t[...] = shape_ref[...].T
    seeds = seeds_ref[...]
    signs = [(2 * ((seeds >> f) & 1) - 1).astype(f32) for f in range(FIELDS)]
    signs = [jnp.broadcast_to(s, (32, s.shape[1])).astype(bf16) for s in signs]
    eddies = rows_ref.shape[0]
    high_row = lax.broadcasted_iota(jnp.int32, (16, eddies), 0)
    low_row = lax.broadcasted_iota(jnp.int32, (CELLS, eddies), 0)

    def chunk(i, total):
        start = pl.multiple_of(i * 8, 8)
        rows = rows_t[pl.ds(start, 8), :]
        shapes = shape_t[pl.ds(start, 8), :]
        for q in range(8):
            row, shape = rows[q : q + 1], shapes[q : q + 1]
            placed = jnp.where((row >> 7) == high_row, shape, 0.0)
            coarse = placed.astype(bf16)
            fine = (placed - coarse.astype(f32)).astype(bf16)
            both = jnp.concatenate([coarse, fine], axis=0)
            signed = jnp.concatenate([both * s for s in signs], axis=0)
            hot = jnp.where((row & 127) == low_row, 1.0, 0.0).astype(bf16)
            total = total + lax.dot_general(
                signed, hot, (((1,), (1,)), ((), ())), preferred_element_type=f32
            )
        return total

    total = lax.fori_loop(0, rows_ref.shape[1] // 8, chunk, jnp.zeros((160, CELLS), f32))
    for f in range(FIELDS):
        plane_ref[f] = (total[32 * f : 32 * f + 16] + total[32 * f + 16 : 32 * f + 32]) * normalizer


def pack_pitch(traces, lane):
    (low0, high0), (low1, high1) = traces
    return jnp.where(
        lane < 32,
        low0,
        jnp.where(
            lane < 64,
            pltpu.roll(low1, 32, 1),
            jnp.where(lane < 96, pltpu.roll(high0, 96, 1), high1),
        ),
    )


def pack_span(held, low, high, layer, first_span, lane):
    edge = jnp.where(first_span, high, low)
    shift = lax.rem(layer + jnp.where(first_span, 97, 0), 128)
    return jnp.where((lane & 31) == layer, pltpu.roll(edge, shift, 1), held)


def pack_pair(values, pair, pick, first_span, lane, pitch_ref, span_held):
    for f in range(FIELDS):
        trace = dot(pick, values[f])
        halves = [trace[:, :CELLS], trace[:, CELLS:]]
        packed = pack_pitch([(h[0:16], h[16:32]) for h in halves], lane)
        at = pl.multiple_of(pair * CELLS, CELLS)
        pitch_ref[f, :, pl.ds(at, CELLS)] = packed.astype(bf16)
        held = span_held[f]
        for h in range(2):
            held = pack_span(
                held, halves[h][32:48], halves[h][48:64], 2 * pair + h, first_span, lane
            )
        span_held[f] = held


def pack_kernel(v_ref, pick_ref, up_ref, down_ref, pitch_ref, span_ref, span_held):
    first_span = lax.axis_index("span") == 0
    lane = lanes()
    pick = pick_ref[...]
    span_held[...] = jnp.zeros_like(span_held)

    def step(pair, _):
        at = pl.multiple_of(pair * PAIR, PAIR)
        values = [v_ref[f, :, pl.ds(at, PAIR)] for f in range(FIELDS)]
        pack_pair(values, pair, pick, first_span, lane, pitch_ref, span_held)
        return 0

    lax.fori_loop(0, EX // 2, step, 0)
    span_ref[...] = span_held[...].astype(bf16)
    up_ref[...] = v_ref[:, 48:64, (EX - 1) * CELLS :]
    down_ref[...] = v_ref[:, 0:16, 0:CELLS]


def mix(coefs, base, arrays):
    total = coefs[base] * arrays[0]
    for g in range(1, FIELDS):
        total = total + coefs[base + g] * arrays[g]
    return total


def advance(
    width, read, lower, upper, pitch, span, pinned, layers, coefs, weights, pick, smooth, mixed,
    first_span, lane, base=None,
):
    for r in range(0, NODES, 16):
        rows = [read(f, r, r + 16).astype(f32) for f in range(FIELDS)]
        for d in range(3):
            for f in range(FIELDS):
                mixed[f, 64 * d + r : 64 * d + r + 16, 0:width] = mix(
                    coefs, 25 * d + 5 * f, rows
                ).astype(bf16)
    jumps = [[None] * FIELDS for _ in range(6)]
    for f in range(FIELDS):
        jumps[0][f] = lower(f) - read(f, 0, 16).astype(f32)
        jumps[1][f] = upper(f) - read(f, 48, 64).astype(f32)
        trace = dot(pick, read(f, 0, 64))
        near, far = pitch(f), span(f)
        parts = [[], [], [], []]
        for h, layer in enumerate(layers):
            t = trace[:, h * CELLS : (h + 1) * CELLS]
            pl_low, pl_high, sp_low, sp_high = t[0:16], t[16:32], t[32:48], t[48:64]
            below = jnp.where(
                lane < 32, pltpu.roll(near, 64 if h == 0 else 32, 1), pltpu.roll(pl_high, 32, 1)
            )
            above = jnp.where(
                lane >= 96, pltpu.roll(near, 96 if h == 0 else 64, 1), pltpu.roll(pl_low, 96, 1)
            )
            shift = lax.rem(jnp.where(first_span, 31, 128) - layer, 128)
            arrived = pltpu.roll(far, shift, 1)
            left = jnp.where(
                (lane & 31) == 0, jnp.where(first_span, sp_low, arrived), pltpu.roll(sp_high, 1, 1)
            )
            right = jnp.where(
                (lane & 31) == 31,
                jnp.where(first_span, arrived, sp_high),
                pltpu.roll(sp_low, 127, 1),
            )
            for held, now in zip(
                parts, (below - pl_low, above - pl_high, left - sp_low, right - sp_high)
            ):
                held.append(now)
        for t in range(4):
            p = parts[t]
            jumps[2 + t][f] = p[0] if len(p) == 1 else jnp.concatenate(p, axis=1)
    for t in range(6):
        for f in range(FIELDS):
            mixed[f, 192 + 16 * t : 208 + 16 * t, 0:width] = mix(
                coefs, 75 + 25 * t + 5 * f, jumps[t]
            ).astype(bf16)
    out = []
    for f in range(FIELDS):
        v = read(f, 0, 64).astype(f32)
        mixed[f, 288:352, 0:width] = (v * pinned).astype(bf16)
        rate = dot(weights, mixed[f, :, 0:width])
        if base is None:
            trial = v - TIME_STEP * rate
        else:
            trial = 0.5 * (base(f).astype(f32) + v - TIME_STEP * rate)
        out.append(dot(smooth, trial.astype(bf16)).astype(bf16))
    return out


def fill_stream(v_ref, from_below, from_above, lower_all, upper_all):
    rans = lax.axis_index("rans")
    last = rans == lax.axis_size("rans") - 1
    lower_all[:, :, CELLS:] = v_ref[:, 48:64, : (EX - 1) * CELLS]
    lower_all[:, :, :CELLS] = from_below[...]
    upper_all[:, :, : (EX - 1) * CELLS] = v_ref[:, 0:16, CELLS:]
    edge = v_ref[:, 48:64, (EX - 1) * CELLS :]
    upper_all[:, :, (EX - 1) * CELLS :] = jnp.where(last, edge, from_above[...])


def phase_kernel(
    *refs, second
):
    if second:
        (v_ref, base_ref, below_ref, above_ref, near_ref, far_ref, pin_ref, coefs, weights_ref,
         pick_ref, smooth_ref, out_ref, mixed, lower_all, upper_all) = refs
    else:
        (v_ref, below_ref, above_ref, near_ref, far_ref, pin_ref, coefs, weights_ref, pick_ref,
         smooth_ref, out_ref, up_ref, down_ref, pitch_ref, span_ref, mixed, lower_all, upper_all,
         span_held) = refs
    first_span = lax.axis_index("span") == 0
    lane = lanes()
    fill_stream(v_ref, below_ref, above_ref, lower_all, upper_all)
    pick, weights, smooth = pick_ref[...], weights_ref[...], smooth_ref[...]
    if not second:
        span_held[...] = jnp.zeros_like(span_held)

    def step(pair, _):
        at = pl.ds(pl.multiple_of(pair * PAIR, PAIR), PAIR)
        near_at = pl.ds(pl.multiple_of(pair * CELLS, CELLS), CELLS)
        values = advance(
            PAIR,
            lambda f, r0, r1: v_ref[f, r0:r1, at],
            lambda f: lower_all[f, :, at].astype(f32),
            lambda f: upper_all[f, :, at].astype(f32),
            lambda f: near_ref[f, :, near_at].astype(f32),
            lambda f: far_ref[f].astype(f32),
            pin_ref[:, at].astype(f32),
            [2 * pair, 2 * pair + 1],
            coefs, weights, pick, smooth, mixed, first_span, lane,
            base=(lambda f: base_ref[f, :, at]) if second else None,
        )
        for f in range(FIELDS):
            out_ref[f, :, at] = values[f]
        if not second:
            pack_pair(values, pair, pick, first_span, lane, pitch_ref, span_held)
        return 0

    lax.fori_loop(0, EX // 2, step, 0)
    if not second:
        span_ref[...] = span_held[...].astype(bf16)
        up_ref[...] = out_ref[:, 48:64, (EX - 1) * CELLS :]
        down_ref[...] = out_ref[:, 0:16, 0:CELLS]


def inflow_of(mean_ref, amp_ref, plane_ref):
    return lambda f: mean_ref[f] + amp_ref[f] * plane_ref[f]


def first_fix_kernel(
    v_ref, mean_ref, amp_ref, plane_ref, near_ref, far_ref, pin_ref, coefs, weights_ref, pick_ref,
    smooth_ref, out_ref, pitch_ref, span_ref, mixed,
):
    first_span = lax.axis_index("span") == 0
    lane = lanes()

    @pl.when(lax.axis_index("rans") == 0)
    def _():
        pick = pick_ref[...]
        values = advance(
            CELLS,
            lambda f, r0, r1: v_ref[f, r0:r1, 0:CELLS],
            inflow_of(mean_ref, amp_ref, plane_ref),
            lambda f: v_ref[f, 0:16, CELLS:PAIR].astype(f32),
            lambda f: near_ref[f, :, 0:CELLS].astype(f32),
            lambda f: far_ref[f].astype(f32),
            pin_ref[:, 0:CELLS].astype(f32),
            [0],
            coefs, weights_ref[...], pick, smooth_ref[...], mixed, first_span, lane,
        )
        for f in range(FIELDS):
            out_ref[f] = values[f]
            t = dot(pick, values[f])
            pitch_ref[f] = jnp.where(lane < 32, t[0:16], pltpu.roll(t[16:32], 96, 1)).astype(bf16)
            span_ref[f] = pack_span(
                jnp.zeros((16, CELLS), f32), t[32:48], t[48:64], 0, first_span, lane
            ).astype(bf16)


def second_fix_kernel(
    held_ref, base_ref, v0_ref, v_ref, mean_ref, amp_ref, plane_ref, near0_ref, far0_ref, near_ref,
    far_ref, pin_ref, coefs, weights_ref, pick_ref, smooth_ref, out_ref, mixed, joined,
):
    first_span = lax.axis_index("span") == 0
    lane = lanes()
    first_rans = lax.axis_index("rans") == 0

    @pl.when(first_rans)
    def _():
        joined[:, :, 0:CELLS] = v0_ref[...]
        joined[:, :, CELLS:] = v_ref[:, :, CELLS : 3 * CELLS]
        inflow = inflow_of(mean_ref, amp_ref, plane_ref)

        def near(f):
            return jnp.where(
                (lane & 63) < 32, near0_ref[f].astype(f32), near_ref[f, :, 0:CELLS].astype(f32)
            )

        def far(f):
            return jnp.where((lane & 31) == 0, far0_ref[f].astype(f32), far_ref[f].astype(f32))

        values = advance(
            PAIR,
            lambda f, r0, r1: joined[f, r0:r1, 0:PAIR],
            lambda f: jnp.concatenate(
                [inflow(f), joined[f, 48:64, 0:CELLS].astype(f32)], axis=1
            ),
            lambda f: joined[f, 0:16, CELLS : 3 * CELLS].astype(f32),
            near,
            far,
            pin_ref[:, 0:PAIR].astype(f32),
            [0, 1],
            coefs, weights_ref[...], pick_ref[...], smooth_ref[...], mixed, first_span, lane,
            base=lambda f: base_ref[f],
        )
        for f in range(FIELDS):
            out_ref[f] = values[f]

    @pl.when(jnp.logical_not(first_rans))
    def _():
        out_ref[...] = held_ref[...]


VMEM = pl.BlockSpec(memory_space=pltpu.VMEM)
SMEM = pl.BlockSpec(memory_space=pltpu.SMEM)
PARAMS = pltpu.CompilerParams(vmem_limit_bytes=40 * 2**20)


def shape_of(*dims, dtype=bf16):
    return jax.ShapeDtypeStruct(dims, dtype)


def front(*dims):
    return pl.BlockSpec(dims, lambda i: (0,) * len(dims))


def cost(us):
    return pl.CostEstimate(flops=int(us * 1e8), bytes_accessed=int(us * 3e6), transcendentals=0)


def body(
    solution, volume_ops, flux_jacobian, lift_matrix, filter_matrix, wall_matrix, pinched_map,
    mode_rows, mode_seeds, mode_shape, mean_inflow, eddy_amplitude,
):
    ranks = lax.axis_size("rans")
    eddies, foot = mode_shape.shape[2:]
    plane_rows = mean_inflow.shape[3]
    faces = shape_of(FIELDS, 16, CELLS)
    pick = trace_selector()

    plane = pl.pallas_call(
        functools.partial(
            plane_kernel, normalizer=float((plane_rows / (eddies * ranks * foot)) ** 0.5)
        ),
        out_shape=shape_of(FIELDS, 16, CELLS, dtype=f32),
        in_specs=[VMEM] * 3,
        out_specs=VMEM,
        scratch_shapes=[pltpu.VMEM((foot, eddies), jnp.int32), pltpu.VMEM((foot, eddies), f32)],
        compiler_params=PARAMS,
        cost_estimate=cost(4),
        name="eddy_plane",
    )(mode_rows.reshape(eddies, foot), mode_seeds.reshape(1, eddies), mode_shape.reshape(eddies, foot))

    def gather_sum(value, offsets, roots):
        parts = [lax.ppermute(value, "rans", [(r + o, r) for r in roots]) for o in offsets]
        for part in parts:
            value = value + part
        return value

    plane = gather_sum(plane, (2, 4, 6), [8 * z + c for z in range(8) for c in range(2)])
    plane = gather_sum(plane, (1, 8, 9), [0, 16, 32, 48])
    plane = gather_sum(plane, (16, 32, 48), [0])

    weights = jnp.concatenate(
        [volume_ops[0], volume_ops[1], volume_ops[2], lift_matrix, wall_matrix], axis=1
    )
    identity = jnp.eye(FIELDS, dtype=f32)
    sides = jnp.array([-1.0, 1.0], f32)
    face_coefs = (
        0.5 * sides[None, :, None, None] * flux_jacobian[:, None] - 0.5 * identity
    ).reshape(-1)
    coefs = jnp.concatenate([flux_jacobian.reshape(-1), face_coefs])
    pins = pinched_map.reshape(1, -1)
    fixed = (pins, coefs, weights, pick, filter_matrix)
    fixed_specs = [VMEM, SMEM, VMEM, VMEM, VMEM]
    elements = solution.shape[2]
    sends = (faces, faces, shape_of(FIELDS, 16, EX // 2 * CELLS), faces)

    def exchange(up, down, pitch, span):
        rise = [(i, i + 1) for i in range(ranks - 1)]
        swap = [(0, 1), (1, 0)]
        return (
            lax.ppermute(up, "rans", rise),
            lax.ppermute(down, "rans", [(b, a) for a, b in rise]),
            lax.ppermute(pitch, "pitch", swap),
            lax.ppermute(span, "span", swap),
        )

    span_scratch = pltpu.VMEM((FIELDS, 16, CELLS), f32)
    sent = pl.pallas_call(
        pack_kernel,
        out_shape=sends,
        in_specs=[VMEM] * 2,
        out_specs=(VMEM,) * 4,
        scratch_shapes=[span_scratch],
        compiler_params=PARAMS,
        cost_estimate=cost(2),
        name="pack_faces",
    )(solution, pick)
    halo_one = exchange(*sent)

    scratch = [
        pltpu.VMEM((FIELDS, MIXED, PAIR), bf16),
        pltpu.VMEM((FIELDS, 16, elements), bf16),
        pltpu.VMEM((FIELDS, 16, elements), bf16),
    ]
    phase_one, *sent = pl.pallas_call(
        functools.partial(phase_kernel, second=False),
        out_shape=(shape_of(*solution.shape),) + sends,
        in_specs=[VMEM] * 5 + fixed_specs,
        out_specs=(VMEM,) * 5,
        scratch_shapes=scratch + [span_scratch],
        compiler_params=PARAMS,
        cost_estimate=cost(8),
        name="phase_one",
    )(solution, *halo_one, *fixed)
    halo_two = exchange(*sent)
    result = pl.pallas_call(
        functools.partial(phase_kernel, second=True),
        out_shape=shape_of(*solution.shape),
        in_specs=[VMEM] * 6 + fixed_specs,
        out_specs=VMEM,
        scratch_shapes=scratch,
        compiler_params=PARAMS,
        cost_estimate=cost(8),
        name="phase_two",
    )(phase_one, solution, *halo_two, *fixed)

    mean = mean_inflow.reshape(FIELDS, 16, CELLS)
    amplitude = eddy_amplitude.reshape(FIELDS, 16, CELLS)
    block = front(FIELDS, NODES, PAIR)
    face_block = front(FIELDS, 16, CELLS)
    fixed_blocks = [front(1, PAIR), SMEM, front(NODES, MIXED), front(64, 64), front(64, 64)]
    edge, *sent = pl.pallas_call(
        first_fix_kernel,
        grid=(1,),
        out_shape=(shape_of(FIELDS, NODES, CELLS), faces, faces),
        in_specs=[block] + [face_block] * 5 + fixed_blocks,
        out_specs=(front(FIELDS, NODES, CELLS), face_block, face_block),
        scratch_shapes=[pltpu.VMEM((FIELDS, MIXED, CELLS), bf16)],
        compiler_params=PARAMS,
        cost_estimate=cost(1),
        name="inflow_phase_one",
    )(solution, mean, amplitude, plane, halo_one[2], halo_one[3], *fixed)
    axes = ("rans", "pitch", "span")
    near0 = lax.ppermute(sent[0], axes, [(0, 2), (2, 0), (1, 3), (3, 1)])
    far0 = lax.ppermute(sent[1], axes, [(0, 1), (1, 0), (2, 3), (3, 2)])
    return pl.pallas_call(
        second_fix_kernel,
        grid=(1,),
        out_shape=shape_of(*solution.shape),
        in_specs=[block, block, front(FIELDS, NODES, CELLS), front(FIELDS, NODES, 3 * CELLS)]
        + [face_block] * 7
        + fixed_blocks,
        out_specs=block,
        scratch_shapes=[
            pltpu.VMEM((FIELDS, MIXED, PAIR), bf16),
            pltpu.VMEM((FIELDS, NODES, 3 * CELLS), bf16),
        ],
        input_output_aliases={0: 0},
        compiler_params=PARAMS,
        cost_estimate=cost(2),
        name="inflow_phase_two",
    )(
        result, solution, edge, phase_one, mean, amplitude, plane, near0, far0, halo_two[2],
        halo_two[3], *fixed,
    )


def solution(mesh):
    spread = P(None, None, ("rans", "pitch", "span"))
    in_specs = (
        spread,
        P(),
        P(),
        P(),
        P(),
        P(),
        P(("rans", "pitch", "span")),
        P("pitch", "span", "rans", None),
        P("pitch", "span", "rans"),
        P("pitch", "span", "rans", None),
        P("pitch", "span", None, None),
        P("pitch", "span", None, None),
    )
    return jax.shard_map(body, mesh=mesh, in_specs=in_specs, out_specs=spread, check_vma=False)
```

```python
import functools

import jax
import jax.numpy as jnp
import numpy as np
from jax import lax
from jax.experimental import pallas as pl
from jax.experimental.pallas import tpu as pltpu
from jax.sharding import PartitionSpec as P

FIELDS = 5
NODES = 64
EX = 12
CELLS = 128
SPAN_CELLS = 32
PAIR = 2 * CELLS
MIXED = 352
TIME_STEP = 0.4
f32 = jnp.float32
bf16 = jnp.bfloat16


def trace_selector():
    pick = np.zeros((64, 64), np.float32)
    for first in range(4):
        for second in range(4):
            w = 4 * first + second
            pick[w, 16 * first + second] = 1
            pick[16 + w, 16 * first + 12 + second] = 1
            pick[32 + w, 16 * first + 4 * second] = 1
            pick[48 + w, 16 * first + 4 * second + 3] = 1
    return jnp.asarray(pick, bf16)


def dot(a, b):
    return jnp.dot(a, b, preferred_element_type=f32)


def lanes():
    return lax.broadcasted_iota(jnp.int32, (16, CELLS), 1)


def plane_kernel(rows_ref, seeds_ref, shape_ref, plane_ref, *, normalizer):
    seeds = seeds_ref[...]
    signs = [(2 * ((seeds >> f) & 1) - 1).astype(f32) for f in range(FIELDS)]
    signs = [jnp.broadcast_to(s, (32, s.shape[1])).astype(bf16) for s in signs]
    eddies = rows_ref.shape[1]
    high_row = lax.broadcasted_iota(jnp.int32, (16, eddies), 0)
    low_row = lax.broadcasted_iota(jnp.int32, (CELLS, eddies), 0)

    def chunk(i, total):
        start = pl.multiple_of(i * 8, 8)
        rows = rows_ref[pl.ds(start, 8), :]
        shapes = shape_ref[pl.ds(start, 8), :]
        for q in range(8):
            row, shape = rows[q : q + 1], shapes[q : q + 1]
            placed = jnp.where((row >> 7) == high_row, shape, 0.0)
            coarse = placed.astype(bf16)
            fine = (placed - coarse.astype(f32)).astype(bf16)
            both = jnp.concatenate([coarse, fine], axis=0)
            signed = jnp.concatenate([both * s for s in signs], axis=0)
            hot = jnp.where((row & 127) == low_row, 1.0, 0.0).astype(bf16)
            total = total + lax.dot_general(
                signed, hot, (((1,), (1,)), ((), ())), preferred_element_type=f32
            )
        return total

    total = lax.fori_loop(0, rows_ref.shape[0] // 8, chunk, jnp.zeros((160, CELLS), f32))
    for f in range(FIELDS):
        plane_ref[f] = (total[32 * f : 32 * f + 16] + total[32 * f + 16 : 32 * f + 32]) * normalizer


def pack_pitch(traces, lane):
    (low0, high0), (low1, high1) = traces
    return jnp.where(
        lane < 32,
        low0,
        jnp.where(
            lane < 64,
            pltpu.roll(low1, 32, 1),
            jnp.where(lane < 96, pltpu.roll(high0, 96, 1), high1),
        ),
    )


def pack_span(held, low, high, layer, first_span, lane):
    edge = jnp.where(first_span, high, low)
    shift = lax.rem(layer + jnp.where(first_span, 97, 0), 128)
    return jnp.where((lane & 31) == layer, pltpu.roll(edge, shift, 1), held)


def pack_pair(traces, pair, first_span, lane, pitch_ref, span_held):
    for f in range(FIELDS):
        halves = [traces[f][:, :CELLS], traces[f][:, CELLS:]]
        packed = pack_pitch([(h[0:16], h[16:32]) for h in halves], lane)
        pitch_ref[f, :, pair * CELLS : (pair + 1) * CELLS] = packed.astype(bf16)
        held = span_held[f]
        for h in range(2):
            held = pack_span(
                held, halves[h][32:48], halves[h][48:64], 2 * pair + h, first_span, lane
            )
        span_held[f] = held


def pack_kernel(
    v_ref, pick_ref, trace_ref, up_ref, down_ref, pitch_ref, span_ref, span_held
):
    first_span = lax.axis_index("span") == 0
    lane = lanes()
    pick = pick_ref[...]
    span_held[...] = jnp.zeros_like(span_held)
    for pair in range(EX // 2):
        at = slice(pair * PAIR, (pair + 1) * PAIR)
        traces = [dot(pick, v_ref[f, :, at]) for f in range(FIELDS)]
        for f in range(FIELDS):
            trace_ref[f, :, at] = traces[f].astype(bf16)
        pack_pair(traces, pair, first_span, lane, pitch_ref, span_held)
    span_ref[...] = span_held[...].astype(bf16)
    up_ref[...] = v_ref[:, 48:64, (EX - 1) * CELLS :]
    down_ref[...] = v_ref[:, 0:16, 0:CELLS]


def mix(coefs, base, arrays):
    total = coefs[base] * arrays[0]
    for g in range(1, FIELDS):
        total = total + coefs[base + g] * arrays[g]
    return total


def advance(
    read, trace, lower, upper, pitch, span, pinned, layers, coefs, weights, smooth, mixed,
    first_span, lane, base=None,
):
    for r in range(0, NODES, 16):
        rows = [read(f, r, r + 16).astype(f32) for f in range(FIELDS)]
        for d in range(3):
            for f in range(FIELDS):
                mixed[f, 64 * d + r : 64 * d + r + 16, :] = mix(
                    coefs, 25 * d + 5 * f, rows
                ).astype(bf16)
    jumps = [[None] * FIELDS for _ in range(6)]
    for f in range(FIELDS):
        jumps[0][f] = lower(f) - read(f, 0, 16).astype(f32)
        jumps[1][f] = upper(f) - read(f, 48, 64).astype(f32)
        own = trace(f).astype(f32)
        near, far = pitch(f), span(f)
        parts = [[], [], [], []]
        for h, layer in enumerate(layers):
            t = own[:, h * CELLS : (h + 1) * CELLS]
            pl_low, pl_high, sp_low, sp_high = t[0:16], t[16:32], t[32:48], t[48:64]
            below = jnp.where(
                lane < 32, pltpu.roll(near, 64 if h == 0 else 32, 1), pltpu.roll(pl_high, 32, 1)
            )
            above = jnp.where(
                lane >= 96, pltpu.roll(near, 96 if h == 0 else 64, 1), pltpu.roll(pl_low, 96, 1)
            )
            shift = lax.rem(jnp.where(first_span, 31, 128) - layer, 128)
            arrived = pltpu.roll(far, shift, 1)
            left = jnp.where(
                (lane & 31) == 0, jnp.where(first_span, sp_low, arrived), pltpu.roll(sp_high, 1, 1)
            )
            right = jnp.where(
                (lane & 31) == 31,
                jnp.where(first_span, arrived, sp_high),
                pltpu.roll(sp_low, 127, 1),
            )
            for held, now in zip(
                parts, (below - pl_low, above - pl_high, left - sp_low, right - sp_high)
            ):
                held.append(now)
        for t in range(4):
            p = parts[t]
            jumps[2 + t][f] = p[0] if len(p) == 1 else jnp.concatenate(p, axis=1)
    for t in range(6):
        for f in range(FIELDS):
            mixed[f, 192 + 16 * t : 208 + 16 * t, :] = mix(
                coefs, 75 + 25 * t + 5 * f, jumps[t]
            ).astype(bf16)
    out = []
    for f in range(FIELDS):
        v = read(f, 0, 64).astype(f32)
        mixed[f, 288:352, :] = (v * pinned).astype(bf16)
        rate = dot(weights, mixed[f])
        if base is None:
            trial = v - TIME_STEP * rate
        else:
            trial = 0.5 * (base(f).astype(f32) + v - TIME_STEP * rate)
        out.append(dot(smooth, trial.astype(bf16)))
    return out


def phase_kernel(*refs, second):
    if second:
        (v_ref, trace_ref, base_ref, mean_ref, amp_ref, plane_ref, below_ref, above_ref, near_ref,
         far_ref, pin_ref, coefs, weights_ref, smooth_ref, out_ref, mixed) = refs
    else:
        (v_ref, trace_ref, below_ref, above_ref, near_ref, far_ref, pin_ref, coefs, weights_ref,
         smooth_ref, out_ref, out_trace_ref, up_ref, down_ref, pitch_ref, span_ref, mixed,
         span_held) = refs
    first_span = lax.axis_index("span") == 0
    rans = lax.axis_index("rans")
    last_rans = rans == lax.axis_size("rans") - 1
    lane = lanes()
    weights, smooth = weights_ref[...], smooth_ref[...]
    if not second:
        span_held[...] = jnp.zeros_like(span_held)

    def lower(f, pair):
        if pair:
            return v_ref[f, 48:64, pair * PAIR - CELLS : (pair + 1) * PAIR - CELLS].astype(f32)
        edge = below_ref[f].astype(f32)
        if second:
            edge = jnp.where(rans == 0, inflow_of(mean_ref, amp_ref, plane_ref)(f), edge)
        return jnp.concatenate([edge, v_ref[f, 48:64, 0:CELLS].astype(f32)], axis=1)

    def upper(f, pair):
        first = pair * PAIR + CELLS
        if pair < EX // 2 - 1:
            return v_ref[f, 0:16, first : first + PAIR].astype(f32)
        edge = jnp.where(
            last_rans, v_ref[f, 48:64, first : first + CELLS].astype(f32), above_ref[f].astype(f32)
        )
        return jnp.concatenate([v_ref[f, 0:16, first : first + CELLS].astype(f32), edge], axis=1)

    for pair in range(EX // 2):
        at = slice(pair * PAIR, (pair + 1) * PAIR)
        values = advance(
            lambda f, r0, r1: v_ref[f, r0:r1, at],
            lambda f: trace_ref[f, :, at],
            lambda f: lower(f, pair),
            lambda f: upper(f, pair),
            lambda f: near_ref[f, :, pair * CELLS : (pair + 1) * CELLS].astype(f32),
            lambda f: far_ref[f].astype(f32),
            pin_ref[:, at].astype(f32),
            [2 * pair, 2 * pair + 1],
            coefs, weights, smooth, mixed.at[pair % mixed.shape[0]], first_span, lane,
            base=(lambda f: base_ref[f, :, at]) if second else None,
        )
        for f in range(FIELDS):
            out_ref[f, :, at] = values[f][0:64].astype(bf16)
        if not second:
            for f in range(FIELDS):
                out_trace_ref[f, :, at] = values[f][64:128].astype(bf16)
            pack_pair(
                [values[f][64:128] for f in range(FIELDS)], pair, first_span, lane, pitch_ref,
                span_held,
            )
    if not second:
        span_ref[...] = span_held[...].astype(bf16)
        up_ref[...] = out_ref[:, 48:64, (EX - 1) * CELLS :]
        down_ref[...] = out_ref[:, 0:16, 0:CELLS]


def inflow_of(mean_ref, amp_ref, plane_ref):
    return lambda f: mean_ref[f] + amp_ref[f] * plane_ref[f]


def inflow_kernel(
    held_ref, held_trace_ref, held_pitch_ref, held_span_ref, v_ref, trace_ref, mean_ref, amp_ref,
    plane_ref, near_ref, far_ref, pin_ref, coefs, weights_ref, smooth_ref, out_ref, out_trace_ref,
    pitch_ref, span_ref, mixed,
):
    first_span = lax.axis_index("span") == 0
    first_rans = lax.axis_index("rans") == 0
    lane = lanes()

    @pl.when(first_rans)
    def _():
        values = advance(
            lambda f, r0, r1: v_ref[f, r0:r1, 0:CELLS],
            lambda f: trace_ref[f],
            inflow_of(mean_ref, amp_ref, plane_ref),
            lambda f: v_ref[f, 0:16, CELLS:PAIR].astype(f32),
            lambda f: near_ref[f].astype(f32),
            lambda f: far_ref[f].astype(f32),
            pin_ref[...].astype(f32),
            [0],
            coefs, weights_ref[...], smooth_ref[...], mixed, first_span, lane,
        )
        for f in range(FIELDS):
            out_ref[f] = values[f][0:64].astype(bf16)
            t = values[f][64:128]
            out_trace_ref[f] = t.astype(bf16)
            pitch = jnp.where(lane < 32, t[0:16], pltpu.roll(t[16:32], 96, 1))
            pitch_ref[f] = jnp.where(
                (lane & 63) < 32, pitch, held_pitch_ref[f].astype(f32)
            ).astype(bf16)
            span_ref[f] = pack_span(
                held_span_ref[f].astype(f32), t[32:48], t[48:64], 0, first_span, lane
            ).astype(bf16)

    @pl.when(jnp.logical_not(first_rans))
    def _():
        out_ref[...] = held_ref[...]
        out_trace_ref[...] = held_trace_ref[...]
        pitch_ref[...] = held_pitch_ref[...]
        span_ref[...] = held_span_ref[...]


VMEM = pl.BlockSpec(memory_space=pltpu.VMEM)
SMEM = pl.BlockSpec(memory_space=pltpu.SMEM)
PARAMS = pltpu.CompilerParams(vmem_limit_bytes=40 * 2**20)
SLOTS = 2


def shape_of(*dims, dtype=bf16):
    return jax.ShapeDtypeStruct(dims, dtype)


def front(*dims):
    return pl.BlockSpec(dims, lambda i: (0,) * len(dims))


def cost(us):
    return pl.CostEstimate(flops=int(us * 1e8), bytes_accessed=int(us * 3e6), transcendentals=0)


def body(
    solution, volume_ops, flux_jacobian, lift_matrix, filter_matrix, wall_matrix, pinched_map,
    mode_rows, mode_seeds, mode_shape, mean_inflow, eddy_amplitude,
):
    ranks = lax.axis_size("rans")
    eddies, foot = mode_shape.shape[2:]
    plane_rows = mean_inflow.shape[3]
    faces = shape_of(FIELDS, 16, CELLS)
    pick = trace_selector()

    plane = pl.pallas_call(
        functools.partial(
            plane_kernel, normalizer=float((plane_rows / (eddies * ranks * foot)) ** 0.5)
        ),
        out_shape=shape_of(FIELDS, 16, CELLS, dtype=f32),
        in_specs=[VMEM] * 3,
        out_specs=VMEM,
        compiler_params=PARAMS,
        cost_estimate=cost(3),
        name="eddy_plane",
    )(mode_rows[0, 0].T, mode_seeds.reshape(1, eddies), mode_shape[0, 0].T)

    def gather_sum(value, offsets, roots):
        parts = [lax.ppermute(value, "rans", [(r + o, r) for r in roots]) for o in offsets]
        for part in parts:
            value = value + part
        return value

    plane = gather_sum(plane, (2, 4, 6), [8 * z + c for z in range(8) for c in range(2)])
    plane = gather_sum(plane, (1, 8, 9), [0, 16, 32, 48])
    plane = gather_sum(plane, (16, 32, 48), [0])

    weights = jnp.concatenate(
        [volume_ops[0], volume_ops[1], volume_ops[2], lift_matrix, wall_matrix], axis=1
    )
    identity = jnp.eye(FIELDS, dtype=f32)
    sides = jnp.array([-1.0, 1.0], f32)
    face_coefs = (
        0.5 * sides[None, :, None, None] * flux_jacobian[:, None] - 0.5 * identity
    ).reshape(-1)
    coefs = jnp.concatenate([flux_jacobian.reshape(-1), face_coefs])
    pins = pinched_map.reshape(1, -1)
    rows = filter_matrix.reshape(4, 4, 4, NODES)
    smooth = jnp.concatenate(
        [filter_matrix]
        + [part.reshape(16, NODES) for part in (rows[:, 0], rows[:, 3], rows[:, :, 0], rows[:, :, 3])]
    )
    fixed_specs = [VMEM, SMEM, VMEM, VMEM]
    elements = solution.shape[2]
    traces = shape_of(FIELDS, NODES, elements)
    sends = (faces, faces, shape_of(FIELDS, 16, EX // 2 * CELLS), faces)
    rise = [(i, i + 1) for i in range(ranks - 1)]
    fall = [(b, a) for a, b in rise]
    swap = [(0, 1), (1, 0)]

    span_scratch = pltpu.VMEM((FIELDS, 16, CELLS), f32)
    trace, up, down, pitch, span = pl.pallas_call(
        pack_kernel,
        out_shape=(traces,) + sends,
        in_specs=[VMEM] * 2,
        out_specs=(VMEM,) * 5,
        scratch_shapes=[span_scratch],
        compiler_params=PARAMS,
        cost_estimate=cost(2),
        name="pack_faces",
    )(solution, pick)
    below = lax.ppermute(up, "rans", rise)
    above = lax.ppermute(down, "rans", fall)
    near = lax.ppermute(pitch, "pitch", swap)
    far = lax.ppermute(span, "span", swap)

    scratch = [pltpu.VMEM((SLOTS, FIELDS, MIXED, PAIR), bf16)]
    phase_one, trace_one, up, down, pitch, span = pl.pallas_call(
        functools.partial(phase_kernel, second=False),
        out_shape=(traces, traces) + sends,
        in_specs=[VMEM] * 6 + fixed_specs,
        out_specs=(VMEM,) * 6,
        scratch_shapes=scratch + [span_scratch],
        compiler_params=PARAMS,
        cost_estimate=cost(6),
        name="phase_one",
    )(solution, trace, below, above, near, far, pins, coefs, weights, smooth)
    below = lax.ppermute(up, "rans", rise)
    above = lax.ppermute(down, "rans", fall)

    mean = mean_inflow.reshape(FIELDS, 16, CELLS)
    amplitude = eddy_amplitude.reshape(FIELDS, 16, CELLS)
    layer = front(FIELDS, NODES, CELLS)
    face = front(FIELDS, 16, CELLS)
    phase_one, trace_one, pitch, span = pl.pallas_call(
        inflow_kernel,
        grid=(1,),
        out_shape=(traces, traces, sends[2], sends[3]),
        in_specs=[layer, layer, face, face, front(FIELDS, NODES, PAIR), layer]
        + [face] * 5
        + [front(1, CELLS), SMEM, front(NODES, MIXED), front(2 * NODES, NODES)],
        out_specs=(layer, layer, face, face),
        scratch_shapes=[pltpu.VMEM((FIELDS, MIXED, CELLS), bf16)],
        input_output_aliases={0: 0, 1: 1, 2: 2, 3: 3},
        compiler_params=PARAMS,
        cost_estimate=cost(1),
        name="inflow_layer",
    )(
        phase_one, trace_one, pitch, span, solution, trace, mean, amplitude, plane, near, far,
        pins, coefs, weights, smooth,
    )
    near = lax.ppermute(pitch, "pitch", swap)
    far = lax.ppermute(span, "span", swap)
    return pl.pallas_call(
        functools.partial(phase_kernel, second=True),
        out_shape=traces,
        in_specs=[VMEM] * 10 + fixed_specs,
        out_specs=VMEM,
        scratch_shapes=scratch,
        compiler_params=PARAMS,
        cost_estimate=cost(6),
        name="phase_two",
    )(
        phase_one, trace_one, solution, mean, amplitude, plane, below, above, near, far, pins,
        coefs, weights, filter_matrix,
    )


def solution(mesh):
    spread = P(None, None, ("rans", "pitch", "span"))
    in_specs = (
        spread,
        P(),
        P(),
        P(),
        P(),
        P(),
        P(("rans", "pitch", "span")),
        P("pitch", "span", "rans", None),
        P("pitch", "span", "rans"),
        P("pitch", "span", "rans", None),
        P("pitch", "span", None, None),
        P("pitch", "span", None, None),
    )
    return jax.shard_map(body, mesh=mesh, in_specs=in_specs, out_specs=spread, check_vma=False)
```

```python
import functools

import jax
import jax.numpy as jnp
import numpy as np
from jax import lax
from jax.experimental import pallas as pl
from jax.experimental.pallas import tpu as pltpu
from jax.sharding import PartitionSpec as P

FIELDS = 5
NODES = 64
EX = 12
CELLS = 128
SPAN_CELLS = 32
PAIR = 2 * CELLS
MIXED = 352
INNER = 224
TIME_STEP = 0.4
f32 = jnp.float32
bf16 = jnp.bfloat16


def trace_selector():
    pick = np.zeros((64, 64), np.float32)
    for first in range(4):
        for second in range(4):
            w = 4 * first + second
            pick[w, 16 * first + second] = 1
            pick[16 + w, 16 * first + 12 + second] = 1
            pick[32 + w, 16 * first + 4 * second] = 1
            pick[48 + w, 16 * first + 4 * second + 3] = 1
    return jnp.asarray(pick, bf16)


def dot(a, b):
    return jnp.dot(a, b, preferred_element_type=f32)


def lanes():
    return lax.broadcasted_iota(jnp.int32, (16, CELLS), 1)


def plane_kernel(rows_ref, seeds_ref, shape_ref, plane_ref, *, normalizer):
    seeds = seeds_ref[...]
    signs = [(2 * ((seeds >> f) & 1) - 1).astype(f32) for f in range(FIELDS)]
    signs = [jnp.broadcast_to(s, (32, s.shape[1])).astype(bf16) for s in signs]
    eddies = rows_ref.shape[1]
    high_row = lax.broadcasted_iota(jnp.int32, (16, eddies), 0)
    low_row = lax.broadcasted_iota(jnp.int32, (CELLS, eddies), 0)

    def chunk(i, total):
        start = pl.multiple_of(i * 8, 8)
        rows = rows_ref[pl.ds(start, 8), :]
        shapes = shape_ref[pl.ds(start, 8), :]
        for q in range(8):
            row, shape = rows[q : q + 1], shapes[q : q + 1]
            placed = jnp.where((row >> 7) == high_row, shape, 0.0)
            coarse = placed.astype(bf16)
            fine = (placed - coarse.astype(f32)).astype(bf16)
            both = jnp.concatenate([coarse, fine], axis=0)
            signed = jnp.concatenate([both * s for s in signs], axis=0)
            hot = jnp.where((row & 127) == low_row, 1.0, 0.0).astype(bf16)
            total = total + lax.dot_general(
                signed, hot, (((1,), (1,)), ((), ())), preferred_element_type=f32
            )
        return total

    total = lax.fori_loop(0, rows_ref.shape[0] // 8, chunk, jnp.zeros((160, CELLS), f32))
    for f in range(FIELDS):
        plane_ref[f] = (total[32 * f : 32 * f + 16] + total[32 * f + 16 : 32 * f + 32]) * normalizer


def pack_pitch(traces, lane):
    (low0, high0), (low1, high1) = traces
    return jnp.where(
        lane < 32,
        low0,
        jnp.where(
            lane < 64,
            pltpu.roll(low1, 32, 1),
            jnp.where(lane < 96, pltpu.roll(high0, 96, 1), high1),
        ),
    )


def pack_span(held, low, high, layer, first_span, lane):
    edge = jnp.where(first_span, high, low)
    shift = lax.rem(layer + jnp.where(first_span, 97, 0), 128)
    return jnp.where((lane & 31) == layer, pltpu.roll(edge, shift, 1), held)


def pack_field(f, trace, pair, first_span, lane, pitch_ref, span_held):
    halves = [trace[:, :CELLS], trace[:, CELLS:]]
    packed = pack_pitch([(h[0:16], h[16:32]) for h in halves], lane)
    pitch_ref[f, :, pair * CELLS : (pair + 1) * CELLS] = packed.astype(bf16)
    held = span_held[f]
    for h in range(2):
        held = pack_span(held, halves[h][32:48], halves[h][48:64], 2 * pair + h, first_span, lane)
    span_held[f] = held


def pack_kernel(
    v_ref, pick_ref, trace_ref, up_ref, down_ref, pitch_ref, span_ref, span_held
):
    first_span = lax.axis_index("span") == 0
    lane = lanes()
    pick = pick_ref[...]
    span_held[...] = jnp.zeros_like(span_held)
    for pair in range(EX // 2):
        at = slice(pair * PAIR, (pair + 1) * PAIR)
        traces = [dot(pick, v_ref[f, :, at]) for f in range(FIELDS)]
        for f in range(FIELDS):
            trace_ref[f, :, at] = traces[f].astype(bf16)
            pack_field(f, traces[f], pair, first_span, lane, pitch_ref, span_held)
    span_ref[...] = span_held[...].astype(bf16)
    up_ref[...] = v_ref[:, 48:64, (EX - 1) * CELLS :]
    down_ref[...] = v_ref[:, 0:16, 0:CELLS]


def mix(coefs, base, arrays):
    total = coefs[base] * arrays[0]
    for g in range(1, FIELDS):
        total = total + coefs[base + g] * arrays[g]
    return total


def mix_fluxes(read, coefs, mixed):
    def rows_step(r):
        def run():
            rows = [read(f, r, r + 16).astype(f32) for f in range(FIELDS)]
            for d in range(3):
                for f in range(FIELDS):
                    mixed[f, 64 * d + r : 64 * d + r + 16, :] = mix(
                        coefs, 25 * d + 5 * f, rows
                    ).astype(bf16)

        return run

    return [rows_step(r) for r in range(0, NODES, 16)]


def write_jumps(t, jumps, coefs, mixed, first_row):
    for f in range(FIELDS):
        mixed[f, first_row : first_row + 16, :] = mix(coefs, 75 + 25 * t + 5 * f, jumps).astype(bf16)


def mix_stream(read, lower, upper, coefs, mixed, row):
    def low():
        jumps = [lower(f) - read(f, 0, 16).astype(f32) for f in range(FIELDS)]
        write_jumps(0, jumps, coefs, mixed, row)

    def high():
        jumps = [upper(f) - read(f, 48, 64).astype(f32) for f in range(FIELDS)]
        write_jumps(1, jumps, coefs, mixed, row + 16)

    return [low, high]


def mix_sides(trace, pitch, span, layers, coefs, mixed, row, first_span, lane):
    def halves(f, r):
        own = trace(f, r, r + 16)
        return [own[:, h * CELLS : (h + 1) * CELLS] for h in range(len(layers))]

    def join(parts):
        return parts[0] if len(parts) == 1 else jnp.concatenate(parts, axis=1)

    def pitch_low():
        jumps = []
        for f in range(FIELDS):
            near, low, high = pitch(f), halves(f, 0), halves(f, 16)
            jumps.append(join([
                jnp.where(
                    lane < 32, pltpu.roll(near, 64 if h == 0 else 32, 1), pltpu.roll(high[h], 32, 1)
                ) - low[h]
                for h in range(len(layers))
            ]))
        write_jumps(2, jumps, coefs, mixed, row)

    def pitch_high():
        jumps = []
        for f in range(FIELDS):
            near, low, high = pitch(f), halves(f, 0), halves(f, 16)
            jumps.append(join([
                jnp.where(
                    lane >= 96, pltpu.roll(near, 96 if h == 0 else 64, 1), pltpu.roll(low[h], 96, 1)
                ) - high[h]
                for h in range(len(layers))
            ]))
        write_jumps(3, jumps, coefs, mixed, row + 16)

    def arrived(f, layer):
        return pltpu.roll(span(f), lax.rem(jnp.where(first_span, 31, 128) - layer, 128), 1)

    def span_low():
        jumps = []
        for f in range(FIELDS):
            low, high = halves(f, 32), halves(f, 48)
            jumps.append(join([
                jnp.where(
                    (lane & 31) == 0,
                    jnp.where(first_span, low[h], arrived(f, layer)),
                    pltpu.roll(high[h], 1, 1),
                ) - low[h]
                for h, layer in enumerate(layers)
            ]))
        write_jumps(4, jumps, coefs, mixed, row + 32)

    def span_high():
        jumps = []
        for f in range(FIELDS):
            low, high = halves(f, 32), halves(f, 48)
            jumps.append(join([
                jnp.where(
                    (lane & 31) == 31,
                    jnp.where(first_span, arrived(f, layer), high[h]),
                    pltpu.roll(low[h], 127, 1),
                ) - high[h]
                for h, layer in enumerate(layers)
            ]))
        write_jumps(5, jumps, coefs, mixed, row + 48)

    return [pitch_low, pitch_high, span_low, span_high]


def mix_wall(read, pinned, mixed, row):
    def run():
        for f in range(FIELDS):
            mixed[f, row : row + 64, :] = (read(f, 0, 64).astype(f32) * pinned()).astype(bf16)

    return [run]


def staggered(stages):
    held = [None] * FIELDS
    steps = []

    def step(stage, f):
        def run():
            held[f] = stage(f, held[f])

        return run

    for turn in range(FIELDS + len(stages) - 1):
        for k, stage in enumerate(stages):
            if 0 <= turn - k < FIELDS:
                steps.append(step(stage, turn - k))
    return steps


def interleave(first, second):
    count = max(len(first), len(second))
    for i in range(count):
        for steps in (first, second):
            for step in steps[i * len(steps) // count : (i + 1) * len(steps) // count]:
                step()


def pipeline(vector, matrix):
    for step in vector[0]:
        step()
    for p in range(len(matrix)):
        interleave(matrix[p], vector[p + 1] if p + 1 < len(vector) else [])


def finish(read, base, smooth):
    def trial(f, rate):
        v = read(f, 0, 64).astype(f32)
        if base is None:
            now = v - TIME_STEP * rate
        else:
            now = 0.5 * (base(f).astype(f32) + v - TIME_STEP * rate)
        return dot(smooth, now.astype(bf16))

    return trial


def place(pair):
    return slice(pair * PAIR, (pair + 1) * PAIR)


def lower_pair(v_ref, edge, pair):
    def lower(f):
        if pair:
            return v_ref[f, 48:64, pair * PAIR - CELLS : (pair + 1) * PAIR - CELLS].astype(f32)
        return jnp.concatenate([edge(f), v_ref[f, 48:64, 0:CELLS].astype(f32)], axis=1)

    return lower


def upper_pair(v_ref, above_ref, pair):
    first = pair * PAIR + CELLS
    last_rans = lax.axis_index("rans") == lax.axis_size("rans") - 1

    def upper(f):
        if pair < EX // 2 - 1:
            return v_ref[f, 0:16, first : first + PAIR].astype(f32)
        edge = jnp.where(
            last_rans, v_ref[f, 48:64, first : first + CELLS].astype(f32), above_ref[f].astype(f32)
        )
        return jnp.concatenate([v_ref[f, 0:16, first : first + CELLS].astype(f32), edge], axis=1)

    return upper


def phase_one_kernel(
    v_ref, trace_ref, below_ref, above_ref, near_ref, far_ref, pin_ref, coefs, weights_ref,
    smooth_ref, out_ref, out_trace_ref, up_ref, down_ref, pitch_ref, span_ref, mixed, span_held,
):
    first_span = lax.axis_index("span") == 0
    lane = lanes()
    weights, smooth = weights_ref[...], smooth_ref[...]
    span_held[...] = jnp.zeros_like(span_held)
    vector, matrix = [], []

    def add(pair):
        at = place(pair)
        rows = mixed.at[pair % 2]

        def read(f, r0, r1):
            return v_ref[f, r0:r1, at]

        def store(f, value):
            out_ref[f, :, at] = value[0:64].astype(bf16)
            trace = value[64:128]
            out_trace_ref[f, :, at] = trace.astype(bf16)
            pack_field(f, trace, pair, first_span, lane, pitch_ref, span_held)

        vector.append(
            mix_fluxes(read, coefs, rows)
            + mix_stream(
                read,
                lower_pair(v_ref, lambda f: below_ref[f].astype(f32), pair),
                upper_pair(v_ref, above_ref, pair),
                coefs, rows, 192,
            )
            + mix_sides(
                lambda f, r0, r1: trace_ref[f, r0:r1, at].astype(f32),
                lambda f: near_ref[f, :, pair * CELLS : (pair + 1) * CELLS].astype(f32),
                lambda f: far_ref[f].astype(f32),
                [2 * pair, 2 * pair + 1], coefs, rows, 224, first_span, lane,
            )
            + mix_wall(read, lambda: pin_ref[:, at].astype(f32), rows, 288)
        )
        matrix.append(
            staggered([lambda f, _: dot(weights, rows[f]), finish(read, None, smooth), store])
        )

    for pair in range(EX // 2):
        add(pair)
    pipeline(vector, matrix)
    span_ref[...] = span_held[...].astype(bf16)
    up_ref[...] = out_ref[:, 48:64, (EX - 1) * CELLS :]
    down_ref[...] = out_ref[:, 0:16, 0:CELLS]


def inner_two_kernel(
    v_ref, mean_ref, amp_ref, plane_ref, below_ref, above_ref, coefs, weights_ref, part_ref, mixed
):
    first_rans = lax.axis_index("rans") == 0
    weights = weights_ref[...]
    vector, matrix = [], []

    def edge(f):
        return jnp.where(
            first_rans, inflow_of(mean_ref, amp_ref, plane_ref)(f), below_ref[f].astype(f32)
        )

    def add(pair):
        at = place(pair)
        rows = mixed.at[pair % 2]

        def read(f, r0, r1):
            return v_ref[f, r0:r1, at]

        def store(f, value):
            part_ref[f, :, at] = value

        vector.append(
            mix_fluxes(read, coefs, rows)
            + mix_stream(
                read, lower_pair(v_ref, edge, pair), upper_pair(v_ref, above_ref, pair), coefs, rows,
                192,
            )
        )
        matrix.append(staggered([lambda f, _: dot(weights, rows[f]), store]))

    for pair in range(EX // 2):
        add(pair)
    pipeline(vector, matrix)


def outer_two_kernel(
    v_ref, trace_ref, base_ref, part_ref, near_ref, far_ref, pin_ref, coefs, weights_ref,
    smooth_ref, out_ref, mixed,
):
    first_span = lax.axis_index("span") == 0
    lane = lanes()
    weights, smooth = weights_ref[...], smooth_ref[...]
    vector, matrix = [], []

    def add(pair):
        at = place(pair)
        rows = mixed.at[pair % 2]

        def read(f, r0, r1):
            return v_ref[f, r0:r1, at]

        def store(f, value):
            out_ref[f, :, at] = value.astype(bf16)

        vector.append(
            mix_sides(
                lambda f, r0, r1: trace_ref[f, r0:r1, at].astype(f32),
                lambda f: near_ref[f, :, pair * CELLS : (pair + 1) * CELLS].astype(f32),
                lambda f: far_ref[f].astype(f32),
                [2 * pair, 2 * pair + 1], coefs, rows, 0, first_span, lane,
            )
            + mix_wall(read, lambda: pin_ref[:, at].astype(f32), rows, 64)
        )
        matrix.append(
            staggered([
                lambda f, _: dot(weights, rows[f]) + part_ref[f, :, at],
                finish(read, lambda f: base_ref[f, :, at], smooth),
                store,
            ])
        )

    for pair in range(EX // 2):
        add(pair)
    pipeline(vector, matrix)


def inflow_of(mean_ref, amp_ref, plane_ref):
    return lambda f: mean_ref[f] + amp_ref[f] * plane_ref[f]


def inflow_kernel(
    held_ref, held_trace_ref, held_pitch_ref, held_span_ref, v_ref, trace_ref, mean_ref, amp_ref,
    plane_ref, near_ref, far_ref, pin_ref, coefs, weights_ref, smooth_ref, out_ref, out_trace_ref,
    pitch_ref, span_ref, mixed,
):
    first_span = lax.axis_index("span") == 0
    first_rans = lax.axis_index("rans") == 0
    lane = lanes()

    @pl.when(first_rans)
    def _():
        weights, smooth = weights_ref[...], smooth_ref[...]

        def read(f, r0, r1):
            return v_ref[f, r0:r1, 0:CELLS]

        def store(f, value):
            out_ref[f] = value[0:64].astype(bf16)
            t = value[64:128]
            out_trace_ref[f] = t.astype(bf16)
            pitch = jnp.where(lane < 32, t[0:16], pltpu.roll(t[16:32], 96, 1))
            pitch_ref[f] = jnp.where(
                (lane & 63) < 32, pitch, held_pitch_ref[f].astype(f32)
            ).astype(bf16)
            span_ref[f] = pack_span(
                held_span_ref[f].astype(f32), t[32:48], t[48:64], 0, first_span, lane
            ).astype(bf16)

        vector = (
            mix_stream(
                read,
                inflow_of(mean_ref, amp_ref, plane_ref),
                lambda f: v_ref[f, 0:16, CELLS:PAIR].astype(f32),
                coefs, mixed, 192,
            )
            + mix_sides(
                lambda f, r0, r1: trace_ref[f, r0:r1].astype(f32),
                lambda f: near_ref[f].astype(f32),
                lambda f: far_ref[f].astype(f32),
                [0], coefs, mixed, 224, first_span, lane,
            )
            + mix_fluxes(read, coefs, mixed)
            + mix_wall(read, lambda: pin_ref[...].astype(f32), mixed, 288)
        )
        matrix = staggered(
            [lambda f, _: dot(weights, mixed[f]), finish(read, None, smooth), store]
        )
        pipeline([vector], [matrix])

    @pl.when(jnp.logical_not(first_rans))
    def _():
        out_ref[...] = held_ref[...]
        out_trace_ref[...] = held_trace_ref[...]
        pitch_ref[...] = held_pitch_ref[...]
        span_ref[...] = held_span_ref[...]


VMEM = pl.BlockSpec(memory_space=pltpu.VMEM)
SMEM = pl.BlockSpec(memory_space=pltpu.SMEM)
PARAMS = pltpu.CompilerParams(vmem_limit_bytes=40 * 2**20)


def shape_of(*dims, dtype=bf16):
    return jax.ShapeDtypeStruct(dims, dtype)


def front(*dims):
    return pl.BlockSpec(dims, lambda i: (0,) * len(dims))


def cost(us):
    return pl.CostEstimate(flops=int(us * 1e8), bytes_accessed=int(us * 3e6), transcendentals=0)


def body(
    solution, volume_ops, flux_jacobian, lift_matrix, filter_matrix, wall_matrix, pinched_map,
    mode_rows, mode_seeds, mode_shape, mean_inflow, eddy_amplitude,
):
    ranks = lax.axis_size("rans")
    eddies, foot = mode_shape.shape[2:]
    plane_rows = mean_inflow.shape[3]
    faces = shape_of(FIELDS, 16, CELLS)
    pick = trace_selector()

    plane = pl.pallas_call(
        functools.partial(
            plane_kernel, normalizer=float((plane_rows / (eddies * ranks * foot)) ** 0.5)
        ),
        out_shape=shape_of(FIELDS, 16, CELLS, dtype=f32),
        in_specs=[VMEM] * 3,
        out_specs=VMEM,
        compiler_params=PARAMS,
        cost_estimate=cost(3),
        name="eddy_plane",
    )(mode_rows[0, 0].T, mode_seeds.reshape(1, eddies), mode_shape[0, 0].T)

    def gather_sum(value, offsets, roots):
        parts = [lax.ppermute(value, "rans", [(r + o, r) for r in roots]) for o in offsets]
        for part in parts:
            value = value + part
        return value

    weights = jnp.concatenate(
        [volume_ops[0], volume_ops[1], volume_ops[2], lift_matrix, wall_matrix], axis=1
    )
    identity = jnp.eye(FIELDS, dtype=f32)
    sides = jnp.array([-1.0, 1.0], f32)
    face_coefs = (
        0.5 * sides[None, :, None, None] * flux_jacobian[:, None] - 0.5 * identity
    ).reshape(-1)
    coefs = jnp.concatenate([flux_jacobian.reshape(-1), face_coefs])
    pins = pinched_map.reshape(1, -1)
    rows = filter_matrix.reshape(4, 4, 4, NODES)
    smooth = jnp.concatenate(
        [filter_matrix]
        + [part.reshape(16, NODES) for part in (rows[:, 0], rows[:, 3], rows[:, :, 0], rows[:, :, 3])]
    )
    fixed_specs = [VMEM, SMEM, VMEM, VMEM]
    elements = solution.shape[2]
    traces = shape_of(FIELDS, NODES, elements)
    sends = (faces, faces, shape_of(FIELDS, 16, EX // 2 * CELLS), faces)
    rise = [(i, i + 1) for i in range(ranks - 1)]
    fall = [(b, a) for a, b in rise]
    swap = [(0, 1), (1, 0)]

    span_scratch = pltpu.VMEM((FIELDS, 16, CELLS), f32)
    trace, up, down, pitch, span = pl.pallas_call(
        pack_kernel,
        out_shape=(traces,) + sends,
        in_specs=[VMEM] * 2,
        out_specs=(VMEM,) * 5,
        scratch_shapes=[span_scratch],
        compiler_params=PARAMS,
        cost_estimate=cost(2),
        name="pack_faces",
    )(solution, pick)
    plane = gather_sum(plane, (2, 6, 4), [8 * z + c for z in range(8) for c in range(2)])
    near = lax.ppermute(pitch, "pitch", swap)
    far = lax.ppermute(span, "span", swap)
    plane, near, far, up, down = lax.optimization_barrier((plane, near, far, up, down))
    plane = gather_sum(plane, (1, 8, 9), [0, 16, 32, 48])
    below = lax.ppermute(up, "rans", rise)
    above = lax.ppermute(down, "rans", fall)
    plane, near, far, below, above = lax.optimization_barrier((plane, near, far, below, above))
    plane = gather_sum(plane, (16, 48, 32), [0])

    phase_one, trace_one, up, down, pitch, span = pl.pallas_call(
        phase_one_kernel,
        out_shape=(traces, traces) + sends,
        in_specs=[VMEM] * 6 + fixed_specs,
        out_specs=(VMEM,) * 6,
        scratch_shapes=[pltpu.VMEM((2, FIELDS, MIXED, PAIR), bf16), span_scratch],
        compiler_params=PARAMS,
        cost_estimate=cost(6),
        name="phase_one",
    )(solution, trace, below, above, near, far, pins, coefs, weights, smooth)
    below = lax.ppermute(up, "rans", rise)
    above = lax.ppermute(down, "rans", fall)

    plane, below, above = lax.optimization_barrier((plane, below, above))

    mean = mean_inflow.reshape(FIELDS, 16, CELLS)
    amplitude = eddy_amplitude.reshape(FIELDS, 16, CELLS)
    layer = front(FIELDS, NODES, CELLS)
    face = front(FIELDS, 16, CELLS)
    phase_one, trace_one, pitch, span = pl.pallas_call(
        inflow_kernel,
        grid=(1,),
        out_shape=(traces, traces, sends[2], sends[3]),
        in_specs=[layer, layer, face, face, front(FIELDS, NODES, PAIR), layer]
        + [face] * 5
        + [front(1, CELLS), SMEM, front(NODES, MIXED), front(2 * NODES, NODES)],
        out_specs=(layer, layer, face, face),
        scratch_shapes=[pltpu.VMEM((FIELDS, MIXED, CELLS), bf16)],
        input_output_aliases={0: 0, 1: 1, 2: 2, 3: 3},
        compiler_params=PARAMS,
        cost_estimate=cost(1),
        name="inflow_layer",
    )(
        phase_one, trace_one, pitch, span, solution, trace, mean, amplitude, plane, near, far,
        pins, coefs, weights, smooth,
    )
    near = lax.ppermute(pitch, "pitch", swap)
    far = lax.ppermute(span, "span", swap)
    part = pl.pallas_call(
        inner_two_kernel,
        out_shape=shape_of(FIELDS, NODES, elements, dtype=f32),
        in_specs=[VMEM] * 6 + [SMEM, VMEM],
        out_specs=VMEM,
        scratch_shapes=[pltpu.VMEM((2, FIELDS, INNER, PAIR), bf16)],
        compiler_params=PARAMS,
        cost_estimate=cost(3),
        name="inner_two",
    )(phase_one, mean, amplitude, plane, below, above, coefs, weights[:, :INNER])
    return pl.pallas_call(
        outer_two_kernel,
        out_shape=traces,
        in_specs=[VMEM] * 7 + fixed_specs[1:],
        out_specs=VMEM,
        scratch_shapes=[pltpu.VMEM((2, FIELDS, MIXED - INNER, PAIR), bf16)],
        compiler_params=PARAMS,
        cost_estimate=cost(4),
        name="outer_two",
    )(
        phase_one, trace_one, solution, part, near, far, pins, coefs, weights[:, INNER:],
        filter_matrix,
    )


def solution(mesh):
    spread = P(None, None, ("rans", "pitch", "span"))
    in_specs = (
        spread,
        P(),
        P(),
        P(),
        P(),
        P(),
        P(("rans", "pitch", "span")),
        P("pitch", "span", "rans", None),
        P("pitch", "span", "rans"),
        P("pitch", "span", "rans", None),
        P("pitch", "span", None, None),
        P("pitch", "span", None, None),
    )
    return jax.shard_map(body, mesh=mesh, in_specs=in_specs, out_specs=spread, check_vma=False)
```

```python
import functools

import jax
import jax.numpy as jnp
from jax import lax
from jax.experimental import pallas as pl
from jax.experimental.pallas import tpu as pltpu
from jax.sharding import PartitionSpec as P

FIELDS = 5
NODES = 64
EX = 12
CELLS = 128
SPAN_CELLS = 32
PAIR = 2 * CELLS
MIXED = 352
INNER = 224
TIME_STEP = 0.4
f32 = jnp.float32
bf16 = jnp.bfloat16


def trace_selector():
    row = lax.broadcasted_iota(jnp.int32, (64, 64), 0)
    node = lax.broadcasted_iota(jnp.int32, (64, 64), 1)
    face, first, second = row >> 4, (row >> 2) & 3, row & 3
    on_pitch = second + jnp.where(face == 1, 12, 0)
    on_span = 4 * second + jnp.where(face == 3, 3, 0)
    source = 16 * first + jnp.where(face < 2, on_pitch, on_span)
    return jnp.where(node == source, 1.0, 0.0).astype(bf16)


def dot(a, b):
    return jnp.dot(a, b, preferred_element_type=f32)


def lanes():
    return lax.broadcasted_iota(jnp.int32, (16, CELLS), 1)


def sum_eddies(rows_ref, seeds_ref, shape_ref, plane_ref, normalizer):
    seeds = seeds_ref[...]
    signs = [(2 * ((seeds >> f) & 1) - 1).astype(f32) for f in range(FIELDS)]
    signs = [jnp.broadcast_to(s, (32, s.shape[1])).astype(bf16) for s in signs]
    eddies = rows_ref.shape[1]
    high_row = lax.broadcasted_iota(jnp.int32, (16, eddies), 0)
    low_row = lax.broadcasted_iota(jnp.int32, (CELLS, eddies), 0)

    def chunk(i, total):
        start = pl.multiple_of(i * 8, 8)
        rows = rows_ref[pl.ds(start, 8), :]
        shapes = shape_ref[pl.ds(start, 8), :]
        for q in range(8):
            row, shape = rows[q : q + 1], shapes[q : q + 1]
            placed = jnp.where((row >> 7) == high_row, shape, 0.0)
            coarse = placed.astype(bf16)
            fine = (placed - coarse.astype(f32)).astype(bf16)
            both = jnp.concatenate([coarse, fine], axis=0)
            signed = jnp.concatenate([both * s for s in signs], axis=0)
            hot = jnp.where((row & 127) == low_row, 1.0, 0.0).astype(bf16)
            total = total + lax.dot_general(
                signed, hot, (((1,), (1,)), ((), ())), preferred_element_type=f32
            )
        return total

    total = lax.fori_loop(0, rows_ref.shape[0] // 8, chunk, jnp.zeros((160, CELLS), f32))
    for f in range(FIELDS):
        plane_ref[f] = (total[32 * f : 32 * f + 16] + total[32 * f + 16 : 32 * f + 32]) * normalizer


def pack_pitch(traces, lane):
    (low0, high0), (low1, high1) = traces
    return jnp.where(
        lane < 32,
        low0,
        jnp.where(
            lane < 64,
            pltpu.roll(low1, 32, 1),
            jnp.where(lane < 96, pltpu.roll(high0, 96, 1), high1),
        ),
    )


def pack_span(held, low, high, layer, first_span, lane):
    edge = jnp.where(first_span, high, low)
    shift = lax.rem(layer + jnp.where(first_span, 97, 0), 128)
    return jnp.where((lane & 31) == layer, pltpu.roll(edge, shift, 1), held)


def pack_field(f, trace, pair, first_span, lane, pitch_ref, span_held):
    halves = [trace[:, :CELLS], trace[:, CELLS:]]
    packed = pack_pitch([(h[0:16], h[16:32]) for h in halves], lane)
    pitch_ref[f, :, pair * CELLS : (pair + 1) * CELLS] = packed.astype(bf16)
    held = span_held[f]
    for h in range(2):
        held = pack_span(held, halves[h][32:48], halves[h][48:64], 2 * pair + h, first_span, lane)
    span_held[f] = held


def is_even():
    return (lax.axis_index("rans") & 1) == 0


def store_stream(up, down, near_chip_ref, far_chip_ref):
    even = is_even()
    near_chip_ref[...] = jnp.where(even, up, down)
    far_chip_ref[...] = jnp.where(even, down, up)


def from_below(near_chip_ref, far_chip_ref):
    even = is_even()
    return lambda f: jnp.where(even, far_chip_ref[f].astype(f32), near_chip_ref[f].astype(f32))


def from_above(near_chip_ref, far_chip_ref):
    even = is_even()
    return lambda f: jnp.where(even, near_chip_ref[f].astype(f32), far_chip_ref[f].astype(f32))


def prepare_kernel(
    rows_hbm, seeds_hbm, shape_hbm, v_hbm, plane_ref, trace_ref, core_ref, chip_ref, pitch_ref,
    span_ref, rows_ref, seeds_ref, shape_ref, v_ref, span_held, sems, *, normalizer,
):
    copies = [
        pltpu.make_async_copy(source, target, sems.at[i])
        for i, (source, target) in enumerate([
            (rows_hbm, rows_ref), (seeds_hbm, seeds_ref), (shape_hbm, shape_ref), (v_hbm, v_ref)
        ])
    ]
    for copy in copies:
        copy.start()
    first_span = lax.axis_index("span") == 0
    lane = lanes()
    pick = trace_selector()
    span_held[...] = jnp.zeros_like(span_held)
    for copy in copies[:3]:
        copy.wait()
    sum_eddies(rows_ref, seeds_ref, shape_ref, plane_ref, normalizer)
    copies[3].wait()
    for pair in range(EX // 2):
        at = slice(pair * PAIR, (pair + 1) * PAIR)
        traces = [dot(pick, v_ref[f, :, at]) for f in range(FIELDS)]
        for f in range(FIELDS):
            trace_ref[f, :, at] = traces[f].astype(bf16)
            pack_field(f, traces[f], pair, first_span, lane, pitch_ref, span_held)
    span_ref[...] = span_held[...].astype(bf16)
    store_stream(
        v_ref[:, 48:64, (EX - 1) * CELLS :], v_ref[:, 0:16, 0:CELLS], core_ref, chip_ref
    )


def mix(coefs, base, arrays):
    total = coefs[base] * arrays[0]
    for g in range(1, FIELDS):
        total = total + coefs[base + g] * arrays[g]
    return total


def mix_fluxes(read, coefs, mixed):
    def rows_step(r):
        def run():
            rows = [read(f, r, r + 16).astype(f32) for f in range(FIELDS)]
            for d in range(3):
                for f in range(FIELDS):
                    mixed[f, 64 * d + r : 64 * d + r + 16, :] = mix(
                        coefs, 25 * d + 5 * f, rows
                    ).astype(bf16)

        return run

    return [rows_step(r) for r in range(0, NODES, 16)]


def write_jumps(t, jumps, coefs, mixed, first_row):
    for f in range(FIELDS):
        mixed[f, first_row : first_row + 16, :] = mix(coefs, 75 + 25 * t + 5 * f, jumps).astype(bf16)


def mix_stream(read, lower, upper, coefs, mixed, row):
    def low():
        jumps = [lower(f) - read(f, 0, 16).astype(f32) for f in range(FIELDS)]
        write_jumps(0, jumps, coefs, mixed, row)

    def high():
        jumps = [upper(f) - read(f, 48, 64).astype(f32) for f in range(FIELDS)]
        write_jumps(1, jumps, coefs, mixed, row + 16)

    return [low, high]


def mix_sides(trace, pitch, span, layers, coefs, mixed, row, first_span, lane):
    def halves(f, r):
        own = trace(f, r, r + 16)
        return [own[:, h * CELLS : (h + 1) * CELLS] for h in range(len(layers))]

    def join(parts):
        return parts[0] if len(parts) == 1 else jnp.concatenate(parts, axis=1)

    def pitch_low():
        jumps = []
        for f in range(FIELDS):
            near, low, high = pitch(f), halves(f, 0), halves(f, 16)
            jumps.append(join([
                jnp.where(
                    lane < 32, pltpu.roll(near, 64 if h == 0 else 32, 1), pltpu.roll(high[h], 32, 1)
                ) - low[h]
                for h in range(len(layers))
            ]))
        write_jumps(2, jumps, coefs, mixed, row)

    def pitch_high():
        jumps = []
        for f in range(FIELDS):
            near, low, high = pitch(f), halves(f, 0), halves(f, 16)
            jumps.append(join([
                jnp.where(
                    lane >= 96, pltpu.roll(near, 96 if h == 0 else 64, 1), pltpu.roll(low[h], 96, 1)
                ) - high[h]
                for h in range(len(layers))
            ]))
        write_jumps(3, jumps, coefs, mixed, row + 16)

    def arrived(f, layer):
        return pltpu.roll(span(f), lax.rem(jnp.where(first_span, 31, 128) - layer, 128), 1)

    def span_low():
        jumps = []
        for f in range(FIELDS):
            low, high = halves(f, 32), halves(f, 48)
            jumps.append(join([
                jnp.where(
                    (lane & 31) == 0,
                    jnp.where(first_span, low[h], arrived(f, layer)),
                    pltpu.roll(high[h], 1, 1),
                ) - low[h]
                for h, layer in enumerate(layers)
            ]))
        write_jumps(4, jumps, coefs, mixed, row + 32)

    def span_high():
        jumps = []
        for f in range(FIELDS):
            low, high = halves(f, 32), halves(f, 48)
            jumps.append(join([
                jnp.where(
                    (lane & 31) == 31,
                    jnp.where(first_span, arrived(f, layer), high[h]),
                    pltpu.roll(low[h], 127, 1),
                ) - high[h]
                for h, layer in enumerate(layers)
            ]))
        write_jumps(5, jumps, coefs, mixed, row + 48)

    return [pitch_low, pitch_high, span_low, span_high]


def mix_wall(read, pinned, mixed, row):
    def run():
        for f in range(FIELDS):
            mixed[f, row : row + 64, :] = (read(f, 0, 64).astype(f32) * pinned()).astype(bf16)

    return [run]


def staggered(stages):
    held = [None] * FIELDS
    steps = []

    def step(stage, f):
        def run():
            held[f] = stage(f, held[f])

        return run

    for turn in range(FIELDS + len(stages) - 1):
        for k, stage in enumerate(stages):
            if 0 <= turn - k < FIELDS:
                steps.append(step(stage, turn - k))
    return steps


def interleave(first, second):
    count = max(len(first), len(second))
    for i in range(count):
        for steps in (first, second):
            for step in steps[i * len(steps) // count : (i + 1) * len(steps) // count]:
                step()


def pipeline(vector, matrix):
    for step in vector[0]:
        step()
    for p in range(len(matrix)):
        interleave(matrix[p], vector[p + 1] if p + 1 < len(vector) else [])


def finish(read, base, smooth):
    def trial(f, rate):
        v = read(f, 0, 64).astype(f32)
        if base is None:
            now = v - TIME_STEP * rate
        else:
            now = 0.5 * (base(f).astype(f32) + v - TIME_STEP * rate)
        return dot(smooth, now.astype(bf16))

    return trial


def place(pair):
    return slice(pair * PAIR, (pair + 1) * PAIR)


def lower_pair(v_ref, edge, pair):
    def lower(f):
        if pair:
            return v_ref[f, 48:64, pair * PAIR - CELLS : (pair + 1) * PAIR - CELLS].astype(f32)
        return jnp.concatenate([edge(f), v_ref[f, 48:64, 0:CELLS].astype(f32)], axis=1)

    return lower


def upper_pair(v_ref, above, pair):
    first = pair * PAIR + CELLS
    last_rans = lax.axis_index("rans") == lax.axis_size("rans") - 1

    def upper(f):
        if pair < EX // 2 - 1:
            return v_ref[f, 0:16, first : first + PAIR].astype(f32)
        edge = jnp.where(
            last_rans, v_ref[f, 48:64, first : first + CELLS].astype(f32), above(f)
        )
        return jnp.concatenate([v_ref[f, 0:16, first : first + CELLS].astype(f32), edge], axis=1)

    return upper


def phase_one_kernel(
    v_ref, trace_ref, from_core_ref, from_chip_ref, near_ref, far_ref, pin_ref, coefs, weights_ref,
    smooth_ref, out_ref, out_trace_ref, core_ref, chip_ref, pitch_ref, span_ref, mixed, span_held,
):
    first_span = lax.axis_index("span") == 0
    lane = lanes()
    weights, smooth = weights_ref[...], smooth_ref[...]
    span_held[...] = jnp.zeros_like(span_held)
    below, above = from_below(from_core_ref, from_chip_ref), from_above(from_core_ref, from_chip_ref)
    vector, matrix = [], []

    def add(pair):
        at = place(pair)
        rows = mixed.at[pair % 2]

        def read(f, r0, r1):
            return v_ref[f, r0:r1, at]

        def store(f, value):
            out_ref[f, :, at] = value[0:64].astype(bf16)
            trace = value[64:128]
            out_trace_ref[f, :, at] = trace.astype(bf16)
            pack_field(f, trace, pair, first_span, lane, pitch_ref, span_held)

        vector.append(
            mix_fluxes(read, coefs, rows)
            + mix_stream(
                read,
                lower_pair(v_ref, below, pair),
                upper_pair(v_ref, above, pair),
                coefs, rows, 192,
            )
            + mix_sides(
                lambda f, r0, r1: trace_ref[f, r0:r1, at].astype(f32),
                lambda f: near_ref[f, :, pair * CELLS : (pair + 1) * CELLS].astype(f32),
                lambda f: far_ref[f].astype(f32),
                [2 * pair, 2 * pair + 1], coefs, rows, 224, first_span, lane,
            )
            + mix_wall(read, lambda: pin_ref[:, at].astype(f32), rows, 288)
        )
        matrix.append(
            staggered([lambda f, _: dot(weights, rows[f]), finish(read, None, smooth), store])
        )

    for pair in range(EX // 2):
        add(pair)
    pipeline(vector, matrix)
    span_ref[...] = span_held[...].astype(bf16)
    store_stream(
        out_ref[:, 48:64, (EX - 1) * CELLS :], out_ref[:, 0:16, 0:CELLS], core_ref, chip_ref
    )


def inner_two_kernel(
    v_ref, mean_ref, amp_ref, plane_ref, from_core_ref, from_chip_ref, coefs, weights_ref, part_ref,
    mixed,
):
    first_rans = lax.axis_index("rans") == 0
    weights = weights_ref[...]
    below, above = from_below(from_core_ref, from_chip_ref), from_above(from_core_ref, from_chip_ref)
    vector, matrix = [], []

    def edge(f):
        return jnp.where(first_rans, inflow_of(mean_ref, amp_ref, plane_ref)(f), below(f))

    def add(pair):
        at = place(pair)
        rows = mixed.at[pair % 2]

        def read(f, r0, r1):
            return v_ref[f, r0:r1, at]

        def store(f, value):
            part_ref[f, :, at] = value

        vector.append(
            mix_fluxes(read, coefs, rows)
            + mix_stream(
                read, lower_pair(v_ref, edge, pair), upper_pair(v_ref, above, pair), coefs, rows, 192,
            )
        )
        matrix.append(staggered([lambda f, _: dot(weights, rows[f]), store]))

    for pair in range(EX // 2):
        add(pair)
    pipeline(vector, matrix)


def outer_two_kernel(
    v_ref, trace_ref, base_ref, part_ref, near_ref, far_ref, pin_ref, coefs, weights_ref,
    smooth_ref, out_ref, mixed,
):
    first_span = lax.axis_index("span") == 0
    lane = lanes()
    weights, smooth = weights_ref[...], smooth_ref[...]
    vector, matrix = [], []

    def add(pair):
        at = place(pair)
        rows = mixed.at[pair % 2]

        def read(f, r0, r1):
            return v_ref[f, r0:r1, at]

        def store(f, value):
            out_ref[f, :, at] = value.astype(bf16)

        vector.append(
            mix_sides(
                lambda f, r0, r1: trace_ref[f, r0:r1, at].astype(f32),
                lambda f: near_ref[f, :, pair * CELLS : (pair + 1) * CELLS].astype(f32),
                lambda f: far_ref[f].astype(f32),
                [2 * pair, 2 * pair + 1], coefs, rows, 0, first_span, lane,
            )
            + mix_wall(read, lambda: pin_ref[:, at].astype(f32), rows, 64)
        )
        matrix.append(
            staggered([
                lambda f, _: dot(weights, rows[f]) + part_ref[f, :, at],
                finish(read, lambda f: base_ref[f, :, at], smooth),
                store,
            ])
        )

    for pair in range(EX // 2):
        add(pair)
    pipeline(vector, matrix)


def inflow_of(mean_ref, amp_ref, plane_ref):
    return lambda f: mean_ref[f] + amp_ref[f] * plane_ref[f]


def inflow_kernel(
    held_ref, held_trace_ref, held_pitch_ref, held_span_ref, v_ref, trace_ref, mean_ref, amp_ref,
    plane_ref, near_ref, far_ref, pin_ref, coefs, weights_ref, smooth_ref, out_ref, out_trace_ref,
    pitch_ref, span_ref, mixed,
):
    first_span = lax.axis_index("span") == 0
    first_rans = lax.axis_index("rans") == 0
    lane = lanes()

    @pl.when(first_rans)
    def _():
        weights, smooth = weights_ref[...], smooth_ref[...]

        def read(f, r0, r1):
            return v_ref[f, r0:r1, 0:CELLS]

        def store(f, value):
            out_ref[f] = value[0:64].astype(bf16)
            t = value[64:128]
            out_trace_ref[f] = t.astype(bf16)
            pitch = jnp.where(lane < 32, t[0:16], pltpu.roll(t[16:32], 96, 1))
            pitch_ref[f] = jnp.where(
                (lane & 63) < 32, pitch, held_pitch_ref[f].astype(f32)
            ).astype(bf16)
            span_ref[f] = pack_span(
                held_span_ref[f].astype(f32), t[32:48], t[48:64], 0, first_span, lane
            ).astype(bf16)

        vector = (
            mix_stream(
                read,
                inflow_of(mean_ref, amp_ref, plane_ref),
                lambda f: v_ref[f, 0:16, CELLS:PAIR].astype(f32),
                coefs, mixed, 192,
            )
            + mix_sides(
                lambda f, r0, r1: trace_ref[f, r0:r1].astype(f32),
                lambda f: near_ref[f].astype(f32),
                lambda f: far_ref[f].astype(f32),
                [0], coefs, mixed, 224, first_span, lane,
            )
            + mix_fluxes(read, coefs, mixed)
            + mix_wall(read, lambda: pin_ref[...].astype(f32), mixed, 288)
        )
        matrix = staggered(
            [lambda f, _: dot(weights, mixed[f]), finish(read, None, smooth), store]
        )
        pipeline([vector], [matrix])

    @pl.when(jnp.logical_not(first_rans))
    def _():
        out_ref[...] = held_ref[...]
        out_trace_ref[...] = held_trace_ref[...]
        pitch_ref[...] = held_pitch_ref[...]
        span_ref[...] = held_span_ref[...]


VMEM = pl.BlockSpec(memory_space=pltpu.VMEM)
SMEM = pl.BlockSpec(memory_space=pltpu.SMEM)
PARAMS = pltpu.CompilerParams(vmem_limit_bytes=40 * 2**20)


def shape_of(*dims, dtype=bf16):
    return jax.ShapeDtypeStruct(dims, dtype)


def front(*dims):
    return pl.BlockSpec(dims, lambda i: (0,) * len(dims))


def cost(us):
    return pl.CostEstimate(flops=int(us * 1e8), bytes_accessed=int(us * 3e6), transcendentals=0)


def body(
    solution, volume_ops, flux_jacobian, lift_matrix, filter_matrix, wall_matrix, pinched_map,
    mode_rows, mode_seeds, mode_shape, mean_inflow, eddy_amplitude,
):
    ranks = lax.axis_size("rans")
    eddies, foot = mode_shape.shape[2:]
    plane_rows = mean_inflow.shape[3]
    faces = shape_of(FIELDS, 16, CELLS)
    def gather_sum(value, offsets, roots):
        parts = [lax.ppermute(value, "rans", [(r + o, r) for r in roots]) for o in offsets]
        for part in parts:
            value = value + part
        return value

    weights = jnp.concatenate(
        [volume_ops[0], volume_ops[1], volume_ops[2], lift_matrix, wall_matrix], axis=1
    )
    identity = jnp.eye(FIELDS, dtype=f32)
    sides = jnp.array([-1.0, 1.0], f32)
    face_coefs = (
        0.5 * sides[None, :, None, None] * flux_jacobian[:, None] - 0.5 * identity
    ).reshape(-1)
    coefs = jnp.concatenate([flux_jacobian.reshape(-1), face_coefs])
    pins = pinched_map.reshape(1, -1)
    rows = filter_matrix.reshape(4, 4, 4, NODES)
    smooth = jnp.concatenate(
        [filter_matrix]
        + [part.reshape(16, NODES) for part in (rows[:, 0], rows[:, 3], rows[:, :, 0], rows[:, :, 3])]
    )
    fixed_specs = [VMEM, SMEM, VMEM, VMEM]
    elements = solution.shape[2]
    traces = shape_of(FIELDS, NODES, elements)
    sends = (faces, faces, shape_of(FIELDS, 16, EX // 2 * CELLS), faces)
    swap = [(0, 1), (1, 0)]
    same_chip = [(i, i ^ 1) for i in range(ranks)]
    next_chip = [(a + 1, b + 1) for a, b in same_chip if max(a, b) + 1 < ranks]

    span_scratch = pltpu.VMEM((FIELDS, 16, CELLS), f32)
    plane, trace, core, chip, pitch, span = pl.pallas_call(
        functools.partial(
            prepare_kernel, normalizer=float((plane_rows / (eddies * ranks * foot)) ** 0.5)
        ),
        out_shape=(shape_of(FIELDS, 16, CELLS, dtype=f32), traces) + sends,
        in_specs=[pl.BlockSpec(memory_space=pltpu.HBM)] * 4,
        out_specs=(VMEM,) * 6,
        scratch_shapes=[
            pltpu.VMEM((foot, eddies), jnp.int32),
            pltpu.VMEM((1, eddies), jnp.int32),
            pltpu.VMEM((foot, eddies), f32),
            pltpu.VMEM(solution.shape, bf16),
            span_scratch,
            pltpu.SemaphoreType.DMA((4,)),
        ],
        compiler_params=pltpu.CompilerParams(vmem_limit_bytes=60 * 2**20),
        cost_estimate=cost(5),
        name="prepare",
    )(mode_rows[0, 0].T, mode_seeds.reshape(1, eddies), mode_shape[0, 0].T, solution)
    plane = gather_sum(plane, (2, 6, 4), [8 * z + c for z in range(8) for c in range(2)])
    near = lax.ppermute(pitch, "pitch", swap)
    from_chip = lax.ppermute(chip, "rans", next_chip)
    plane, core, span = lax.optimization_barrier((plane, core, span))
    plane = gather_sum(plane, (1, 8, 9), [0, 16, 32, 48])
    core, span, near, from_chip = lax.optimization_barrier((core, span, near, from_chip))
    far = lax.ppermute(span, "span", swap)
    from_core = lax.ppermute(core, "rans", same_chip)
    plane, near, far, from_core, from_chip = lax.optimization_barrier(
        (plane, near, far, from_core, from_chip)
    )
    plane = gather_sum(plane, (16, 48, 32), [0])

    phase_one, trace_one, core, chip, pitch, span = pl.pallas_call(
        phase_one_kernel,
        out_shape=(traces, traces) + sends,
        in_specs=[VMEM] * 6 + fixed_specs,
        out_specs=(VMEM,) * 6,
        scratch_shapes=[pltpu.VMEM((2, FIELDS, MIXED, PAIR), bf16), span_scratch],
        compiler_params=PARAMS,
        cost_estimate=cost(6),
        name="phase_one",
    )(solution, trace, from_core, from_chip, near, far, pins, coefs, weights, smooth)
    from_core = lax.ppermute(core, "rans", same_chip)
    from_chip = lax.ppermute(chip, "rans", next_chip)
    plane, from_core, from_chip = lax.optimization_barrier((plane, from_core, from_chip))

    mean = mean_inflow.reshape(FIELDS, 16, CELLS)
    amplitude = eddy_amplitude.reshape(FIELDS, 16, CELLS)
    layer = front(FIELDS, NODES, CELLS)
    face = front(FIELDS, 16, CELLS)
    phase_one, trace_one, pitch, span = pl.pallas_call(
        inflow_kernel,
        grid=(1,),
        out_shape=(traces, traces, sends[2], sends[3]),
        in_specs=[layer, layer, face, face, front(FIELDS, NODES, PAIR), layer]
        + [face] * 5
        + [front(1, CELLS), SMEM, front(NODES, MIXED), front(2 * NODES, NODES)],
        out_specs=(layer, layer, face, face),
        scratch_shapes=[pltpu.VMEM((FIELDS, MIXED, CELLS), bf16)],
        input_output_aliases={0: 0, 1: 1, 2: 2, 3: 3},
        compiler_params=PARAMS,
        cost_estimate=cost(1),
        name="inflow_layer",
    )(
        phase_one, trace_one, pitch, span, solution, trace, mean, amplitude, plane, near, far,
        pins, coefs, weights, smooth,
    )
    near = lax.ppermute(pitch, "pitch", swap)
    far = lax.ppermute(span, "span", swap)
    part = pl.pallas_call(
        inner_two_kernel,
        out_shape=shape_of(FIELDS, NODES, elements, dtype=f32),
        in_specs=[VMEM] * 6 + [SMEM, VMEM],
        out_specs=VMEM,
        scratch_shapes=[pltpu.VMEM((2, FIELDS, INNER, PAIR), bf16)],
        compiler_params=PARAMS,
        cost_estimate=cost(3),
        name="inner_two",
    )(phase_one, mean, amplitude, plane, from_core, from_chip, coefs, weights[:, :INNER])
    return pl.pallas_call(
        outer_two_kernel,
        out_shape=traces,
        in_specs=[VMEM] * 7 + fixed_specs[1:],
        out_specs=VMEM,
        scratch_shapes=[pltpu.VMEM((2, FIELDS, MIXED - INNER, PAIR), bf16)],
        compiler_params=PARAMS,
        cost_estimate=cost(4),
        name="outer_two",
    )(
        phase_one, trace_one, solution, part, near, far, pins, coefs, weights[:, INNER:],
        filter_matrix,
    )


def solution(mesh):
    spread = P(None, None, ("rans", "pitch", "span"))
    in_specs = (
        spread,
        P(),
        P(),
        P(),
        P(),
        P(),
        P(("rans", "pitch", "span")),
        P("pitch", "span", "rans", None),
        P("pitch", "span", "rans"),
        P("pitch", "span", "rans", None),
        P("pitch", "span", None, None),
        P("pitch", "span", None, None),
    )
    return jax.shard_map(body, mesh=mesh, in_specs=in_specs, out_specs=spread, check_vma=False)
```

```python
import functools

import jax
import jax.numpy as jnp
from jax import lax
from jax.experimental import pallas as pl
from jax.experimental.pallas import tpu as pltpu
from jax.sharding import PartitionSpec as P

FIELDS = 5
NODES = 64
EX = 12
CELLS = 128
SPAN_CELLS = 32
PAIR = 2 * CELLS
MIXED = 352
INNER = 192
TIME_STEP = 0.4
f32 = jnp.float32
bf16 = jnp.bfloat16


def trace_selector():
    row = lax.broadcasted_iota(jnp.int32, (64, 64), 0)
    node = lax.broadcasted_iota(jnp.int32, (64, 64), 1)
    face, first, second = row >> 4, (row >> 2) & 3, row & 3
    on_pitch = second + jnp.where(face == 1, 12, 0)
    on_span = 4 * second + jnp.where(face == 3, 3, 0)
    source = 16 * first + jnp.where(face < 2, on_pitch, on_span)
    return jnp.where(node == source, 1.0, 0.0).astype(bf16)


def dot(a, b):
    return jnp.dot(a, b, preferred_element_type=f32)


def lanes():
    return lax.broadcasted_iota(jnp.int32, (16, CELLS), 1)


def sum_eddies(rows_ref, seeds_ref, shape_ref, plane_ref, normalizer):
    seeds = seeds_ref[...]
    signs = [(2 * ((seeds >> f) & 1) - 1).astype(f32) for f in range(FIELDS)]
    signs = [jnp.broadcast_to(s, (32, s.shape[1])).astype(bf16) for s in signs]
    eddies = rows_ref.shape[1]
    high_row = lax.broadcasted_iota(jnp.int32, (16, eddies), 0)
    low_row = lax.broadcasted_iota(jnp.int32, (CELLS, eddies), 0)

    def chunk(i, total):
        start = pl.multiple_of(i * 8, 8)
        rows = rows_ref[pl.ds(start, 8), :]
        shapes = shape_ref[pl.ds(start, 8), :]
        for q in range(8):
            row, shape = rows[q : q + 1], shapes[q : q + 1]
            placed = jnp.where((row >> 7) == high_row, shape, 0.0)
            coarse = placed.astype(bf16)
            fine = (placed - coarse.astype(f32)).astype(bf16)
            both = jnp.concatenate([coarse, fine], axis=0)
            signed = jnp.concatenate([both * s for s in signs], axis=0)
            hot = jnp.where((row & 127) == low_row, 1.0, 0.0).astype(bf16)
            total = total + lax.dot_general(
                signed, hot, (((1,), (1,)), ((), ())), preferred_element_type=f32
            )
        return total

    total = lax.fori_loop(0, rows_ref.shape[0] // 8, chunk, jnp.zeros((160, CELLS), f32))
    for f in range(FIELDS):
        plane_ref[f] = (total[32 * f : 32 * f + 16] + total[32 * f + 16 : 32 * f + 32]) * normalizer


def pack_pitch(traces, lane):
    (low0, high0), (low1, high1) = traces
    return jnp.where(
        lane < 32,
        low0,
        jnp.where(
            lane < 64,
            pltpu.roll(low1, 32, 1),
            jnp.where(lane < 96, pltpu.roll(high0, 96, 1), high1),
        ),
    )


def pack_span(held, low, high, layer, first_span, lane):
    edge = jnp.where(first_span, high, low)
    shift = lax.rem(layer + jnp.where(first_span, 97, 0), 128)
    return jnp.where((lane & 31) == layer, pltpu.roll(edge, shift, 1), held)


def pack_field(f, trace, pair, first_span, lane, pitch_ref, span_held):
    halves = [trace[:, :CELLS], trace[:, CELLS:]]
    packed = pack_pitch([(h[0:16], h[16:32]) for h in halves], lane)
    pitch_ref[f, :, pair * CELLS : (pair + 1) * CELLS] = packed.astype(bf16)
    held = span_held[f]
    for h in range(2):
        held = pack_span(held, halves[h][32:48], halves[h][48:64], 2 * pair + h, first_span, lane)
    span_held[f] = held


def is_even():
    return (lax.axis_index("rans") & 1) == 0


def store_stream(up, down, near_chip_ref, far_chip_ref):
    even = is_even()
    near_chip_ref[...] = jnp.where(even, up, down)
    far_chip_ref[...] = jnp.where(even, down, up)


def from_below(near_chip_ref, far_chip_ref):
    even = is_even()
    return lambda f: jnp.where(even, far_chip_ref[f].astype(f32), near_chip_ref[f].astype(f32))


def from_above(near_chip_ref, far_chip_ref):
    even = is_even()
    return lambda f: jnp.where(even, near_chip_ref[f].astype(f32), far_chip_ref[f].astype(f32))


def prepare_kernel(
    rows_hbm, seeds_hbm, shape_hbm, v_hbm, plane_ref, core_ref, chip_ref, pitch_ref,
    span_ref, rows_ref, seeds_ref, shape_ref, v_ref, span_held, sems, *, normalizer,
):
    copies = [
        pltpu.make_async_copy(source, target, sems.at[i])
        for i, (source, target) in enumerate([
            (rows_hbm, rows_ref), (seeds_hbm, seeds_ref), (shape_hbm, shape_ref), (v_hbm, v_ref),
        ])
    ]
    for copy in copies:
        copy.start()
    first_span = lax.axis_index("span") == 0
    lane = lanes()
    pick = trace_selector()
    span_held[...] = jnp.zeros_like(span_held)
    for copy in copies[:3]:
        copy.wait()
    sum_eddies(rows_ref, seeds_ref, shape_ref, plane_ref, normalizer)
    copies[3].wait()
    for pair in range(EX // 2):
        at = slice(pair * PAIR, (pair + 1) * PAIR)
        for f in range(FIELDS):
            pack_field(
                f, dot(pick, v_ref[f, :, at]), pair, first_span, lane, pitch_ref, span_held
            )
    span_ref[...] = span_held[...].astype(bf16)
    store_stream(
        v_ref[:, 48:64, (EX - 1) * CELLS :], v_ref[:, 0:16, 0:CELLS], core_ref, chip_ref
    )


def mix(coefs, base, arrays):
    total = coefs[base] * arrays[0]
    for g in range(1, FIELDS):
        total = total + coefs[base + g] * arrays[g]
    return total


def mix_fluxes(read, coefs, mixed):
    def rows_step(r):
        def run():
            rows = [read(f, r, r + 16).astype(f32) for f in range(FIELDS)]
            for d in range(3):
                for f in range(FIELDS):
                    mixed[f, 64 * d + r : 64 * d + r + 16, :] = mix(
                        coefs, 25 * d + 5 * f, rows
                    ).astype(bf16)

        return run

    return [rows_step(r) for r in range(0, NODES, 16)]


def write_jumps(t, jumps, coefs, mixed, first_row):
    for f in range(FIELDS):
        mixed[f, first_row : first_row + 16, :] = mix(coefs, 75 + 25 * t + 5 * f, jumps).astype(bf16)


def mix_stream(read, lower, upper, coefs, mixed, row):
    def low():
        jumps = [lower(f) - read(f, 0, 16).astype(f32) for f in range(FIELDS)]
        write_jumps(0, jumps, coefs, mixed, row)

    def high():
        jumps = [upper(f) - read(f, 48, 64).astype(f32) for f in range(FIELDS)]
        write_jumps(1, jumps, coefs, mixed, row + 16)

    return [low, high]


def mix_sides(trace, pitch, span, layers, coefs, mixed, row, first_span, lane):
    def halves(f, r):
        own = trace(f, r, r + 16)
        return [own[:, h * CELLS : (h + 1) * CELLS] for h in range(len(layers))]

    def join(parts):
        return parts[0] if len(parts) == 1 else jnp.concatenate(parts, axis=1)

    def pitch_low():
        jumps = []
        for f in range(FIELDS):
            near, low, high = pitch(f), halves(f, 0), halves(f, 16)
            jumps.append(join([
                jnp.where(
                    lane < 32, pltpu.roll(near, 64 if h == 0 else 32, 1), pltpu.roll(high[h], 32, 1)
                ) - low[h]
                for h in range(len(layers))
            ]))
        write_jumps(2, jumps, coefs, mixed, row)

    def pitch_high():
        jumps = []
        for f in range(FIELDS):
            near, low, high = pitch(f), halves(f, 0), halves(f, 16)
            jumps.append(join([
                jnp.where(
                    lane >= 96, pltpu.roll(near, 96 if h == 0 else 64, 1), pltpu.roll(low[h], 96, 1)
                ) - high[h]
                for h in range(len(layers))
            ]))
        write_jumps(3, jumps, coefs, mixed, row + 16)

    def arrived(f, layer):
        return pltpu.roll(span(f), lax.rem(jnp.where(first_span, 31, 128) - layer, 128), 1)

    def span_low():
        jumps = []
        for f in range(FIELDS):
            low, high = halves(f, 32), halves(f, 48)
            jumps.append(join([
                jnp.where(
                    (lane & 31) == 0,
                    jnp.where(first_span, low[h], arrived(f, layer)),
                    pltpu.roll(high[h], 1, 1),
                ) - low[h]
                for h, layer in enumerate(layers)
            ]))
        write_jumps(4, jumps, coefs, mixed, row + 32)

    def span_high():
        jumps = []
        for f in range(FIELDS):
            low, high = halves(f, 32), halves(f, 48)
            jumps.append(join([
                jnp.where(
                    (lane & 31) == 31,
                    jnp.where(first_span, arrived(f, layer), high[h]),
                    pltpu.roll(low[h], 127, 1),
                ) - high[h]
                for h, layer in enumerate(layers)
            ]))
        write_jumps(5, jumps, coefs, mixed, row + 48)

    return [pitch_low, pitch_high, span_low, span_high]


def mix_wall(read, pinned, mixed, row):
    def run():
        for f in range(FIELDS):
            mixed[f, row : row + 64, :] = (read(f, 0, 64).astype(f32) * pinned()).astype(bf16)

    return [run]


def staggered(stages):
    held = [None] * FIELDS
    steps = []

    def step(stage, f):
        def run():
            held[f] = stage(f, held[f])

        return run

    for turn in range(FIELDS + len(stages) - 1):
        for k, stage in enumerate(stages):
            if 0 <= turn - k < FIELDS:
                steps.append(step(stage, turn - k))
    return steps


def interleave(first, second):
    count = max(len(first), len(second))
    for i in range(count):
        for steps in (first, second):
            for step in steps[i * len(steps) // count : (i + 1) * len(steps) // count]:
                step()


def pipeline(vector, matrix):
    for step in vector[0]:
        step()
    for p in range(len(matrix)):
        interleave(matrix[p], vector[p + 1] if p + 1 < len(vector) else [])


def finish(read, base, smooth):
    def trial(f, rate):
        v = read(f, 0, 64).astype(f32)
        if base is None:
            now = v - TIME_STEP * rate
        else:
            now = 0.5 * (base(f).astype(f32) + v - TIME_STEP * rate)
        return dot(smooth, now.astype(bf16))

    return trial


def with_traces(filter_matrix, pick):
    return jnp.concatenate([filter_matrix, dot(pick, filter_matrix).astype(bf16)], axis=0)


def mix_traces(read, pick, own):
    def run():
        for f in range(FIELDS):
            own[f] = dot(pick, read(f, 0, 64)).astype(bf16)

    return [run]


def place(pair):
    return slice(pair * PAIR, (pair + 1) * PAIR)


def lower_pair(v_ref, edge, pair):
    def lower(f):
        if pair:
            return v_ref[f, 48:64, pair * PAIR - CELLS : (pair + 1) * PAIR - CELLS].astype(f32)
        return jnp.concatenate([edge(f), v_ref[f, 48:64, 0:CELLS].astype(f32)], axis=1)

    return lower


def upper_pair(v_ref, above, pair):
    first = pair * PAIR + CELLS
    last_rans = lax.axis_index("rans") == lax.axis_size("rans") - 1

    def upper(f):
        if pair < EX // 2 - 1:
            return v_ref[f, 0:16, first : first + PAIR].astype(f32)
        edge = jnp.where(
            last_rans, v_ref[f, 48:64, first : first + CELLS].astype(f32), above(f)
        )
        return jnp.concatenate([v_ref[f, 0:16, first : first + CELLS].astype(f32), edge], axis=1)

    return upper


def phase_one_kernel(
    v_ref, from_core_ref, from_chip_ref, near_ref, far_ref, pin_ref, coefs, weights_ref, filter_ref,
    out_ref, out_trace_ref, core_ref, chip_ref, pitch_ref, span_ref, mixed, own, span_held,
):
    first_span = lax.axis_index("span") == 0
    lane = lanes()
    pick = trace_selector()
    weights, smooth = weights_ref[...], with_traces(filter_ref[...], pick)
    span_held[...] = jnp.zeros_like(span_held)
    below, above = from_below(from_core_ref, from_chip_ref), from_above(from_core_ref, from_chip_ref)
    vector, matrix = [], []

    def add(pair):
        at = place(pair)
        rows, held = mixed.at[pair % 2], own.at[pair % 2]

        def read(f, r0, r1):
            return v_ref[f, r0:r1, at]

        def store(f, value):
            out_ref[f, :, at] = value[0:64].astype(bf16)
            trace = value[64:128]
            out_trace_ref[f, :, at] = trace.astype(bf16)
            pack_field(f, trace, pair, first_span, lane, pitch_ref, span_held)

        vector.append(
            mix_traces(read, pick, held)
            + mix_fluxes(read, coefs, rows)
            + mix_stream(
                read,
                lower_pair(v_ref, below, pair),
                upper_pair(v_ref, above, pair),
                coefs, rows, 192,
            )
            + mix_sides(
                lambda f, r0, r1: held[f, r0:r1].astype(f32),
                lambda f: near_ref[f, :, pair * CELLS : (pair + 1) * CELLS].astype(f32),
                lambda f: far_ref[f].astype(f32),
                [2 * pair, 2 * pair + 1], coefs, rows, 224, first_span, lane,
            )
            + mix_wall(read, lambda: pin_ref[:, at].astype(f32), rows, 288)
        )
        matrix.append(
            staggered([lambda f, _: dot(weights, rows[f]), finish(read, None, smooth), store])
        )

    for pair in range(EX // 2):
        add(pair)
    pipeline(vector, matrix)
    span_ref[...] = span_held[...].astype(bf16)
    store_stream(
        out_ref[:, 48:64, (EX - 1) * CELLS :], out_ref[:, 0:16, 0:CELLS], core_ref, chip_ref
    )


def inner_two_kernel(v_ref, coefs, weights_ref, part_ref, mixed):
    weights = weights_ref[...]
    vector, matrix = [], []

    def add(pair):
        at = place(pair)
        rows = mixed.at[pair % 2]

        def store(f, value):
            part_ref[f, :, at] = value

        vector.append(mix_fluxes(lambda f, r0, r1: v_ref[f, r0:r1, at], coefs, rows))
        matrix.append(staggered([lambda f, _: dot(weights, rows[f]), store]))

    for pair in range(EX // 2):
        add(pair)
    pipeline(vector, matrix)


def outer_two_kernel(
    v_ref, trace_ref, base_ref, part_ref, mean_ref, amp_ref, plane_ref, from_core_ref, from_chip_ref,
    near_ref, far_ref, pin_ref, coefs, weights_ref, smooth_ref, out_ref, mixed,
):
    first_span = lax.axis_index("span") == 0
    first_rans = lax.axis_index("rans") == 0
    lane = lanes()
    weights, smooth = weights_ref[...], smooth_ref[...]
    below, above = from_below(from_core_ref, from_chip_ref), from_above(from_core_ref, from_chip_ref)
    vector, matrix = [], []

    def edge(f):
        return jnp.where(first_rans, inflow_of(mean_ref, amp_ref, plane_ref)(f), below(f))

    def add(pair):
        at = place(pair)
        rows = mixed.at[pair % 2]

        def read(f, r0, r1):
            return v_ref[f, r0:r1, at]

        def store(f, value):
            out_ref[f, :, at] = value.astype(bf16)

        vector.append(
            mix_stream(
                read, lower_pair(v_ref, edge, pair), upper_pair(v_ref, above, pair), coefs, rows, 0
            )
            + mix_sides(
                lambda f, r0, r1: trace_ref[f, r0:r1, at].astype(f32),
                lambda f: near_ref[f, :, pair * CELLS : (pair + 1) * CELLS].astype(f32),
                lambda f: far_ref[f].astype(f32),
                [2 * pair, 2 * pair + 1], coefs, rows, 32, first_span, lane,
            )
            + mix_wall(read, lambda: pin_ref[:, at].astype(f32), rows, 96)
        )
        matrix.append(
            staggered([
                lambda f, _: dot(weights, rows[f]) + part_ref[f, :, at],
                finish(read, lambda f: base_ref[f, :, at], smooth),
                store,
            ])
        )

    for pair in range(EX // 2):
        add(pair)
    pipeline(vector, matrix)


def inflow_of(mean_ref, amp_ref, plane_ref):
    return lambda f: mean_ref[f] + amp_ref[f] * plane_ref[f]


def inflow_kernel(
    held_ref, held_trace_ref, held_pitch_ref, held_span_ref, v_ref, mean_ref, amp_ref,
    plane_ref, near_ref, far_ref, pin_ref, coefs, weights_ref, filter_ref, out_ref, out_trace_ref,
    pitch_ref, span_ref, mixed, own,
):
    first_span = lax.axis_index("span") == 0
    first_rans = lax.axis_index("rans") == 0
    lane = lanes()

    @pl.when(first_rans)
    def _():
        pick = trace_selector()
        weights, smooth = weights_ref[...], with_traces(filter_ref[...], pick)

        def read(f, r0, r1):
            return v_ref[f, r0:r1, 0:CELLS]

        def store(f, value):
            out_ref[f] = value[0:64].astype(bf16)
            t = value[64:128]
            out_trace_ref[f] = t.astype(bf16)
            pitch = jnp.where(lane < 32, t[0:16], pltpu.roll(t[16:32], 96, 1))
            pitch_ref[f] = jnp.where(
                (lane & 63) < 32, pitch, held_pitch_ref[f].astype(f32)
            ).astype(bf16)
            span_ref[f] = pack_span(
                held_span_ref[f].astype(f32), t[32:48], t[48:64], 0, first_span, lane
            ).astype(bf16)

        vector = (
            mix_traces(read, pick, own)
            + mix_stream(
                read,
                inflow_of(mean_ref, amp_ref, plane_ref),
                lambda f: v_ref[f, 0:16, CELLS:PAIR].astype(f32),
                coefs, mixed, 192,
            )
            + mix_sides(
                lambda f, r0, r1: own[f, r0:r1].astype(f32),
                lambda f: near_ref[f].astype(f32),
                lambda f: far_ref[f].astype(f32),
                [0], coefs, mixed, 224, first_span, lane,
            )
            + mix_fluxes(read, coefs, mixed)
            + mix_wall(read, lambda: pin_ref[...].astype(f32), mixed, 288)
        )
        matrix = staggered(
            [lambda f, _: dot(weights, mixed[f]), finish(read, None, smooth), store]
        )
        pipeline([vector], [matrix])

    @pl.when(jnp.logical_not(first_rans))
    def _():
        out_ref[...] = held_ref[...]
        out_trace_ref[...] = held_trace_ref[...]
        pitch_ref[...] = held_pitch_ref[...]
        span_ref[...] = held_span_ref[...]


VMEM = pl.BlockSpec(memory_space=pltpu.VMEM)
SMEM = pl.BlockSpec(memory_space=pltpu.SMEM)
PARAMS = pltpu.CompilerParams(vmem_limit_bytes=40 * 2**20)


def shape_of(*dims, dtype=bf16):
    return jax.ShapeDtypeStruct(dims, dtype)


def front(*dims):
    return pl.BlockSpec(dims, lambda i: (0,) * len(dims))


def cost(us):
    return pl.CostEstimate(flops=int(us * 1e8), bytes_accessed=int(us * 3e6), transcendentals=0)


def body(
    solution, volume_ops, flux_jacobian, lift_matrix, filter_matrix, wall_matrix, pinched_map,
    mode_rows, mode_seeds, mode_shape, mean_inflow, eddy_amplitude,
):
    ranks = lax.axis_size("rans")
    eddies, foot = mode_shape.shape[2:]
    plane_rows = mean_inflow.shape[3]
    faces = shape_of(FIELDS, 16, CELLS)
    def gather_sum(value, offsets, roots):
        parts = [lax.ppermute(value, "rans", [(r + o, r) for r in roots]) for o in offsets]
        for part in parts:
            value = value + part
        return value

    weights = jnp.concatenate(
        [volume_ops[0], volume_ops[1], volume_ops[2], lift_matrix, wall_matrix], axis=1
    )
    identity = jnp.eye(FIELDS, dtype=f32)
    sides = jnp.array([-1.0, 1.0], f32)
    face_coefs = (
        0.5 * sides[None, :, None, None] * flux_jacobian[:, None] - 0.5 * identity
    ).reshape(-1)
    coefs = jnp.concatenate([flux_jacobian.reshape(-1), face_coefs])
    pins = pinched_map.reshape(1, -1)
    fixed_specs = [VMEM, SMEM, VMEM, VMEM]
    elements = solution.shape[2]
    traces = shape_of(FIELDS, NODES, elements)
    sends = (faces, faces, shape_of(FIELDS, 16, EX // 2 * CELLS), faces)
    swap = [(0, 1), (1, 0)]
    same_chip = [(i, i ^ 1) for i in range(ranks)]
    next_chip = [(a + 1, b + 1) for a, b in same_chip if max(a, b) + 1 < ranks]

    span_scratch = pltpu.VMEM((FIELDS, 16, CELLS), f32)
    plane, core, chip, pitch, span = pl.pallas_call(
        functools.partial(
            prepare_kernel, normalizer=float((plane_rows / (eddies * ranks * foot)) ** 0.5)
        ),
        out_shape=(shape_of(FIELDS, 16, CELLS, dtype=f32),) + sends,
        in_specs=[pl.BlockSpec(memory_space=pltpu.HBM)] * 4,
        out_specs=(VMEM,) * 5,
        scratch_shapes=[
            pltpu.VMEM((foot, eddies), jnp.int32),
            pltpu.VMEM((1, eddies), jnp.int32),
            pltpu.VMEM((foot, eddies), f32),
            pltpu.VMEM(solution.shape, bf16),
            span_scratch,
            pltpu.SemaphoreType.DMA((4,)),
        ],
        compiler_params=pltpu.CompilerParams(vmem_limit_bytes=60 * 2**20),
        cost_estimate=cost(5),
        name="prepare",
    )(mode_rows[0, 0].T, mode_seeds.reshape(1, eddies), mode_shape[0, 0].T, solution)
    plane = gather_sum(plane, (2, 6, 4), [8 * z + c for z in range(8) for c in range(2)])
    near = lax.ppermute(pitch, "pitch", swap)
    from_chip = lax.ppermute(chip, "rans", next_chip)
    plane, core, span = lax.optimization_barrier((plane, core, span))
    plane = gather_sum(plane, (1, 8, 9), [0, 16, 32, 48])
    core, span, near, from_chip = lax.optimization_barrier((core, span, near, from_chip))
    far = lax.ppermute(span, "span", swap)
    from_core = lax.ppermute(core, "rans", same_chip)
    plane, near, far, from_core, from_chip = lax.optimization_barrier(
        (plane, near, far, from_core, from_chip)
    )
    plane = gather_sum(plane, (16, 48, 32), [0])

    phase_one, trace_one, core, chip, pitch, span = pl.pallas_call(
        phase_one_kernel,
        out_shape=(traces, traces) + sends,
        in_specs=[VMEM] * 5 + fixed_specs,
        out_specs=(VMEM,) * 6,
        scratch_shapes=[
            pltpu.VMEM((2, FIELDS, MIXED, PAIR), bf16),
            pltpu.VMEM((2, FIELDS, NODES, PAIR), bf16),
            span_scratch,
        ],
        compiler_params=PARAMS,
        cost_estimate=cost(6),
        name="phase_one",
    )(solution, from_core, from_chip, near, far, pins, coefs, weights, filter_matrix)
    from_core = lax.ppermute(core, "rans", same_chip)
    from_chip = lax.ppermute(chip, "rans", next_chip)
    mean = mean_inflow.reshape(FIELDS, 16, CELLS)
    amplitude = eddy_amplitude.reshape(FIELDS, 16, CELLS)
    layer = front(FIELDS, NODES, CELLS)
    face = front(FIELDS, 16, CELLS)
    phase_one, trace_one, pitch, span = pl.pallas_call(
        inflow_kernel,
        grid=(1,),
        out_shape=(traces, traces, sends[2], sends[3]),
        in_specs=[layer, layer, face, face, front(FIELDS, NODES, PAIR)]
        + [face] * 5
        + [front(1, CELLS), SMEM, front(NODES, MIXED), front(NODES, NODES)],
        out_specs=(layer, layer, face, face),
        scratch_shapes=[
            pltpu.VMEM((FIELDS, MIXED, CELLS), bf16),
            pltpu.VMEM((FIELDS, NODES, CELLS), bf16),
        ],
        input_output_aliases={0: 0, 1: 1, 2: 2, 3: 3},
        compiler_params=PARAMS,
        cost_estimate=cost(1),
        name="inflow_layer",
    )(
        phase_one, trace_one, pitch, span, solution, mean, amplitude, plane, near, far,
        pins, coefs, weights, filter_matrix,
    )
    near = lax.ppermute(pitch, "pitch", swap)
    far = lax.ppermute(span, "span", swap)
    part = pl.pallas_call(
        inner_two_kernel,
        out_shape=shape_of(FIELDS, NODES, elements, dtype=f32),
        in_specs=[VMEM, SMEM, VMEM],
        out_specs=VMEM,
        scratch_shapes=[pltpu.VMEM((2, FIELDS, INNER, PAIR), bf16)],
        compiler_params=PARAMS,
        cost_estimate=cost(3),
        name="inner_two",
    )(phase_one, coefs, weights[:, :INNER])
    return pl.pallas_call(
        outer_two_kernel,
        out_shape=traces,
        in_specs=[VMEM] * 12 + fixed_specs[1:],
        out_specs=VMEM,
        scratch_shapes=[pltpu.VMEM((2, FIELDS, MIXED - INNER, PAIR), bf16)],
        compiler_params=PARAMS,
        cost_estimate=cost(4),
        name="outer_two",
    )(
        phase_one, trace_one, solution, part, mean, amplitude, plane, from_core, from_chip, near, far,
        pins, coefs, weights[:, INNER:], filter_matrix,
    )


def solution(mesh):
    spread = P(None, None, ("rans", "pitch", "span"))
    in_specs = (
        spread,
        P(),
        P(),
        P(),
        P(),
        P(),
        P(("rans", "pitch", "span")),
        P("pitch", "span", "rans", None),
        P("pitch", "span", "rans"),
        P("pitch", "span", "rans", None),
        P("pitch", "span", None, None),
        P("pitch", "span", None, None),
    )
    return jax.shard_map(body, mesh=mesh, in_specs=in_specs, out_specs=spread, check_vma=False)
```

```python
import functools

import jax
import jax.numpy as jnp
from jax import lax
from jax.experimental import pallas as pl
from jax.experimental.pallas import tpu as pltpu
from jax.sharding import PartitionSpec as P

FIELDS = 5
NODES = 64
EX = 12
CELLS = 128
SPAN_CELLS = 32
PAIR = 2 * CELLS
MIXED = 352
INNER = 192
TIME_STEP = 0.4
f32 = jnp.float32
bf16 = jnp.bfloat16


def trace_selector():
    row = lax.broadcasted_iota(jnp.int32, (64, 64), 0)
    node = lax.broadcasted_iota(jnp.int32, (64, 64), 1)
    face, first, second = row >> 4, (row >> 2) & 3, row & 3
    on_pitch = second + jnp.where(face == 1, 12, 0)
    on_span = 4 * second + jnp.where(face == 3, 3, 0)
    source = 16 * first + jnp.where(face < 2, on_pitch, on_span)
    return jnp.where(node == source, 1.0, 0.0).astype(bf16)


def dot(a, b):
    return jnp.dot(a, b, preferred_element_type=f32)


def lanes():
    return lax.broadcasted_iota(jnp.int32, (16, CELLS), 1)


def sum_eddies(rows_ref, seeds_ref, shape_ref, plane_ref, normalizer):
    seeds = seeds_ref[...]
    signs = [(2 * ((seeds >> f) & 1) - 1).astype(f32) for f in range(FIELDS)]
    signs = [jnp.broadcast_to(s, (32, s.shape[1])).astype(bf16) for s in signs]
    eddies = rows_ref.shape[1]
    high_row = lax.broadcasted_iota(jnp.int32, (16, eddies), 0)
    low_row = lax.broadcasted_iota(jnp.int32, (CELLS, eddies), 0)

    def chunk(i, total):
        start = pl.multiple_of(i * 8, 8)
        rows = rows_ref[pl.ds(start, 8), :]
        shapes = shape_ref[pl.ds(start, 8), :]
        for q in range(8):
            row, shape = rows[q : q + 1], shapes[q : q + 1]
            placed = jnp.where((row >> 7) == high_row, shape, 0.0)
            coarse = placed.astype(bf16)
            fine = (placed - coarse.astype(f32)).astype(bf16)
            both = jnp.concatenate([coarse, fine], axis=0)
            signed = jnp.concatenate([both * s for s in signs], axis=0)
            hot = jnp.where((row & 127) == low_row, 1.0, 0.0).astype(bf16)
            total = total + lax.dot_general(
                signed, hot, (((1,), (1,)), ((), ())), preferred_element_type=f32
            )
        return total

    total = lax.fori_loop(0, rows_ref.shape[0] // 8, chunk, jnp.zeros((160, CELLS), f32))
    for f in range(FIELDS):
        plane_ref[f] = (total[32 * f : 32 * f + 16] + total[32 * f + 16 : 32 * f + 32]) * normalizer


def pack_pitch(traces, lane):
    (low0, high0), (low1, high1) = traces
    return jnp.where(
        lane < 32,
        low0,
        jnp.where(
            lane < 64,
            pltpu.roll(low1, 32, 1),
            jnp.where(lane < 96, pltpu.roll(high0, 96, 1), high1),
        ),
    )


def pack_span(held, low, high, layer, first_span, lane):
    edge = jnp.where(first_span, high, low)
    shift = lax.rem(layer + jnp.where(first_span, 97, 0), 128)
    return jnp.where((lane & 31) == layer, pltpu.roll(edge, shift, 1), held)


def pack_field(f, trace, pair, first_span, lane, pitch_ref, span_held):
    halves = [trace[:, :CELLS], trace[:, CELLS:]]
    packed = pack_pitch([(h[0:16], h[16:32]) for h in halves], lane)
    pitch_ref[f, :, pair * CELLS : (pair + 1) * CELLS] = packed.astype(bf16)
    held = span_held[f]
    for h in range(2):
        held = pack_span(held, halves[h][32:48], halves[h][48:64], 2 * pair + h, first_span, lane)
    span_held[f] = held


def is_even():
    return (lax.axis_index("rans") & 1) == 0


def store_stream(up, down, near_chip_ref, far_chip_ref):
    even = is_even()
    near_chip_ref[...] = jnp.where(even, up, down)
    far_chip_ref[...] = jnp.where(even, down, up)


def from_below(near_chip_ref, far_chip_ref):
    even = is_even()
    return lambda f: jnp.where(even, far_chip_ref[f].astype(f32), near_chip_ref[f].astype(f32))


def from_above(near_chip_ref, far_chip_ref):
    even = is_even()
    return lambda f: jnp.where(even, near_chip_ref[f].astype(f32), far_chip_ref[f].astype(f32))


def prepare_kernel(
    rows_hbm, seeds_hbm, shape_hbm, v_hbm, plane_ref, core_ref, chip_ref, pitch_ref,
    span_ref, rows_ref, seeds_ref, shape_ref, v_ref, span_held, sems, *, normalizer,
):
    copies = [
        pltpu.make_async_copy(source, target, sems.at[i])
        for i, (source, target) in enumerate([
            (rows_hbm, rows_ref), (seeds_hbm, seeds_ref), (shape_hbm, shape_ref), (v_hbm, v_ref),
        ])
    ]
    for copy in copies:
        copy.start()
    first_span = lax.axis_index("span") == 0
    lane = lanes()
    pick = trace_selector()
    span_held[...] = jnp.zeros_like(span_held)
    for copy in copies[:3]:
        copy.wait()
    sum_eddies(rows_ref, seeds_ref, shape_ref, plane_ref, normalizer)
    copies[3].wait()
    for pair in range(EX // 2):
        at = slice(pair * PAIR, (pair + 1) * PAIR)
        for f in range(FIELDS):
            pack_field(
                f, dot(pick, v_ref[f, :, at]), pair, first_span, lane, pitch_ref, span_held
            )
    span_ref[...] = span_held[...].astype(bf16)
    store_stream(
        v_ref[:, 48:64, (EX - 1) * CELLS :], v_ref[:, 0:16, 0:CELLS], core_ref, chip_ref
    )


def mix(row, arrays):
    total = row[0] * arrays[0]
    for g in range(1, FIELDS):
        total = total + row[g] * arrays[g]
    return total


def flux_row(jacobian, d, f):
    return [jacobian[f, d, g] for g in range(FIELDS)]


def face_row(jacobian, t, f):
    half = 0.5 * (1.0 if t % 2 else -1.0)
    row = [half * jacobian[f, t // 2, g] for g in range(FIELDS)]
    row[f] = row[f] - 0.5
    return row


def fill(weights, parts):
    column = 0
    for part in parts:
        weights[:, column : column + part.shape[1]] = part
        column += part.shape[1]
    return weights[...]


def mix_fluxes(read, coefs, mixed):
    def rows_step(r):
        def run():
            rows = [read(f, r, r + 16).astype(f32) for f in range(FIELDS)]
            for d in range(3):
                for f in range(FIELDS):
                    mixed[f, 64 * d + r : 64 * d + r + 16, :] = mix(
                        flux_row(coefs, d, f), rows
                    ).astype(bf16)

        return run

    return [rows_step(r) for r in range(0, NODES, 16)]


def write_jumps(t, jumps, coefs, mixed, first_row):
    for f in range(FIELDS):
        mixed[f, first_row : first_row + 16, :] = mix(face_row(coefs, t, f), jumps).astype(bf16)


def mix_stream(read, lower, upper, coefs, mixed, row):
    def low():
        jumps = [lower(f) - read(f, 0, 16).astype(f32) for f in range(FIELDS)]
        write_jumps(0, jumps, coefs, mixed, row)

    def high():
        jumps = [upper(f) - read(f, 48, 64).astype(f32) for f in range(FIELDS)]
        write_jumps(1, jumps, coefs, mixed, row + 16)

    return [low, high]


def mix_sides(trace, pitch, span, layers, coefs, mixed, row, first_span, lane):
    def halves(f, r):
        own = trace(f, r, r + 16)
        return [own[:, h * CELLS : (h + 1) * CELLS] for h in range(len(layers))]

    def join(parts):
        return parts[0] if len(parts) == 1 else jnp.concatenate(parts, axis=1)

    def pitch_low():
        jumps = []
        for f in range(FIELDS):
            near, low, high = pitch(f), halves(f, 0), halves(f, 16)
            jumps.append(join([
                jnp.where(
                    lane < 32, pltpu.roll(near, 64 if h == 0 else 32, 1), pltpu.roll(high[h], 32, 1)
                ) - low[h]
                for h in range(len(layers))
            ]))
        write_jumps(2, jumps, coefs, mixed, row)

    def pitch_high():
        jumps = []
        for f in range(FIELDS):
            near, low, high = pitch(f), halves(f, 0), halves(f, 16)
            jumps.append(join([
                jnp.where(
                    lane >= 96, pltpu.roll(near, 96 if h == 0 else 64, 1), pltpu.roll(low[h], 96, 1)
                ) - high[h]
                for h in range(len(layers))
            ]))
        write_jumps(3, jumps, coefs, mixed, row + 16)

    def arrived(f, layer):
        return pltpu.roll(span(f), lax.rem(jnp.where(first_span, 31, 128) - layer, 128), 1)

    def span_low():
        jumps = []
        for f in range(FIELDS):
            low, high = halves(f, 32), halves(f, 48)
            jumps.append(join([
                jnp.where(
                    (lane & 31) == 0,
                    jnp.where(first_span, low[h], arrived(f, layer)),
                    pltpu.roll(high[h], 1, 1),
                ) - low[h]
                for h, layer in enumerate(layers)
            ]))
        write_jumps(4, jumps, coefs, mixed, row + 32)

    def span_high():
        jumps = []
        for f in range(FIELDS):
            low, high = halves(f, 32), halves(f, 48)
            jumps.append(join([
                jnp.where(
                    (lane & 31) == 31,
                    jnp.where(first_span, arrived(f, layer), high[h]),
                    pltpu.roll(low[h], 127, 1),
                ) - high[h]
                for h, layer in enumerate(layers)
            ]))
        write_jumps(5, jumps, coefs, mixed, row + 48)

    return [pitch_low, pitch_high, span_low, span_high]


def mix_wall(read, pinned, mixed, row):
    def run():
        for f in range(FIELDS):
            mixed[f, row : row + 64, :] = (read(f, 0, 64).astype(f32) * pinned()).astype(bf16)

    return [run]


def staggered(stages):
    held = [None] * FIELDS
    steps = []

    def step(stage, f):
        def run():
            held[f] = stage(f, held[f])

        return run

    for turn in range(FIELDS + len(stages) - 1):
        for k, stage in enumerate(stages):
            if 0 <= turn - k < FIELDS:
                steps.append(step(stage, turn - k))
    return steps


def interleave(first, second):
    count = max(len(first), len(second))
    for i in range(count):
        for steps in (first, second):
            for step in steps[i * len(steps) // count : (i + 1) * len(steps) // count]:
                step()


def pipeline(vector, matrix):
    for step in vector[0]:
        step()
    for p in range(len(matrix)):
        interleave(matrix[p], vector[p + 1] if p + 1 < len(vector) else [])


def finish(read, base, smooth):
    def trial(f, rate):
        v = read(f, 0, 64).astype(f32)
        if base is None:
            now = v - TIME_STEP * rate
        else:
            now = 0.5 * (base(f).astype(f32) + v - TIME_STEP * rate)
        return dot(smooth, now.astype(bf16))

    return trial


def with_traces(filter_matrix, pick):
    return jnp.concatenate([filter_matrix, dot(pick, filter_matrix).astype(bf16)], axis=0)


def mix_traces(read, pick, own):
    def run():
        for f in range(FIELDS):
            own[f] = dot(pick, read(f, 0, 64)).astype(bf16)

    return [run]


def place(pair):
    return slice(pair * PAIR, (pair + 1) * PAIR)


def lower_pair(v_ref, edge, pair):
    def lower(f):
        if pair:
            return v_ref[f, 48:64, pair * PAIR - CELLS : (pair + 1) * PAIR - CELLS].astype(f32)
        return jnp.concatenate([edge(f), v_ref[f, 48:64, 0:CELLS].astype(f32)], axis=1)

    return lower


def upper_pair(v_ref, above, pair):
    first = pair * PAIR + CELLS
    last_rans = lax.axis_index("rans") == lax.axis_size("rans") - 1

    def upper(f):
        if pair < EX // 2 - 1:
            return v_ref[f, 0:16, first : first + PAIR].astype(f32)
        edge = jnp.where(
            last_rans, v_ref[f, 48:64, first : first + CELLS].astype(f32), above(f)
        )
        return jnp.concatenate([v_ref[f, 0:16, first : first + CELLS].astype(f32), edge], axis=1)

    return upper


def phase_one_kernel(
    v_ref, from_core_ref, from_chip_ref, near_ref, far_ref, pin_ref, coefs, volume_ref, lift_ref,
    wall_ref, filter_ref,
    out_ref, out_trace_ref, core_ref, chip_ref, pitch_ref, span_ref, mixed, own, weights_held,
    span_held,
):
    first_span = lax.axis_index("span") == 0
    lane = lanes()
    pick = trace_selector()
    smooth = with_traces(filter_ref[...], pick)
    weights = fill(
        weights_held, [volume_ref[0], volume_ref[1], volume_ref[2], lift_ref[...], wall_ref[...]]
    )
    span_held[...] = jnp.zeros_like(span_held)
    below, above = from_below(from_core_ref, from_chip_ref), from_above(from_core_ref, from_chip_ref)
    vector, matrix = [], []

    def add(pair):
        at = place(pair)
        rows, held = mixed.at[pair % 2], own.at[pair % 2]

        def read(f, r0, r1):
            return v_ref[f, r0:r1, at]

        def store(f, value):
            out_ref[f, :, at] = value[0:64].astype(bf16)
            trace = value[64:128]
            out_trace_ref[f, :, at] = trace.astype(bf16)
            pack_field(f, trace, pair, first_span, lane, pitch_ref, span_held)

        vector.append(
            mix_traces(read, pick, held)
            + mix_fluxes(read, coefs, rows)
            + mix_stream(
                read,
                lower_pair(v_ref, below, pair),
                upper_pair(v_ref, above, pair),
                coefs, rows, 192,
            )
            + mix_sides(
                lambda f, r0, r1: held[f, r0:r1].astype(f32),
                lambda f: near_ref[f, :, pair * CELLS : (pair + 1) * CELLS].astype(f32),
                lambda f: far_ref[f].astype(f32),
                [2 * pair, 2 * pair + 1], coefs, rows, 224, first_span, lane,
            )
            + mix_wall(read, lambda: pin_ref[:, at].astype(f32), rows, 288)
        )
        matrix.append(
            staggered([lambda f, _: dot(weights, rows[f]), finish(read, None, smooth), store])
        )

    for pair in range(EX // 2):
        add(pair)
    pipeline(vector, matrix)
    span_ref[...] = span_held[...].astype(bf16)
    store_stream(
        out_ref[:, 48:64, (EX - 1) * CELLS :], out_ref[:, 0:16, 0:CELLS], core_ref, chip_ref
    )


def inner_two_kernel(v_ref, coefs, volume_ref, part_ref, mixed, weights_held):
    weights = fill(weights_held, [volume_ref[d] for d in range(3)])
    vector, matrix = [], []

    def add(pair):
        at = place(pair)
        rows = mixed.at[pair % 2]

        def store(f, value):
            part_ref[f, :, at] = value

        vector.append(mix_fluxes(lambda f, r0, r1: v_ref[f, r0:r1, at], coefs, rows))
        matrix.append(staggered([lambda f, _: dot(weights, rows[f]), store]))

    for pair in range(EX // 2):
        add(pair)
    pipeline(vector, matrix)


def outer_two_kernel(
    v_ref, trace_ref, base_ref, part_ref, mean_ref, amp_ref, plane_ref, from_core_ref, from_chip_ref,
    near_ref, far_ref, pin_ref, coefs, lift_ref, wall_ref, smooth_ref, out_ref, mixed, weights_held,
):
    first_span = lax.axis_index("span") == 0
    first_rans = lax.axis_index("rans") == 0
    lane = lanes()
    weights, smooth = fill(weights_held, [lift_ref[...], wall_ref[...]]), smooth_ref[...]
    below, above = from_below(from_core_ref, from_chip_ref), from_above(from_core_ref, from_chip_ref)
    vector, matrix = [], []

    def edge(f):
        return jnp.where(first_rans, inflow_of(mean_ref, amp_ref, plane_ref)(f), below(f))

    def add(pair):
        at = place(pair)
        rows = mixed.at[pair % 2]

        def read(f, r0, r1):
            return v_ref[f, r0:r1, at]

        def store(f, value):
            out_ref[f, :, at] = value.astype(bf16)

        vector.append(
            mix_stream(
                read, lower_pair(v_ref, edge, pair), upper_pair(v_ref, above, pair), coefs, rows, 0
            )
            + mix_sides(
                lambda f, r0, r1: trace_ref[f, r0:r1, at].astype(f32),
                lambda f: near_ref[f, :, pair * CELLS : (pair + 1) * CELLS].astype(f32),
                lambda f: far_ref[f].astype(f32),
                [2 * pair, 2 * pair + 1], coefs, rows, 32, first_span, lane,
            )
            + mix_wall(read, lambda: pin_ref[:, at].astype(f32), rows, 96)
        )
        matrix.append(
            staggered([
                lambda f, _: dot(weights, rows[f]) + part_ref[f, :, at],
                finish(read, lambda f: base_ref[f, :, at], smooth),
                store,
            ])
        )

    for pair in range(EX // 2):
        add(pair)
    pipeline(vector, matrix)


def inflow_of(mean_ref, amp_ref, plane_ref):
    return lambda f: mean_ref[f] + amp_ref[f] * plane_ref[f]


def inflow_kernel(
    held_ref, held_trace_ref, held_pitch_ref, held_span_ref, v_ref, mean_ref, amp_ref,
    plane_ref, near_ref, far_ref, pin_ref, coefs, volume_ref, lift_ref, wall_ref, filter_ref, out_ref,
    out_trace_ref,
    pitch_ref, span_ref, mixed, own, weights_held,
):
    first_span = lax.axis_index("span") == 0
    first_rans = lax.axis_index("rans") == 0
    lane = lanes()

    @pl.when(first_rans)
    def _():
        pick = trace_selector()
        smooth = with_traces(filter_ref[...], pick)
        weights = fill(
            weights_held, [volume_ref[0], volume_ref[1], volume_ref[2], lift_ref[...], wall_ref[...]]
        )

        def read(f, r0, r1):
            return v_ref[f, r0:r1, 0:CELLS]

        def store(f, value):
            out_ref[f] = value[0:64].astype(bf16)
            t = value[64:128]
            out_trace_ref[f] = t.astype(bf16)
            pitch = jnp.where(lane < 32, t[0:16], pltpu.roll(t[16:32], 96, 1))
            pitch_ref[f] = jnp.where(
                (lane & 63) < 32, pitch, held_pitch_ref[f].astype(f32)
            ).astype(bf16)
            span_ref[f] = pack_span(
                held_span_ref[f].astype(f32), t[32:48], t[48:64], 0, first_span, lane
            ).astype(bf16)

        vector = (
            mix_traces(read, pick, own)
            + mix_stream(
                read,
                inflow_of(mean_ref, amp_ref, plane_ref),
                lambda f: v_ref[f, 0:16, CELLS:PAIR].astype(f32),
                coefs, mixed, 192,
            )
            + mix_sides(
                lambda f, r0, r1: own[f, r0:r1].astype(f32),
                lambda f: near_ref[f].astype(f32),
                lambda f: far_ref[f].astype(f32),
                [0], coefs, mixed, 224, first_span, lane,
            )
            + mix_fluxes(read, coefs, mixed)
            + mix_wall(read, lambda: pin_ref[...].astype(f32), mixed, 288)
        )
        matrix = staggered(
            [lambda f, _: dot(weights, mixed[f]), finish(read, None, smooth), store]
        )
        pipeline([vector], [matrix])

    @pl.when(jnp.logical_not(first_rans))
    def _():
        out_ref[...] = held_ref[...]
        out_trace_ref[...] = held_trace_ref[...]
        pitch_ref[...] = held_pitch_ref[...]
        span_ref[...] = held_span_ref[...]


VMEM = pl.BlockSpec(memory_space=pltpu.VMEM)
SMEM = pl.BlockSpec(memory_space=pltpu.SMEM)
PARAMS = pltpu.CompilerParams(vmem_limit_bytes=40 * 2**20)


def shape_of(*dims, dtype=bf16):
    return jax.ShapeDtypeStruct(dims, dtype)


def front(*dims):
    return pl.BlockSpec(dims, lambda i: (0,) * len(dims))


def cost(us):
    return pl.CostEstimate(flops=int(us * 1e8), bytes_accessed=int(us * 3e6), transcendentals=0)


def body(
    solution, volume_ops, flux_jacobian, lift_matrix, filter_matrix, wall_matrix, pinched_map,
    mode_rows, mode_seeds, mode_shape, mean_inflow, eddy_amplitude,
):
    ranks = lax.axis_size("rans")
    eddies, foot = mode_shape.shape[2:]
    plane_rows = mean_inflow.shape[3]
    faces = shape_of(FIELDS, 16, CELLS)
    def gather_sum(value, offsets, roots):
        parts = [lax.ppermute(value, "rans", [(r + o, r) for r in roots]) for o in offsets]
        for part in parts:
            value = value + part
        return value

    jacobian = flux_jacobian.transpose(1, 0, 2)
    pins = pinched_map.reshape(1, -1)
    elements = solution.shape[2]
    traces = shape_of(FIELDS, NODES, elements)
    sends = (faces, faces, shape_of(FIELDS, 16, EX // 2 * CELLS), faces)
    swap = [(0, 1), (1, 0)]
    same_chip = [(i, i ^ 1) for i in range(ranks)]
    next_chip = [(a + 1, b + 1) for a, b in same_chip if max(a, b) + 1 < ranks]

    span_scratch = pltpu.VMEM((FIELDS, 16, CELLS), f32)
    plane, core, chip, pitch, span = pl.pallas_call(
        functools.partial(
            prepare_kernel, normalizer=float((plane_rows / (eddies * ranks * foot)) ** 0.5)
        ),
        out_shape=(shape_of(FIELDS, 16, CELLS, dtype=f32),) + sends,
        in_specs=[pl.BlockSpec(memory_space=pltpu.HBM)] * 4,
        out_specs=(VMEM,) * 5,
        scratch_shapes=[
            pltpu.VMEM((foot, eddies), jnp.int32),
            pltpu.VMEM((1, eddies), jnp.int32),
            pltpu.VMEM((foot, eddies), f32),
            pltpu.VMEM(solution.shape, bf16),
            span_scratch,
            pltpu.SemaphoreType.DMA((4,)),
        ],
        compiler_params=pltpu.CompilerParams(vmem_limit_bytes=60 * 2**20),
        cost_estimate=cost(5),
        name="prepare",
    )(mode_rows[0, 0].T, mode_seeds.reshape(1, eddies), mode_shape[0, 0].T, solution)
    plane = gather_sum(plane, (2, 6, 4), [8 * z + c for z in range(8) for c in range(2)])
    near = lax.ppermute(pitch, "pitch", swap)
    plane, chip, core, span = lax.optimization_barrier((plane, chip, core, span))
    plane = gather_sum(plane, (1, 8, 9), [0, 16, 32, 48])
    from_chip = lax.ppermute(chip, "rans", next_chip)
    core, span, near = lax.optimization_barrier((core, span, near))
    far = lax.ppermute(span, "span", swap)
    from_core = lax.ppermute(core, "rans", same_chip)
    plane, near, far, from_core = lax.optimization_barrier((plane, near, far, from_core))
    plane = gather_sum(plane, (16, 48, 32), [0])

    phase_one, trace_one, core, chip, pitch, span = pl.pallas_call(
        phase_one_kernel,
        out_shape=(traces, traces) + sends,
        in_specs=[VMEM] * 6 + [SMEM] + [VMEM] * 4,
        out_specs=(VMEM,) * 6,
        scratch_shapes=[
            pltpu.VMEM((2, FIELDS, MIXED, PAIR), bf16),
            pltpu.VMEM((2, FIELDS, NODES, PAIR), bf16),
            pltpu.VMEM((NODES, MIXED), bf16),
            span_scratch,
        ],
        compiler_params=PARAMS,
        cost_estimate=cost(6),
        name="phase_one",
    )(
        solution, from_core, from_chip, near, far, pins, jacobian, volume_ops, lift_matrix, wall_matrix,
        filter_matrix,
    )
    from_core = lax.ppermute(core, "rans", same_chip)
    from_chip = lax.ppermute(chip, "rans", next_chip)
    plane, from_core = lax.optimization_barrier((plane, from_core))

    mean = mean_inflow.reshape(FIELDS, 16, CELLS)
    amplitude = eddy_amplitude.reshape(FIELDS, 16, CELLS)
    layer = front(FIELDS, NODES, CELLS)
    face = front(FIELDS, 16, CELLS)
    phase_one, trace_one, pitch, span = pl.pallas_call(
        inflow_kernel,
        grid=(1,),
        out_shape=(traces, traces, sends[2], sends[3]),
        in_specs=[layer, layer, face, face, front(FIELDS, NODES, PAIR)]
        + [face] * 5
        + [
            front(1, CELLS), SMEM, front(3, NODES, NODES), front(NODES, 96), front(NODES, NODES),
            front(NODES, NODES),
        ],
        out_specs=(layer, layer, face, face),
        scratch_shapes=[
            pltpu.VMEM((FIELDS, MIXED, CELLS), bf16),
            pltpu.VMEM((FIELDS, NODES, CELLS), bf16),
            pltpu.VMEM((NODES, MIXED), bf16),
        ],
        input_output_aliases={0: 0, 1: 1, 2: 2, 3: 3},
        compiler_params=PARAMS,
        cost_estimate=cost(0.1),
        name="inflow_layer",
    )(
        phase_one, trace_one, pitch, span, solution, mean, amplitude, plane, near, far,
        pins, jacobian, volume_ops, lift_matrix, wall_matrix, filter_matrix,
    )
    near = lax.ppermute(pitch, "pitch", swap)
    far = lax.ppermute(span, "span", swap)
    part = pl.pallas_call(
        inner_two_kernel,
        out_shape=shape_of(FIELDS, NODES, elements, dtype=f32),
        in_specs=[VMEM, SMEM, VMEM],
        out_specs=VMEM,
        scratch_shapes=[
            pltpu.VMEM((2, FIELDS, INNER, PAIR), bf16), pltpu.VMEM((NODES, INNER), bf16)
        ],
        compiler_params=PARAMS,
        cost_estimate=cost(0.1),
        name="inner_two",
    )(phase_one, jacobian, volume_ops)
    return pl.pallas_call(
        outer_two_kernel,
        out_shape=traces,
        in_specs=[VMEM] * 12 + [SMEM] + [VMEM] * 3,
        out_specs=VMEM,
        scratch_shapes=[
            pltpu.VMEM((2, FIELDS, MIXED - INNER, PAIR), bf16),
            pltpu.VMEM((NODES, MIXED - INNER), bf16),
        ],
        compiler_params=PARAMS,
        cost_estimate=cost(4),
        name="outer_two",
    )(
        phase_one, trace_one, solution, part, mean, amplitude, plane, from_core, from_chip, near, far,
        pins, jacobian, lift_matrix, wall_matrix, filter_matrix,
    )


def solution(mesh):
    spread = P(None, None, ("rans", "pitch", "span"))
    in_specs = (
        spread,
        P(),
        P(),
        P(),
        P(),
        P(),
        P(("rans", "pitch", "span")),
        P("pitch", "span", "rans", None),
        P("pitch", "span", "rans"),
        P("pitch", "span", "rans", None),
        P("pitch", "span", None, None),
        P("pitch", "span", None, None),
    )
    return jax.shard_map(body, mesh=mesh, in_specs=in_specs, out_specs=spread, check_vma=False)
```

```python
import functools

import jax
import jax.numpy as jnp
from jax import lax
from jax.experimental import pallas as pl
from jax.experimental.pallas import tpu as pltpu
from jax.sharding import PartitionSpec as P

FIELDS = 5
NODES = 64
EX = 12
CELLS = 128
SPAN_CELLS = 32
PAIR = 2 * CELLS
MIXED = 352
INNER = 192
TIME_STEP = 0.4
f32 = jnp.float32
bf16 = jnp.bfloat16


def trace_selector():
    row = lax.broadcasted_iota(jnp.int32, (64, 64), 0)
    node = lax.broadcasted_iota(jnp.int32, (64, 64), 1)
    face, first, second = row >> 4, (row >> 2) & 3, row & 3
    on_pitch = second + jnp.where(face == 1, 12, 0)
    on_span = 4 * second + jnp.where(face == 3, 3, 0)
    source = 16 * first + jnp.where(face < 2, on_pitch, on_span)
    return jnp.where(node == source, 1.0, 0.0).astype(bf16)


def dot(a, b):
    return jnp.dot(a, b, preferred_element_type=f32)


def lanes():
    return lax.broadcasted_iota(jnp.int32, (16, CELLS), 1)


def sum_eddies(rows_ref, seeds_ref, shape_ref, plane_ref, normalizer):
    seeds = seeds_ref[...]
    signs = [(2 * ((seeds >> f) & 1) - 1).astype(f32) for f in range(FIELDS)]
    signs = [jnp.broadcast_to(s, (32, s.shape[1])).astype(bf16) for s in signs]
    eddies = rows_ref.shape[1]
    high_row = lax.broadcasted_iota(jnp.int32, (16, eddies), 0)
    low_row = lax.broadcasted_iota(jnp.int32, (CELLS, eddies), 0)

    def chunk(i, total):
        start = pl.multiple_of(i * 8, 8)
        rows = rows_ref[pl.ds(start, 8), :]
        shapes = shape_ref[pl.ds(start, 8), :]
        for q in range(8):
            row, shape = rows[q : q + 1], shapes[q : q + 1]
            placed = jnp.where((row >> 7) == high_row, shape, 0.0)
            coarse = placed.astype(bf16)
            fine = (placed - coarse.astype(f32)).astype(bf16)
            both = jnp.concatenate([coarse, fine], axis=0)
            signed = jnp.concatenate([both * s for s in signs], axis=0)
            hot = jnp.where((row & 127) == low_row, 1.0, 0.0).astype(bf16)
            total = total + lax.dot_general(
                signed, hot, (((1,), (1,)), ((), ())), preferred_element_type=f32
            )
        return total

    total = lax.fori_loop(0, rows_ref.shape[0] // 8, chunk, jnp.zeros((160, CELLS), f32))
    for f in range(FIELDS):
        plane_ref[f] = (total[32 * f : 32 * f + 16] + total[32 * f + 16 : 32 * f + 32]) * normalizer


def pack_pitch(traces, lane):
    (low0, high0), (low1, high1) = traces
    return jnp.where(
        lane < 32,
        low0,
        jnp.where(
            lane < 64,
            pltpu.roll(low1, 32, 1),
            jnp.where(lane < 96, pltpu.roll(high0, 96, 1), high1),
        ),
    )


def pack_span(held, low, high, layer, first_span, lane):
    edge = jnp.where(first_span, high, low)
    shift = lax.rem(layer + jnp.where(first_span, 97, 0), 128)
    return jnp.where((lane & 31) == layer, pltpu.roll(edge, shift, 1), held)


def pack_field(f, trace, pair, first_span, lane, pitch_ref, span_held):
    halves = [trace[:, :CELLS], trace[:, CELLS:]]
    packed = pack_pitch([(h[0:16], h[16:32]) for h in halves], lane)
    pitch_ref[f, :, pair * CELLS : (pair + 1) * CELLS] = packed.astype(bf16)
    held = span_held[f]
    for h in range(2):
        held = pack_span(held, halves[h][32:48], halves[h][48:64], 2 * pair + h, first_span, lane)
    span_held[f] = held


def is_even():
    return (lax.axis_index("rans") & 1) == 0


def store_stream(up, down, near_chip_ref, far_chip_ref):
    even = is_even()
    near_chip_ref[...] = jnp.where(even, up, down)
    far_chip_ref[...] = jnp.where(even, down, up)


def from_below(near_chip_ref, far_chip_ref):
    even = is_even()
    return lambda f: jnp.where(even, far_chip_ref[f].astype(f32), near_chip_ref[f].astype(f32))


def from_above(near_chip_ref, far_chip_ref):
    even = is_even()
    return lambda f: jnp.where(even, near_chip_ref[f].astype(f32), far_chip_ref[f].astype(f32))


def prepare_kernel(
    rows_hbm, seeds_hbm, shape_hbm, v_hbm, plane_ref, core_ref, chip_ref, pitch_ref,
    span_ref, rows_ref, seeds_ref, shape_ref, v_ref, span_held, sems, *, normalizer,
):
    copies = [
        pltpu.make_async_copy(source, target, sems.at[i])
        for i, (source, target) in enumerate([
            (rows_hbm, rows_ref), (seeds_hbm, seeds_ref), (shape_hbm, shape_ref), (v_hbm, v_ref),
        ])
    ]
    for copy in copies:
        copy.start()
    first_span = lax.axis_index("span") == 0
    lane = lanes()
    pick = trace_selector()
    span_held[...] = jnp.zeros_like(span_held)
    for copy in copies[:3]:
        copy.wait()
    sum_eddies(rows_ref, seeds_ref, shape_ref, plane_ref, normalizer)
    copies[3].wait()
    for pair in range(EX // 2):
        at = slice(pair * PAIR, (pair + 1) * PAIR)
        for f in range(FIELDS):
            pack_field(
                f, dot(pick, v_ref[f, :, at]), pair, first_span, lane, pitch_ref, span_held
            )
    span_ref[...] = span_held[...].astype(bf16)
    store_stream(
        v_ref[:, 48:64, (EX - 1) * CELLS :], v_ref[:, 0:16, 0:CELLS], core_ref, chip_ref
    )


def mix(row, arrays):
    total = row[0] * arrays[0]
    for g in range(1, FIELDS):
        total = total + row[g] * arrays[g]
    return total


def flux_row(jacobian, d, f):
    return [jacobian[f, d, g] for g in range(FIELDS)]


def face_row(jacobian, t, f):
    half = 0.5 * (1.0 if t % 2 else -1.0)
    row = [half * jacobian[f, t // 2, g] for g in range(FIELDS)]
    row[f] = row[f] - 0.5
    return row


def fill(weights, parts):
    column = 0
    for part in parts:
        weights[:, column : column + part.shape[1]] = part
        column += part.shape[1]
    return weights[...]


def mix_fluxes(read, coefs, mixed):
    def rows_step(r):
        def run():
            rows = [read(f, r, r + 16).astype(f32) for f in range(FIELDS)]
            for d in range(3):
                for f in range(FIELDS):
                    mixed[f, 64 * d + r : 64 * d + r + 16, :] = mix(
                        flux_row(coefs, d, f), rows
                    ).astype(bf16)

        return run

    return [rows_step(r) for r in range(0, NODES, 16)]


def write_jumps(t, jumps, coefs, mixed, first_row):
    for f in range(FIELDS):
        mixed[f, first_row : first_row + 16, :] = mix(face_row(coefs, t, f), jumps).astype(bf16)


def mix_stream(read, lower, upper, coefs, mixed, row):
    def low():
        jumps = [lower(f) - read(f, 0, 16).astype(f32) for f in range(FIELDS)]
        write_jumps(0, jumps, coefs, mixed, row)

    def high():
        jumps = [upper(f) - read(f, 48, 64).astype(f32) for f in range(FIELDS)]
        write_jumps(1, jumps, coefs, mixed, row + 16)

    return [low, high]


def mix_sides(trace, pitch, span, layers, coefs, mixed, row, first_span, lane):
    def halves(f, r):
        own = trace(f, r, r + 16)
        return [own[:, h * CELLS : (h + 1) * CELLS] for h in range(len(layers))]

    def join(parts):
        return parts[0] if len(parts) == 1 else jnp.concatenate(parts, axis=1)

    def pitch_low():
        jumps = []
        for f in range(FIELDS):
            near, low, high = pitch(f), halves(f, 0), halves(f, 16)
            jumps.append(join([
                jnp.where(
                    lane < 32, pltpu.roll(near, 64 if h == 0 else 32, 1), pltpu.roll(high[h], 32, 1)
                ) - low[h]
                for h in range(len(layers))
            ]))
        write_jumps(2, jumps, coefs, mixed, row)

    def pitch_high():
        jumps = []
        for f in range(FIELDS):
            near, low, high = pitch(f), halves(f, 0), halves(f, 16)
            jumps.append(join([
                jnp.where(
                    lane >= 96, pltpu.roll(near, 96 if h == 0 else 64, 1), pltpu.roll(low[h], 96, 1)
                ) - high[h]
                for h in range(len(layers))
            ]))
        write_jumps(3, jumps, coefs, mixed, row + 16)

    def arrived(f, layer):
        return pltpu.roll(span(f), lax.rem(jnp.where(first_span, 31, 128) - layer, 128), 1)

    def span_low():
        jumps = []
        for f in range(FIELDS):
            low, high = halves(f, 32), halves(f, 48)
            jumps.append(join([
                jnp.where(
                    (lane & 31) == 0,
                    jnp.where(first_span, low[h], arrived(f, layer)),
                    pltpu.roll(high[h], 1, 1),
                ) - low[h]
                for h, layer in enumerate(layers)
            ]))
        write_jumps(4, jumps, coefs, mixed, row + 32)

    def span_high():
        jumps = []
        for f in range(FIELDS):
            low, high = halves(f, 32), halves(f, 48)
            jumps.append(join([
                jnp.where(
                    (lane & 31) == 31,
                    jnp.where(first_span, arrived(f, layer), high[h]),
                    pltpu.roll(low[h], 127, 1),
                ) - high[h]
                for h, layer in enumerate(layers)
            ]))
        write_jumps(5, jumps, coefs, mixed, row + 48)

    return [pitch_low, pitch_high, span_low, span_high]


def mix_wall(read, pinned, mixed, row):
    def run():
        for f in range(FIELDS):
            mixed[f, row : row + 64, :] = (read(f, 0, 64).astype(f32) * pinned()).astype(bf16)

    return [run]


def staggered(stages):
    held = [None] * FIELDS
    steps = []

    def step(stage, f):
        def run():
            held[f] = stage(f, held[f])

        return run

    for turn in range(FIELDS + len(stages) - 1):
        for k, stage in enumerate(stages):
            if 0 <= turn - k < FIELDS:
                steps.append(step(stage, turn - k))
    return steps


def interleave(first, second):
    count = max(len(first), len(second))
    for i in range(count):
        for steps in (first, second):
            for step in steps[i * len(steps) // count : (i + 1) * len(steps) // count]:
                step()


def pipeline(vector, matrix):
    for step in vector[0]:
        step()
    for p in range(len(matrix)):
        interleave(matrix[p], vector[p + 1] if p + 1 < len(vector) else [])


def finish(read, base, smooth):
    def trial(f, rate):
        v = read(f, 0, 64).astype(f32)
        if base is None:
            now = v - TIME_STEP * rate
        else:
            now = 0.5 * (base(f).astype(f32) + v - TIME_STEP * rate)
        return dot(smooth, now.astype(bf16))

    return trial


def with_traces(filter_matrix, pick):
    return jnp.concatenate([filter_matrix, dot(pick, filter_matrix).astype(bf16)], axis=0)


def mix_traces(read, pick, own):
    def run():
        for f in range(FIELDS):
            own[f] = dot(pick, read(f, 0, 64)).astype(bf16)

    return [run]


def place(pair):
    return slice(pair * PAIR, (pair + 1) * PAIR)


def lower_pair(v_ref, edge, pair):
    def lower(f):
        if pair:
            return v_ref[f, 48:64, pair * PAIR - CELLS : (pair + 1) * PAIR - CELLS].astype(f32)
        return jnp.concatenate([edge(f), v_ref[f, 48:64, 0:CELLS].astype(f32)], axis=1)

    return lower


def upper_pair(v_ref, above, pair):
    first = pair * PAIR + CELLS
    last_rans = lax.axis_index("rans") == lax.axis_size("rans") - 1

    def upper(f):
        if pair < EX // 2 - 1:
            return v_ref[f, 0:16, first : first + PAIR].astype(f32)
        edge = jnp.where(
            last_rans, v_ref[f, 48:64, first : first + CELLS].astype(f32), above(f)
        )
        return jnp.concatenate([v_ref[f, 0:16, first : first + CELLS].astype(f32), edge], axis=1)

    return upper


def phase_one_kernel(
    v_ref, from_core_ref, from_chip_ref, near_ref, far_ref, pin_ref, coefs, volume_ref, lift_ref,
    wall_ref, filter_ref,
    out_ref, out_trace_ref, core_ref, chip_ref, pitch_ref, span_ref, mixed, own, weights_held,
    span_held,
):
    first_span = lax.axis_index("span") == 0
    lane = lanes()
    pick = trace_selector()
    smooth = with_traces(filter_ref[...], pick)
    weights = fill(
        weights_held, [volume_ref[0], volume_ref[1], volume_ref[2], lift_ref[...], wall_ref[...]]
    )
    span_held[...] = jnp.zeros_like(span_held)
    below, above = from_below(from_core_ref, from_chip_ref), from_above(from_core_ref, from_chip_ref)
    vector, matrix = [], []

    def add(pair):
        at = place(pair)
        rows, held = mixed.at[pair % 2], own.at[pair % 2]

        def read(f, r0, r1):
            return v_ref[f, r0:r1, at]

        def store(f, value):
            out_ref[f, :, at] = value[0:64].astype(bf16)
            trace = value[64:128]
            out_trace_ref[f, :, at] = trace.astype(bf16)
            pack_field(f, trace, pair, first_span, lane, pitch_ref, span_held)

        vector.append(
            mix_traces(read, pick, held)
            + mix_fluxes(read, coefs, rows)
            + mix_stream(
                read,
                lower_pair(v_ref, below, pair),
                upper_pair(v_ref, above, pair),
                coefs, rows, 192,
            )
            + mix_sides(
                lambda f, r0, r1: held[f, r0:r1].astype(f32),
                lambda f: near_ref[f, :, pair * CELLS : (pair + 1) * CELLS].astype(f32),
                lambda f: far_ref[f].astype(f32),
                [2 * pair, 2 * pair + 1], coefs, rows, 224, first_span, lane,
            )
            + mix_wall(read, lambda: pin_ref[:, at].astype(f32), rows, 288)
        )
        matrix.append(
            staggered([lambda f, _: dot(weights, rows[f]), finish(read, None, smooth), store])
        )

    for pair in range(EX // 2):
        add(pair)
    pipeline(vector, matrix)
    span_ref[...] = span_held[...].astype(bf16)
    store_stream(
        out_ref[:, 48:64, (EX - 1) * CELLS :], out_ref[:, 0:16, 0:CELLS], core_ref, chip_ref
    )


def inner_two_kernel(v_ref, coefs, volume_ref, part_ref, mixed, weights_held):
    weights = fill(weights_held, [volume_ref[d] for d in range(3)])
    vector, matrix = [], []

    def add(pair):
        at = place(pair)
        rows = mixed.at[pair % 2]

        def store(f, value):
            part_ref[f, :, at] = value

        vector.append(mix_fluxes(lambda f, r0, r1: v_ref[f, r0:r1, at], coefs, rows))
        matrix.append(staggered([lambda f, _: dot(weights, rows[f]), store]))

    for pair in range(EX // 2):
        add(pair)
    pipeline(vector, matrix)


def outer_two_kernel(
    v_ref, trace_ref, base_ref, part_ref, mean_ref, amp_ref, plane_ref, from_core_ref, from_chip_ref,
    near_ref, far_ref, pin_ref, coefs, lift_ref, wall_ref, smooth_ref, out_ref, mixed, weights_held,
):
    first_span = lax.axis_index("span") == 0
    first_rans = lax.axis_index("rans") == 0
    lane = lanes()
    weights, smooth = fill(weights_held, [lift_ref[...], wall_ref[...]]), smooth_ref[...]
    below, above = from_below(from_core_ref, from_chip_ref), from_above(from_core_ref, from_chip_ref)
    vector, matrix = [], []

    def edge(f):
        return jnp.where(first_rans, inflow_of(mean_ref, amp_ref, plane_ref)(f), below(f))

    def add(pair):
        at = place(pair)
        rows = mixed.at[pair % 2]

        def read(f, r0, r1):
            return v_ref[f, r0:r1, at]

        def store(f, value):
            out_ref[f, :, at] = value.astype(bf16)

        vector.append(
            mix_stream(
                read, lower_pair(v_ref, edge, pair), upper_pair(v_ref, above, pair), coefs, rows, 0
            )
            + mix_sides(
                lambda f, r0, r1: trace_ref[f, r0:r1, at].astype(f32),
                lambda f: near_ref[f, :, pair * CELLS : (pair + 1) * CELLS].astype(f32),
                lambda f: far_ref[f].astype(f32),
                [2 * pair, 2 * pair + 1], coefs, rows, 32, first_span, lane,
            )
            + mix_wall(read, lambda: pin_ref[:, at].astype(f32), rows, 96)
        )
        matrix.append(
            staggered([
                lambda f, _: dot(weights, rows[f]) + part_ref[f, :, at],
                finish(read, lambda f: base_ref[f, :, at], smooth),
                store,
            ])
        )

    for pair in range(EX // 2):
        add(pair)
    pipeline(vector, matrix)


def inflow_of(mean_ref, amp_ref, plane_ref):
    return lambda f: mean_ref[f] + amp_ref[f] * plane_ref[f]


def inflow_kernel(
    held_ref, held_trace_ref, held_pitch_ref, held_span_ref, v_ref, mean_ref, amp_ref,
    plane_ref, near_ref, far_ref, pin_ref, coefs, volume_ref, lift_ref, wall_ref, filter_ref, out_ref,
    out_trace_ref,
    pitch_ref, span_ref, mixed, own, weights_held,
):
    first_span = lax.axis_index("span") == 0
    first_rans = lax.axis_index("rans") == 0
    lane = lanes()

    @pl.when(first_rans)
    def _():
        pick = trace_selector()
        smooth = with_traces(filter_ref[...], pick)
        weights = fill(
            weights_held, [volume_ref[0], volume_ref[1], volume_ref[2], lift_ref[...], wall_ref[...]]
        )

        def read(f, r0, r1):
            return v_ref[f, r0:r1, 0:CELLS]

        def store(f, value):
            out_ref[f] = value[0:64].astype(bf16)
            t = value[64:128]
            out_trace_ref[f] = t.astype(bf16)
            pitch = jnp.where(lane < 32, t[0:16], pltpu.roll(t[16:32], 96, 1))
            pitch_ref[f] = jnp.where(
                (lane & 63) < 32, pitch, held_pitch_ref[f].astype(f32)
            ).astype(bf16)
            span_ref[f] = pack_span(
                held_span_ref[f].astype(f32), t[32:48], t[48:64], 0, first_span, lane
            ).astype(bf16)

        vector = (
            mix_traces(read, pick, own)
            + mix_stream(
                read,
                inflow_of(mean_ref, amp_ref, plane_ref),
                lambda f: v_ref[f, 0:16, CELLS:PAIR].astype(f32),
                coefs, mixed, 192,
            )
            + mix_sides(
                lambda f, r0, r1: own[f, r0:r1].astype(f32),
                lambda f: near_ref[f].astype(f32),
                lambda f: far_ref[f].astype(f32),
                [0], coefs, mixed, 224, first_span, lane,
            )
            + mix_fluxes(read, coefs, mixed)
            + mix_wall(read, lambda: pin_ref[...].astype(f32), mixed, 288)
        )
        matrix = staggered(
            [lambda f, _: dot(weights, mixed[f]), finish(read, None, smooth), store]
        )
        pipeline([vector], [matrix])

    @pl.when(jnp.logical_not(first_rans))
    def _():
        out_ref[...] = held_ref[...]
        out_trace_ref[...] = held_trace_ref[...]
        pitch_ref[...] = held_pitch_ref[...]
        span_ref[...] = held_span_ref[...]


VMEM = pl.BlockSpec(memory_space=pltpu.VMEM)
SMEM = pl.BlockSpec(memory_space=pltpu.SMEM)
PARAMS = pltpu.CompilerParams(vmem_limit_bytes=40 * 2**20)


def shape_of(*dims, dtype=bf16):
    return jax.ShapeDtypeStruct(dims, dtype)


def front(*dims):
    return pl.BlockSpec(dims, lambda i: (0,) * len(dims))


def cost(us):
    return pl.CostEstimate(flops=int(us * 1e8), bytes_accessed=int(us * 3e6), transcendentals=0)


def body(
    solution, volume_ops, flux_jacobian, lift_matrix, filter_matrix, wall_matrix, pinched_map,
    mode_rows, mode_seeds, mode_shape, mean_inflow, eddy_amplitude,
):
    ranks = lax.axis_size("rans")
    eddies, foot = mode_shape.shape[2:]
    plane_rows = mean_inflow.shape[3]
    faces = shape_of(FIELDS, 16, CELLS)
    def slab(z, y, core):
        return 8 * z + 2 * y + core

    columns = ranks // 8
    root_y = [0] + [1] * (columns - 1)
    first_level = [
        [
            (slab(z, [y for y in range(4) if y != root_y[z]][turn], core), slab(z, root_y[z], core))
            for z in range(columns)
            for core in range(2)
        ]
        for turn in range(3)
    ]
    second_level = [
        [
            (slab(z + up, root_y[z + up], core), slab(z, root_y[z], 0))
            for z in range(0, columns, 2)
        ]
        for up, core in ((0, 1), (1, 0), (1, 1))
    ]
    third_level = [[(slab(z, root_y[z], 0), 0)] for z in (2, 6, 4)]

    def gather_sum(value, level):
        parts = [lax.ppermute(value, "rans", pairs) for pairs in level]
        for part in parts:
            value = value + part
        return value

    jacobian = flux_jacobian.transpose(1, 0, 2)
    pins = pinched_map.reshape(1, -1)
    elements = solution.shape[2]
    traces = shape_of(FIELDS, NODES, elements)
    sends = (faces, faces, shape_of(FIELDS, 16, EX // 2 * CELLS), faces)
    swap = [(0, 1), (1, 0)]
    same_chip = [(i, i ^ 1) for i in range(ranks)]
    next_chip = [(a + 1, b + 1) for a, b in same_chip if max(a, b) + 1 < ranks]

    span_scratch = pltpu.VMEM((FIELDS, 16, CELLS), f32)
    plane, core, chip, pitch, span = pl.pallas_call(
        functools.partial(
            prepare_kernel, normalizer=float((plane_rows / (eddies * ranks * foot)) ** 0.5)
        ),
        out_shape=(shape_of(FIELDS, 16, CELLS, dtype=f32),) + sends,
        in_specs=[pl.BlockSpec(memory_space=pltpu.HBM)] * 4,
        out_specs=(VMEM,) * 5,
        scratch_shapes=[
            pltpu.VMEM((foot, eddies), jnp.int32),
            pltpu.VMEM((1, eddies), jnp.int32),
            pltpu.VMEM((foot, eddies), f32),
            pltpu.VMEM(solution.shape, bf16),
            span_scratch,
            pltpu.SemaphoreType.DMA((4,)),
        ],
        compiler_params=pltpu.CompilerParams(vmem_limit_bytes=60 * 2**20),
        cost_estimate=cost(5),
        name="prepare",
    )(mode_rows[0, 0].T, mode_seeds.reshape(1, eddies), mode_shape[0, 0].T, solution)
    plane = gather_sum(plane, first_level)
    near = lax.ppermute(pitch, "pitch", swap)
    plane, chip, core, span = lax.optimization_barrier((plane, chip, core, span))
    plane = gather_sum(plane, second_level)
    from_chip = lax.ppermute(chip, "rans", next_chip)
    core, span, near = lax.optimization_barrier((core, span, near))
    far = lax.ppermute(span, "span", swap)
    from_core = lax.ppermute(core, "rans", same_chip)
    plane, near, far, from_core = lax.optimization_barrier((plane, near, far, from_core))
    plane = gather_sum(plane, third_level)

    phase_one, trace_one, core, chip, pitch, span = pl.pallas_call(
        phase_one_kernel,
        out_shape=(traces, traces) + sends,
        in_specs=[VMEM] * 6 + [SMEM] + [VMEM] * 4,
        out_specs=(VMEM,) * 6,
        scratch_shapes=[
            pltpu.VMEM((2, FIELDS, MIXED, PAIR), bf16),
            pltpu.VMEM((2, FIELDS, NODES, PAIR), bf16),
            pltpu.VMEM((NODES, MIXED), bf16),
            span_scratch,
        ],
        compiler_params=PARAMS,
        cost_estimate=cost(6),
        name="phase_one",
    )(
        solution, from_core, from_chip, near, far, pins, jacobian, volume_ops, lift_matrix, wall_matrix,
        filter_matrix,
    )
    from_core = lax.ppermute(core, "rans", same_chip)
    from_chip = lax.ppermute(chip, "rans", next_chip)
    plane, from_core = lax.optimization_barrier((plane, from_core))

    mean = mean_inflow.reshape(FIELDS, 16, CELLS)
    amplitude = eddy_amplitude.reshape(FIELDS, 16, CELLS)
    layer = front(FIELDS, NODES, CELLS)
    face = front(FIELDS, 16, CELLS)
    phase_one, trace_one, pitch, span = pl.pallas_call(
        inflow_kernel,
        grid=(1,),
        out_shape=(traces, traces, sends[2], sends[3]),
        in_specs=[layer, layer, face, face, front(FIELDS, NODES, PAIR)]
        + [face] * 5
        + [
            front(1, CELLS), SMEM, front(3, NODES, NODES), front(NODES, 96), front(NODES, NODES),
            front(NODES, NODES),
        ],
        out_specs=(layer, layer, face, face),
        scratch_shapes=[
            pltpu.VMEM((FIELDS, MIXED, CELLS), bf16),
            pltpu.VMEM((FIELDS, NODES, CELLS), bf16),
            pltpu.VMEM((NODES, MIXED), bf16),
        ],
        input_output_aliases={0: 0, 1: 1, 2: 2, 3: 3},
        compiler_params=PARAMS,
        cost_estimate=cost(0.1),
        name="inflow_layer",
    )(
        phase_one, trace_one, pitch, span, solution, mean, amplitude, plane, near, far,
        pins, jacobian, volume_ops, lift_matrix, wall_matrix, filter_matrix,
    )
    near = lax.ppermute(pitch, "pitch", swap)
    far = lax.ppermute(span, "span", swap)
    part = pl.pallas_call(
        inner_two_kernel,
        out_shape=shape_of(FIELDS, NODES, elements, dtype=f32),
        in_specs=[VMEM, SMEM, VMEM],
        out_specs=VMEM,
        scratch_shapes=[
            pltpu.VMEM((2, FIELDS, INNER, PAIR), bf16), pltpu.VMEM((NODES, INNER), bf16)
        ],
        compiler_params=PARAMS,
        cost_estimate=cost(0.1),
        name="inner_two",
    )(phase_one, jacobian, volume_ops)
    return pl.pallas_call(
        outer_two_kernel,
        out_shape=traces,
        in_specs=[VMEM] * 12 + [SMEM] + [VMEM] * 3,
        out_specs=VMEM,
        scratch_shapes=[
            pltpu.VMEM((2, FIELDS, MIXED - INNER, PAIR), bf16),
            pltpu.VMEM((NODES, MIXED - INNER), bf16),
        ],
        compiler_params=PARAMS,
        cost_estimate=cost(4),
        name="outer_two",
    )(
        phase_one, trace_one, solution, part, mean, amplitude, plane, from_core, from_chip, near, far,
        pins, jacobian, lift_matrix, wall_matrix, filter_matrix,
    )


def solution(mesh):
    spread = P(None, None, ("rans", "pitch", "span"))
    in_specs = (
        spread,
        P(),
        P(),
        P(),
        P(),
        P(),
        P(("rans", "pitch", "span")),
        P("pitch", "span", "rans", None),
        P("pitch", "span", "rans"),
        P("pitch", "span", "rans", None),
        P("pitch", "span", None, None),
        P("pitch", "span", None, None),
    )
    return jax.shard_map(body, mesh=mesh, in_specs=in_specs, out_specs=spread, check_vma=False)
```

```python
import functools

import jax
import jax.numpy as jnp
from jax import lax
from jax.experimental import pallas as pl
from jax.experimental.pallas import tpu as pltpu
from jax.sharding import PartitionSpec as P

FIELDS = 5
NODES = 64
EX = 12
CELLS = 128
SPAN_CELLS = 32
PAIR = 2 * CELLS
MIXED = 352
INNER = 192
TIME_STEP = 0.4
f32 = jnp.float32
bf16 = jnp.bfloat16


def trace_selector():
    row = lax.broadcasted_iota(jnp.int32, (64, 64), 0)
    node = lax.broadcasted_iota(jnp.int32, (64, 64), 1)
    face, first, second = row >> 4, (row >> 2) & 3, row & 3
    on_pitch = second + jnp.where(face == 1, 12, 0)
    on_span = 4 * second + jnp.where(face == 3, 3, 0)
    source = 16 * first + jnp.where(face < 2, on_pitch, on_span)
    return jnp.where(node == source, 1.0, 0.0).astype(bf16)


def dot(a, b):
    return jnp.dot(a, b, preferred_element_type=f32)


def lanes():
    return lax.broadcasted_iota(jnp.int32, (16, CELLS), 1)


def sum_eddies(rows_ref, seeds_ref, shape_ref, plane_ref, normalizer):
    seeds = seeds_ref[...]
    signs = [(2 * ((seeds >> f) & 1) - 1).astype(f32) for f in range(FIELDS)]
    signs = [jnp.broadcast_to(s, (32, s.shape[1])).astype(bf16) for s in signs]
    eddies = rows_ref.shape[1]
    high_row = lax.broadcasted_iota(jnp.int32, (16, eddies), 0)
    low_row = lax.broadcasted_iota(jnp.int32, (CELLS, eddies), 0)

    def chunk(i, total):
        start = pl.multiple_of(i * 8, 8)
        rows = rows_ref[pl.ds(start, 8), :]
        shapes = shape_ref[pl.ds(start, 8), :]
        for q in range(8):
            row, shape = rows[q : q + 1], shapes[q : q + 1]
            placed = jnp.where((row >> 7) == high_row, shape, 0.0)
            coarse = placed.astype(bf16)
            fine = (placed - coarse.astype(f32)).astype(bf16)
            both = jnp.concatenate([coarse, fine], axis=0)
            signed = jnp.concatenate([both * s for s in signs], axis=0)
            hot = jnp.where((row & 127) == low_row, 1.0, 0.0).astype(bf16)
            total = total + lax.dot_general(
                signed, hot, (((1,), (1,)), ((), ())), preferred_element_type=f32
            )
        return total

    total = lax.fori_loop(0, rows_ref.shape[0] // 8, chunk, jnp.zeros((160, CELLS), f32))
    for f in range(FIELDS):
        plane_ref[f] = (total[32 * f : 32 * f + 16] + total[32 * f + 16 : 32 * f + 32]) * normalizer


def pack_pitch(traces, lane):
    (low0, high0), (low1, high1) = traces
    return jnp.where(
        lane < 32,
        low0,
        jnp.where(
            lane < 64,
            pltpu.roll(low1, 32, 1),
            jnp.where(lane < 96, pltpu.roll(high0, 96, 1), high1),
        ),
    )


def pack_span(held, low, high, layer, first_span, lane):
    edge = jnp.where(first_span, high, low)
    shift = lax.rem(layer + jnp.where(first_span, 97, 0), 128)
    return jnp.where((lane & 31) == layer, pltpu.roll(edge, shift, 1), held)


def pack_field(f, trace, pair, first_span, lane, pitch_ref, span_held):
    halves = [trace[:, :CELLS], trace[:, CELLS:]]
    packed = pack_pitch([(h[0:16], h[16:32]) for h in halves], lane)
    pitch_ref[f, :, pair * CELLS : (pair + 1) * CELLS] = packed.astype(bf16)
    held = span_held[f]
    for h in range(2):
        held = pack_span(held, halves[h][32:48], halves[h][48:64], 2 * pair + h, first_span, lane)
    span_held[f] = held


def is_even():
    return (lax.axis_index("rans") & 1) == 0


def store_stream(up, down, near_chip_ref, far_chip_ref):
    even = is_even()
    near_chip_ref[...] = jnp.where(even, up, down)
    far_chip_ref[...] = jnp.where(even, down, up)


def from_below(near_chip_ref, far_chip_ref):
    even = is_even()
    return lambda f: jnp.where(even, far_chip_ref[f].astype(f32), near_chip_ref[f].astype(f32))


def from_above(near_chip_ref, far_chip_ref):
    even = is_even()
    return lambda f: jnp.where(even, near_chip_ref[f].astype(f32), far_chip_ref[f].astype(f32))


def plane_kernel(
    rows_hbm, seeds_hbm, shape_hbm, plane_ref, rows_ref, seeds_ref, shape_ref, sems, *, normalizer
):
    copies = [
        pltpu.make_async_copy(source, target, sems.at[i])
        for i, (source, target) in enumerate([
            (rows_hbm, rows_ref), (seeds_hbm, seeds_ref), (shape_hbm, shape_ref)
        ])
    ]
    for copy in copies:
        copy.start()
    for copy in copies:
        copy.wait()
    sum_eddies(rows_ref, seeds_ref, shape_ref, plane_ref, normalizer)


def pack_kernel(
    plane_ref, v_ref, held_plane_ref, core_ref, chip_ref, pitch_ref, span_ref, span_held
):
    first_span = lax.axis_index("span") == 0
    lane = lanes()
    pick = trace_selector()
    held_plane_ref[...] = plane_ref[...]
    span_held[...] = jnp.zeros_like(span_held)
    for pair in range(EX // 2):
        at = slice(pair * PAIR, (pair + 1) * PAIR)
        for f in range(FIELDS):
            pack_field(
                f, dot(pick, v_ref[f, :, at]), pair, first_span, lane, pitch_ref, span_held
            )
    span_ref[...] = span_held[...].astype(bf16)
    store_stream(
        v_ref[:, 48:64, (EX - 1) * CELLS :], v_ref[:, 0:16, 0:CELLS], core_ref, chip_ref
    )


def mix(row, arrays):
    total = row[0] * arrays[0]
    for g in range(1, FIELDS):
        total = total + row[g] * arrays[g]
    return total


def flux_row(jacobian, d, f):
    return [jacobian[f, d, g] for g in range(FIELDS)]


def face_row(jacobian, t, f):
    half = 0.5 * (1.0 if t % 2 else -1.0)
    row = [half * jacobian[f, t // 2, g] for g in range(FIELDS)]
    row[f] = row[f] - 0.5
    return row


def fill(weights, parts):
    column = 0
    for part in parts:
        weights[:, column : column + part.shape[1]] = part
        column += part.shape[1]
    return weights[...]


def mix_fluxes(read, coefs, mixed):
    def rows_step(r):
        def run():
            rows = [read(f, r, r + 16).astype(f32) for f in range(FIELDS)]
            for d in range(3):
                for f in range(FIELDS):
                    mixed[f, 64 * d + r : 64 * d + r + 16, :] = mix(
                        flux_row(coefs, d, f), rows
                    ).astype(bf16)

        return run

    return [rows_step(r) for r in range(0, NODES, 16)]


def write_jumps(t, jumps, coefs, mixed, first_row):
    for f in range(FIELDS):
        mixed[f, first_row : first_row + 16, :] = mix(face_row(coefs, t, f), jumps).astype(bf16)


def mix_stream(read, lower, upper, coefs, mixed, row):
    def low():
        jumps = [lower(f) - read(f, 0, 16).astype(f32) for f in range(FIELDS)]
        write_jumps(0, jumps, coefs, mixed, row)

    def high():
        jumps = [upper(f) - read(f, 48, 64).astype(f32) for f in range(FIELDS)]
        write_jumps(1, jumps, coefs, mixed, row + 16)

    return [low, high]


def mix_sides(trace, pitch, span, layers, coefs, mixed, row, first_span, lane):
    def halves(f, r):
        own = trace(f, r, r + 16)
        return [own[:, h * CELLS : (h + 1) * CELLS] for h in range(len(layers))]

    def join(parts):
        return parts[0] if len(parts) == 1 else jnp.concatenate(parts, axis=1)

    def pitch_low():
        jumps = []
        for f in range(FIELDS):
            near, low, high = pitch(f), halves(f, 0), halves(f, 16)
            jumps.append(join([
                jnp.where(
                    lane < 32, pltpu.roll(near, 64 if h == 0 else 32, 1), pltpu.roll(high[h], 32, 1)
                ) - low[h]
                for h in range(len(layers))
            ]))
        write_jumps(2, jumps, coefs, mixed, row)

    def pitch_high():
        jumps = []
        for f in range(FIELDS):
            near, low, high = pitch(f), halves(f, 0), halves(f, 16)
            jumps.append(join([
                jnp.where(
                    lane >= 96, pltpu.roll(near, 96 if h == 0 else 64, 1), pltpu.roll(low[h], 96, 1)
                ) - high[h]
                for h in range(len(layers))
            ]))
        write_jumps(3, jumps, coefs, mixed, row + 16)

    def arrived(f, layer):
        return pltpu.roll(span(f), lax.rem(jnp.where(first_span, 31, 128) - layer, 128), 1)

    def span_low():
        jumps = []
        for f in range(FIELDS):
            low, high = halves(f, 32), halves(f, 48)
            jumps.append(join([
                jnp.where(
                    (lane & 31) == 0,
                    jnp.where(first_span, low[h], arrived(f, layer)),
                    pltpu.roll(high[h], 1, 1),
                ) - low[h]
                for h, layer in enumerate(layers)
            ]))
        write_jumps(4, jumps, coefs, mixed, row + 32)

    def span_high():
        jumps = []
        for f in range(FIELDS):
            low, high = halves(f, 32), halves(f, 48)
            jumps.append(join([
                jnp.where(
                    (lane & 31) == 31,
                    jnp.where(first_span, arrived(f, layer), high[h]),
                    pltpu.roll(low[h], 127, 1),
                ) - high[h]
                for h, layer in enumerate(layers)
            ]))
        write_jumps(5, jumps, coefs, mixed, row + 48)

    return [pitch_low, pitch_high, span_low, span_high]


def mix_wall(read, pinned, mixed, row):
    def run():
        for f in range(FIELDS):
            mixed[f, row : row + 64, :] = (read(f, 0, 64).astype(f32) * pinned()).astype(bf16)

    return [run]


def staggered(stages):
    held = [None] * FIELDS
    steps = []

    def step(stage, f):
        def run():
            held[f] = stage(f, held[f])

        return run

    for turn in range(FIELDS + len(stages) - 1):
        for k, stage in enumerate(stages):
            if 0 <= turn - k < FIELDS:
                steps.append(step(stage, turn - k))
    return steps


def interleave(first, second):
    count = max(len(first), len(second))
    for i in range(count):
        for steps in (first, second):
            for step in steps[i * len(steps) // count : (i + 1) * len(steps) // count]:
                step()


def pipeline(vector, matrix):
    for step in vector[0]:
        step()
    for p in range(len(matrix)):
        interleave(matrix[p], vector[p + 1] if p + 1 < len(vector) else [])


def finish(read, base, smooth):
    def trial(f, rate):
        v = read(f, 0, 64).astype(f32)
        if base is None:
            now = v - TIME_STEP * rate
        else:
            now = 0.5 * (base(f).astype(f32) + v - TIME_STEP * rate)
        return dot(smooth, now.astype(bf16))

    return trial


def with_traces(filter_matrix, pick):
    return jnp.concatenate([filter_matrix, dot(pick, filter_matrix).astype(bf16)], axis=0)


def mix_traces(read, pick, own):
    def run():
        for f in range(FIELDS):
            own[f] = dot(pick, read(f, 0, 64)).astype(bf16)

    return [run]


def place(pair):
    return slice(pair * PAIR, (pair + 1) * PAIR)


def lower_pair(v_ref, edge, pair):
    def lower(f):
        if pair:
            return v_ref[f, 48:64, pair * PAIR - CELLS : (pair + 1) * PAIR - CELLS].astype(f32)
        return jnp.concatenate([edge(f), v_ref[f, 48:64, 0:CELLS].astype(f32)], axis=1)

    return lower


def upper_pair(v_ref, above, pair):
    first = pair * PAIR + CELLS
    last_rans = lax.axis_index("rans") == lax.axis_size("rans") - 1

    def upper(f):
        if pair < EX // 2 - 1:
            return v_ref[f, 0:16, first : first + PAIR].astype(f32)
        edge = jnp.where(
            last_rans, v_ref[f, 48:64, first : first + CELLS].astype(f32), above(f)
        )
        return jnp.concatenate([v_ref[f, 0:16, first : first + CELLS].astype(f32), edge], axis=1)

    return upper


def phase_one_kernel(
    v_ref, from_core_ref, from_chip_ref, near_ref, far_ref, pin_ref, coefs, volume_ref, lift_ref,
    wall_ref, filter_ref,
    out_ref, out_trace_ref, core_ref, chip_ref, pitch_ref, span_ref, mixed, own, weights_held,
    span_held,
):
    first_span = lax.axis_index("span") == 0
    lane = lanes()
    pick = trace_selector()
    smooth = with_traces(filter_ref[...], pick)
    weights = fill(
        weights_held, [volume_ref[0], volume_ref[1], volume_ref[2], lift_ref[...], wall_ref[...]]
    )
    span_held[...] = jnp.zeros_like(span_held)
    below, above = from_below(from_core_ref, from_chip_ref), from_above(from_core_ref, from_chip_ref)
    vector, matrix = [], []

    def add(pair):
        at = place(pair)
        rows, held = mixed.at[pair % 2], own.at[pair % 2]

        def read(f, r0, r1):
            return v_ref[f, r0:r1, at]

        def store(f, value):
            out_ref[f, :, at] = value[0:64].astype(bf16)
            trace = value[64:128]
            out_trace_ref[f, :, at] = trace.astype(bf16)
            pack_field(f, trace, pair, first_span, lane, pitch_ref, span_held)

        vector.append(
            mix_traces(read, pick, held)
            + mix_fluxes(read, coefs, rows)
            + mix_stream(
                read,
                lower_pair(v_ref, below, pair),
                upper_pair(v_ref, above, pair),
                coefs, rows, 192,
            )
            + mix_sides(
                lambda f, r0, r1: held[f, r0:r1].astype(f32),
                lambda f: near_ref[f, :, pair * CELLS : (pair + 1) * CELLS].astype(f32),
                lambda f: far_ref[f].astype(f32),
                [2 * pair, 2 * pair + 1], coefs, rows, 224, first_span, lane,
            )
            + mix_wall(read, lambda: pin_ref[:, at].astype(f32), rows, 288)
        )
        matrix.append(
            staggered([lambda f, _: dot(weights, rows[f]), finish(read, None, smooth), store])
        )

    for pair in range(EX // 2):
        add(pair)
    pipeline(vector, matrix)
    span_ref[...] = span_held[...].astype(bf16)
    store_stream(
        out_ref[:, 48:64, (EX - 1) * CELLS :], out_ref[:, 0:16, 0:CELLS], core_ref, chip_ref
    )


def inner_two_kernel(v_ref, coefs, volume_ref, part_ref, mixed, weights_held):
    weights = fill(weights_held, [volume_ref[d] for d in range(3)])
    vector, matrix = [], []

    def add(pair):
        at = place(pair)
        rows = mixed.at[pair % 2]

        def store(f, value):
            part_ref[f, :, at] = value

        vector.append(mix_fluxes(lambda f, r0, r1: v_ref[f, r0:r1, at], coefs, rows))
        matrix.append(staggered([lambda f, _: dot(weights, rows[f]), store]))

    for pair in range(EX // 2):
        add(pair)
    pipeline(vector, matrix)


def outer_two_kernel(
    v_ref, trace_ref, base_ref, part_ref, mean_ref, amp_ref, plane_ref, from_core_ref, from_chip_ref,
    near_ref, far_ref, pin_ref, coefs, lift_ref, wall_ref, smooth_ref, out_ref, mixed, weights_held,
):
    first_span = lax.axis_index("span") == 0
    first_rans = lax.axis_index("rans") == 0
    lane = lanes()
    weights, smooth = fill(weights_held, [lift_ref[...], wall_ref[...]]), smooth_ref[...]
    below, above = from_below(from_core_ref, from_chip_ref), from_above(from_core_ref, from_chip_ref)
    vector, matrix = [], []

    def edge(f):
        return jnp.where(first_rans, inflow_of(mean_ref, amp_ref, plane_ref)(f), below(f))

    def add(pair):
        at = place(pair)
        rows = mixed.at[pair % 2]

        def read(f, r0, r1):
            return v_ref[f, r0:r1, at]

        def store(f, value):
            out_ref[f, :, at] = value.astype(bf16)

        vector.append(
            mix_stream(
                read, lower_pair(v_ref, edge, pair), upper_pair(v_ref, above, pair), coefs, rows, 0
            )
            + mix_sides(
                lambda f, r0, r1: trace_ref[f, r0:r1, at].astype(f32),
                lambda f: near_ref[f, :, pair * CELLS : (pair + 1) * CELLS].astype(f32),
                lambda f: far_ref[f].astype(f32),
                [2 * pair, 2 * pair + 1], coefs, rows, 32, first_span, lane,
            )
            + mix_wall(read, lambda: pin_ref[:, at].astype(f32), rows, 96)
        )
        matrix.append(
            staggered([
                lambda f, _: dot(weights, rows[f]) + part_ref[f, :, at],
                finish(read, lambda f: base_ref[f, :, at], smooth),
                store,
            ])
        )

    for pair in range(EX // 2):
        add(pair)
    pipeline(vector, matrix)


def inflow_of(mean_ref, amp_ref, plane_ref):
    return lambda f: mean_ref[f] + amp_ref[f] * plane_ref[f]


def inflow_kernel(
    held_ref, held_trace_ref, held_pitch_ref, held_span_ref, v_ref, mean_ref, amp_ref,
    plane_ref, near_ref, far_ref, pin_ref, coefs, volume_ref, lift_ref, wall_ref, filter_ref, out_ref,
    out_trace_ref,
    pitch_ref, span_ref, mixed, own, weights_held,
):
    first_span = lax.axis_index("span") == 0
    first_rans = lax.axis_index("rans") == 0
    lane = lanes()

    @pl.when(first_rans)
    def _():
        pick = trace_selector()
        smooth = with_traces(filter_ref[...], pick)
        weights = fill(
            weights_held, [volume_ref[0], volume_ref[1], volume_ref[2], lift_ref[...], wall_ref[...]]
        )

        def read(f, r0, r1):
            return v_ref[f, r0:r1, 0:CELLS]

        def store(f, value):
            out_ref[f] = value[0:64].astype(bf16)
            t = value[64:128]
            out_trace_ref[f] = t.astype(bf16)
            pitch = jnp.where(lane < 32, t[0:16], pltpu.roll(t[16:32], 96, 1))
            pitch_ref[f] = jnp.where(
                (lane & 63) < 32, pitch, held_pitch_ref[f].astype(f32)
            ).astype(bf16)
            span_ref[f] = pack_span(
                held_span_ref[f].astype(f32), t[32:48], t[48:64], 0, first_span, lane
            ).astype(bf16)

        vector = (
            mix_traces(read, pick, own)
            + mix_stream(
                read,
                inflow_of(mean_ref, amp_ref, plane_ref),
                lambda f: v_ref[f, 0:16, CELLS:PAIR].astype(f32),
                coefs, mixed, 192,
            )
            + mix_sides(
                lambda f, r0, r1: own[f, r0:r1].astype(f32),
                lambda f: near_ref[f].astype(f32),
                lambda f: far_ref[f].astype(f32),
                [0], coefs, mixed, 224, first_span, lane,
            )
            + mix_fluxes(read, coefs, mixed)
            + mix_wall(read, lambda: pin_ref[...].astype(f32), mixed, 288)
        )
        matrix = staggered(
            [lambda f, _: dot(weights, mixed[f]), finish(read, None, smooth), store]
        )
        pipeline([vector], [matrix])

    @pl.when(jnp.logical_not(first_rans))
    def _():
        out_ref[...] = held_ref[...]
        out_trace_ref[...] = held_trace_ref[...]
        pitch_ref[...] = held_pitch_ref[...]
        span_ref[...] = held_span_ref[...]


VMEM = pl.BlockSpec(memory_space=pltpu.VMEM)
SMEM = pl.BlockSpec(memory_space=pltpu.SMEM)
PARAMS = pltpu.CompilerParams(vmem_limit_bytes=40 * 2**20)


def shape_of(*dims, dtype=bf16):
    return jax.ShapeDtypeStruct(dims, dtype)


def front(*dims):
    return pl.BlockSpec(dims, lambda i: (0,) * len(dims))


def cost(us):
    return pl.CostEstimate(flops=int(us * 1e8), bytes_accessed=int(us * 3e6), transcendentals=0)


def body(
    solution, volume_ops, flux_jacobian, lift_matrix, filter_matrix, wall_matrix, pinched_map,
    mode_rows, mode_seeds, mode_shape, mean_inflow, eddy_amplitude,
):
    ranks = lax.axis_size("rans")
    eddies, foot = mode_shape.shape[2:]
    plane_rows = mean_inflow.shape[3]
    faces = shape_of(FIELDS, 16, CELLS)
    def slab(z, y, core):
        return 8 * z + 2 * y + core

    columns = ranks // 8
    root_y = [0] + [1] * (columns - 1)
    first_level = [
        [
            (slab(z, [y for y in range(4) if y != root_y[z]][turn], core), slab(z, root_y[z], core))
            for z in range(columns)
            for core in range(2)
        ]
        for turn in range(3)
    ]
    second_level = [
        [
            (slab(z + up, root_y[z + up], core), slab(z, root_y[z], 0))
            for z in range(0, columns, 2)
        ]
        for up, core in ((0, 1), (1, 0), (1, 1))
    ]
    third_level = [[(slab(z, root_y[z], 0), 0)] for z in (2, 6, 4)]

    def gather_sum(value, level, own=None):
        parts = [lax.ppermute(value, "rans", pairs) for pairs in level]
        value = value if own is None else own
        for part in parts:
            value = value + part
        return value

    jacobian = flux_jacobian.transpose(1, 0, 2)
    pins = pinched_map.reshape(1, -1)
    elements = solution.shape[2]
    traces = shape_of(FIELDS, NODES, elements)
    sends = (faces, faces, shape_of(FIELDS, 16, EX // 2 * CELLS), faces)
    swap = [(0, 1), (1, 0)]
    same_chip = [(i, i ^ 1) for i in range(ranks)]
    next_chip = [(a + 1, b + 1) for a, b in same_chip if max(a, b) + 1 < ranks]

    span_scratch = pltpu.VMEM((FIELDS, 16, CELLS), f32)
    plane = pl.pallas_call(
        functools.partial(
            plane_kernel, normalizer=float((plane_rows / (eddies * ranks * foot)) ** 0.5)
        ),
        out_shape=shape_of(FIELDS, 16, CELLS, dtype=f32),
        in_specs=[pl.BlockSpec(memory_space=pltpu.HBM)] * 3,
        out_specs=VMEM,
        scratch_shapes=[
            pltpu.VMEM((foot, eddies), jnp.int32),
            pltpu.VMEM((1, eddies), jnp.int32),
            pltpu.VMEM((foot, eddies), f32),
            pltpu.SemaphoreType.DMA((3,)),
        ],
        compiler_params=pltpu.CompilerParams(vmem_limit_bytes=60 * 2**20),
        cost_estimate=cost(4),
        name="eddy_plane",
    )(mode_rows[0, 0].T, mode_seeds.reshape(1, eddies), mode_shape[0, 0].T)
    held_plane, core, chip, pitch, span = pl.pallas_call(
        pack_kernel,
        out_shape=(shape_of(FIELDS, 16, CELLS, dtype=f32),) + sends,
        in_specs=[VMEM] * 2,
        out_specs=(VMEM,) * 5,
        scratch_shapes=[span_scratch],
        compiler_params=PARAMS,
        cost_estimate=cost(1),
        name="pack_faces",
    )(plane, solution)
    plane = gather_sum(plane, first_level, held_plane)
    near = lax.ppermute(pitch, "pitch", swap)
    plane, chip, core, span = lax.optimization_barrier((plane, chip, core, span))
    plane = gather_sum(plane, second_level)
    from_chip = lax.ppermute(chip, "rans", next_chip)
    core, span, near = lax.optimization_barrier((core, span, near))
    far = lax.ppermute(span, "span", swap)
    from_core = lax.ppermute(core, "rans", same_chip)
    plane, near, far, from_core = lax.optimization_barrier((plane, near, far, from_core))
    plane = gather_sum(plane, third_level)

    phase_one, trace_one, core, chip, pitch, span = pl.pallas_call(
        phase_one_kernel,
        out_shape=(traces, traces) + sends,
        in_specs=[VMEM] * 6 + [SMEM] + [VMEM] * 4,
        out_specs=(VMEM,) * 6,
        scratch_shapes=[
            pltpu.VMEM((2, FIELDS, MIXED, PAIR), bf16),
            pltpu.VMEM((2, FIELDS, NODES, PAIR), bf16),
            pltpu.VMEM((NODES, MIXED), bf16),
            span_scratch,
        ],
        compiler_params=PARAMS,
        cost_estimate=cost(6),
        name="phase_one",
    )(
        solution, from_core, from_chip, near, far, pins, jacobian, volume_ops, lift_matrix, wall_matrix,
        filter_matrix,
    )
    from_core = lax.ppermute(core, "rans", same_chip)
    from_chip = lax.ppermute(chip, "rans", next_chip)
    plane, from_core = lax.optimization_barrier((plane, from_core))

    mean = mean_inflow.reshape(FIELDS, 16, CELLS)
    amplitude = eddy_amplitude.reshape(FIELDS, 16, CELLS)
    layer = front(FIELDS, NODES, CELLS)
    face = front(FIELDS, 16, CELLS)
    phase_one, trace_one, pitch, span = pl.pallas_call(
        inflow_kernel,
        grid=(1,),
        out_shape=(traces, traces, sends[2], sends[3]),
        in_specs=[layer, layer, face, face, front(FIELDS, NODES, PAIR)]
        + [face] * 5
        + [
            front(1, CELLS), SMEM, front(3, NODES, NODES), front(NODES, 96), front(NODES, NODES),
            front(NODES, NODES),
        ],
        out_specs=(layer, layer, face, face),
        scratch_shapes=[
            pltpu.VMEM((FIELDS, MIXED, CELLS), bf16),
            pltpu.VMEM((FIELDS, NODES, CELLS), bf16),
            pltpu.VMEM((NODES, MIXED), bf16),
        ],
        input_output_aliases={0: 0, 1: 1, 2: 2, 3: 3},
        compiler_params=PARAMS,
        cost_estimate=cost(0.1),
        name="inflow_layer",
    )(
        phase_one, trace_one, pitch, span, solution, mean, amplitude, plane, near, far,
        pins, jacobian, volume_ops, lift_matrix, wall_matrix, filter_matrix,
    )
    near = lax.ppermute(pitch, "pitch", swap)
    far = lax.ppermute(span, "span", swap)
    part = pl.pallas_call(
        inner_two_kernel,
        out_shape=shape_of(FIELDS, NODES, elements, dtype=f32),
        in_specs=[VMEM, SMEM, VMEM],
        out_specs=VMEM,
        scratch_shapes=[
            pltpu.VMEM((2, FIELDS, INNER, PAIR), bf16), pltpu.VMEM((NODES, INNER), bf16)
        ],
        compiler_params=PARAMS,
        cost_estimate=cost(0.1),
        name="inner_two",
    )(phase_one, jacobian, volume_ops)
    return pl.pallas_call(
        outer_two_kernel,
        out_shape=traces,
        in_specs=[VMEM] * 12 + [SMEM] + [VMEM] * 3,
        out_specs=VMEM,
        scratch_shapes=[
            pltpu.VMEM((2, FIELDS, MIXED - INNER, PAIR), bf16),
            pltpu.VMEM((NODES, MIXED - INNER), bf16),
        ],
        compiler_params=PARAMS,
        cost_estimate=cost(4),
        name="outer_two",
    )(
        phase_one, trace_one, solution, part, mean, amplitude, plane, from_core, from_chip, near, far,
        pins, jacobian, lift_matrix, wall_matrix, filter_matrix,
    )


def solution(mesh):
    spread = P(None, None, ("rans", "pitch", "span"))
    in_specs = (
        spread,
        P(),
        P(),
        P(),
        P(),
        P(),
        P(("rans", "pitch", "span")),
        P("pitch", "span", "rans", None),
        P("pitch", "span", "rans"),
        P("pitch", "span", "rans", None),
        P("pitch", "span", None, None),
        P("pitch", "span", None, None),
    )
    return jax.shard_map(body, mesh=mesh, in_specs=in_specs, out_specs=spread, check_vma=False)
```

```python
import functools

import jax
import jax.numpy as jnp
from jax import lax
from jax.experimental import pallas as pl
from jax.experimental.pallas import tpu as pltpu
from jax.sharding import PartitionSpec as P

FIELDS = 5
NODES = 64
EX = 12
CELLS = 128
SPAN_CELLS = 32
PAIR = 2 * CELLS
MIXED = 352
INNER = 192
TIME_STEP = 0.4
f32 = jnp.float32
bf16 = jnp.bfloat16


def trace_selector():
    row = lax.broadcasted_iota(jnp.int32, (64, 64), 0)
    node = lax.broadcasted_iota(jnp.int32, (64, 64), 1)
    face, first, second = row >> 4, (row >> 2) & 3, row & 3
    on_pitch = second + jnp.where(face == 1, 12, 0)
    on_span = 4 * second + jnp.where(face == 3, 3, 0)
    source = 16 * first + jnp.where(face < 2, on_pitch, on_span)
    return jnp.where(node == source, 1.0, 0.0).astype(bf16)


def dot(a, b):
    return jnp.dot(a, b, preferred_element_type=f32)


def lanes():
    return lax.broadcasted_iota(jnp.int32, (16, CELLS), 1)


def sum_eddies(rows_ref, seeds_ref, shape_ref, plane_ref, normalizer):
    seeds = seeds_ref[...]
    signs = [(2 * ((seeds >> f) & 1) - 1).astype(f32) for f in range(FIELDS)]
    signs = [jnp.broadcast_to(s, (32, s.shape[1])).astype(bf16) for s in signs]
    eddies = rows_ref.shape[1]
    high_row = lax.broadcasted_iota(jnp.int32, (16, eddies), 0)
    low_row = lax.broadcasted_iota(jnp.int32, (CELLS, eddies), 0)

    def chunk(i, total):
        start = pl.multiple_of(i * 8, 8)
        rows = rows_ref[pl.ds(start, 8), :]
        shapes = shape_ref[pl.ds(start, 8), :]
        for q in range(8):
            row, shape = rows[q : q + 1], shapes[q : q + 1]
            placed = jnp.where((row >> 7) == high_row, shape, 0.0)
            coarse = placed.astype(bf16)
            fine = (placed - coarse.astype(f32)).astype(bf16)
            both = jnp.concatenate([coarse, fine], axis=0)
            signed = jnp.concatenate([both * s for s in signs], axis=0)
            hot = jnp.where((row & 127) == low_row, 1.0, 0.0).astype(bf16)
            total = total + lax.dot_general(
                signed, hot, (((1,), (1,)), ((), ())), preferred_element_type=f32
            )
        return total

    total = lax.fori_loop(
        0, rows_ref.shape[0] // 8, chunk, jnp.zeros((160, CELLS), f32), unroll=True
    )
    for f in range(FIELDS):
        plane_ref[f] = (total[32 * f : 32 * f + 16] + total[32 * f + 16 : 32 * f + 32]) * normalizer


def pack_pitch(traces, lane):
    (low0, high0), (low1, high1) = traces
    return jnp.where(
        lane < 32,
        low0,
        jnp.where(
            lane < 64,
            pltpu.roll(low1, 32, 1),
            jnp.where(lane < 96, pltpu.roll(high0, 96, 1), high1),
        ),
    )


def pack_span(held, low, high, layer, first_span, lane):
    edge = jnp.where(first_span, high, low)
    shift = lax.rem(layer + jnp.where(first_span, 97, 0), 128)
    return jnp.where((lane & 31) == layer, pltpu.roll(edge, shift, 1), held)


def pack_field(f, trace, pair, first_span, lane, pitch_ref, span_held):
    halves = [trace[:, :CELLS], trace[:, CELLS:]]
    packed = pack_pitch([(h[0:16], h[16:32]) for h in halves], lane)
    pitch_ref[f, :, pair * CELLS : (pair + 1) * CELLS] = packed.astype(bf16)
    held = span_held[f]
    for h in range(2):
        held = pack_span(held, halves[h][32:48], halves[h][48:64], 2 * pair + h, first_span, lane)
    span_held[f] = held


def is_even():
    return (lax.axis_index("rans") & 1) == 0


def store_stream(up, down, near_chip_ref, far_chip_ref):
    even = is_even()
    near_chip_ref[...] = jnp.where(even, up, down)
    far_chip_ref[...] = jnp.where(even, down, up)


def from_below(near_chip_ref, far_chip_ref):
    even = is_even()
    return lambda f: jnp.where(even, far_chip_ref[f].astype(f32), near_chip_ref[f].astype(f32))


def from_above(near_chip_ref, far_chip_ref):
    even = is_even()
    return lambda f: jnp.where(even, near_chip_ref[f].astype(f32), far_chip_ref[f].astype(f32))


def plane_kernel(
    rows_hbm, seeds_hbm, shape_hbm, plane_ref, rows_ref, seeds_ref, shape_ref, sems, *, normalizer
):
    copies = [
        pltpu.make_async_copy(source, target, sems.at[i])
        for i, (source, target) in enumerate([
            (rows_hbm, rows_ref), (seeds_hbm, seeds_ref), (shape_hbm, shape_ref)
        ])
    ]
    for copy in copies:
        copy.start()
    for copy in copies:
        copy.wait()
    sum_eddies(rows_ref, seeds_ref, shape_ref, plane_ref, normalizer)


def pack_kernel(
    plane_ref, v_ref, held_plane_ref, core_ref, chip_ref, pitch_ref, span_ref, span_held
):
    first_span = lax.axis_index("span") == 0
    lane = lanes()
    pick = trace_selector()
    held_plane_ref[...] = plane_ref[...]
    span_held[...] = jnp.zeros_like(span_held)
    for pair in range(EX // 2):
        at = slice(pair * PAIR, (pair + 1) * PAIR)
        for f in range(FIELDS):
            pack_field(
                f, dot(pick, v_ref[f, :, at]), pair, first_span, lane, pitch_ref, span_held
            )
    span_ref[...] = span_held[...].astype(bf16)
    store_stream(
        v_ref[:, 48:64, (EX - 1) * CELLS :], v_ref[:, 0:16, 0:CELLS], core_ref, chip_ref
    )


def mix(row, arrays):
    total = row[0] * arrays[0]
    for g in range(1, FIELDS):
        total = total + row[g] * arrays[g]
    return total


def flux_row(jacobian, d, f):
    return [jacobian[f, d, g] for g in range(FIELDS)]


def face_row(jacobian, t, f):
    half = 0.5 * (1.0 if t % 2 else -1.0)
    row = [half * jacobian[f, t // 2, g] for g in range(FIELDS)]
    row[f] = row[f] - 0.5
    return row


def fill(weights, parts):
    column = 0
    for part in parts:
        weights[:, column : column + part.shape[1]] = part
        column += part.shape[1]
    return weights[...]


def mix_fluxes(read, coefs, mixed):
    def rows_step(r):
        def run():
            rows = [read(f, r, r + 16).astype(f32) for f in range(FIELDS)]
            for d in range(3):
                for f in range(FIELDS):
                    mixed[f, 64 * d + r : 64 * d + r + 16, :] = mix(
                        flux_row(coefs, d, f), rows
                    ).astype(bf16)

        return run

    return [rows_step(r) for r in range(0, NODES, 16)]


def write_jumps(t, jumps, coefs, mixed, first_row):
    for f in range(FIELDS):
        mixed[f, first_row : first_row + 16, :] = mix(face_row(coefs, t, f), jumps).astype(bf16)


def mix_stream(read, lower, upper, coefs, mixed, row):
    def low():
        jumps = [lower(f) - read(f, 0, 16).astype(f32) for f in range(FIELDS)]
        write_jumps(0, jumps, coefs, mixed, row)

    def high():
        jumps = [upper(f) - read(f, 48, 64).astype(f32) for f in range(FIELDS)]
        write_jumps(1, jumps, coefs, mixed, row + 16)

    return [low, high]


def mix_sides(trace, pitch, span, layers, coefs, mixed, row, first_span, lane):
    def halves(f, r):
        own = trace(f, r, r + 16)
        return [own[:, h * CELLS : (h + 1) * CELLS] for h in range(len(layers))]

    def join(parts):
        return parts[0] if len(parts) == 1 else jnp.concatenate(parts, axis=1)

    def pitch_low():
        jumps = []
        for f in range(FIELDS):
            near, low, high = pitch(f), halves(f, 0), halves(f, 16)
            jumps.append(join([
                jnp.where(
                    lane < 32, pltpu.roll(near, 64 if h == 0 else 32, 1), pltpu.roll(high[h], 32, 1)
                ) - low[h]
                for h in range(len(layers))
            ]))
        write_jumps(2, jumps, coefs, mixed, row)

    def pitch_high():
        jumps = []
        for f in range(FIELDS):
            near, low, high = pitch(f), halves(f, 0), halves(f, 16)
            jumps.append(join([
                jnp.where(
                    lane >= 96, pltpu.roll(near, 96 if h == 0 else 64, 1), pltpu.roll(low[h], 96, 1)
                ) - high[h]
                for h in range(len(layers))
            ]))
        write_jumps(3, jumps, coefs, mixed, row + 16)

    def arrived(f, layer):
        return pltpu.roll(span(f), lax.rem(jnp.where(first_span, 31, 128) - layer, 128), 1)

    def span_low():
        jumps = []
        for f in range(FIELDS):
            low, high = halves(f, 32), halves(f, 48)
            jumps.append(join([
                jnp.where(
                    (lane & 31) == 0,
                    jnp.where(first_span, low[h], arrived(f, layer)),
                    pltpu.roll(high[h], 1, 1),
                ) - low[h]
                for h, layer in enumerate(layers)
            ]))
        write_jumps(4, jumps, coefs, mixed, row + 32)

    def span_high():
        jumps = []
        for f in range(FIELDS):
            low, high = halves(f, 32), halves(f, 48)
            jumps.append(join([
                jnp.where(
                    (lane & 31) == 31,
                    jnp.where(first_span, arrived(f, layer), high[h]),
                    pltpu.roll(low[h], 127, 1),
                ) - high[h]
                for h, layer in enumerate(layers)
            ]))
        write_jumps(5, jumps, coefs, mixed, row + 48)

    return [pitch_low, pitch_high, span_low, span_high]


def mix_wall(read, pinned, mixed, row):
    def run():
        for f in range(FIELDS):
            mixed[f, row : row + 64, :] = (read(f, 0, 64).astype(f32) * pinned()).astype(bf16)

    return [run]


def staggered(stages):
    held = [None] * FIELDS
    steps = []

    def step(stage, f):
        def run():
            held[f] = stage(f, held[f])

        return run

    for turn in range(FIELDS + len(stages) - 1):
        for k, stage in enumerate(stages):
            if 0 <= turn - k < FIELDS:
                steps.append(step(stage, turn - k))
    return steps


def interleave(first, second):
    count = max(len(first), len(second))
    for i in range(count):
        for steps in (first, second):
            for step in steps[i * len(steps) // count : (i + 1) * len(steps) // count]:
                step()


def pipeline(vector, matrix):
    for step in vector[0]:
        step()
    for p in range(len(matrix)):
        interleave(matrix[p], vector[p + 1] if p + 1 < len(vector) else [])


def finish(read, base, smooth):
    def trial(f, rate):
        v = read(f, 0, 64).astype(f32)
        if base is None:
            now = v - TIME_STEP * rate
        else:
            now = 0.5 * (base(f).astype(f32) + v - TIME_STEP * rate)
        return dot(smooth, now.astype(bf16))

    return trial


def with_traces(filter_matrix, pick):
    return jnp.concatenate([filter_matrix, dot(pick, filter_matrix).astype(bf16)], axis=0)


def mix_traces(read, pick, own):
    def run():
        for f in range(FIELDS):
            own[f] = dot(pick, read(f, 0, 64)).astype(bf16)

    return [run]


def place(pair):
    return slice(pair * PAIR, (pair + 1) * PAIR)


def lower_pair(v_ref, edge, pair):
    def lower(f):
        if pair:
            return v_ref[f, 48:64, pair * PAIR - CELLS : (pair + 1) * PAIR - CELLS].astype(f32)
        return jnp.concatenate([edge(f), v_ref[f, 48:64, 0:CELLS].astype(f32)], axis=1)

    return lower


def upper_pair(v_ref, above, pair):
    first = pair * PAIR + CELLS
    last_rans = lax.axis_index("rans") == lax.axis_size("rans") - 1

    def upper(f):
        if pair < EX // 2 - 1:
            return v_ref[f, 0:16, first : first + PAIR].astype(f32)
        edge = jnp.where(
            last_rans, v_ref[f, 48:64, first : first + CELLS].astype(f32), above(f)
        )
        return jnp.concatenate([v_ref[f, 0:16, first : first + CELLS].astype(f32), edge], axis=1)

    return upper


def phase_one_kernel(
    v_ref, from_core_ref, from_chip_ref, near_ref, far_ref, pin_ref, coefs, volume_ref, lift_ref,
    wall_ref, filter_ref,
    out_ref, out_trace_ref, core_ref, chip_ref, pitch_ref, span_ref, mixed, own, weights_held,
    span_held,
):
    first_span = lax.axis_index("span") == 0
    lane = lanes()
    pick = trace_selector()
    smooth = with_traces(filter_ref[...], pick)
    weights = fill(
        weights_held, [volume_ref[0], volume_ref[1], volume_ref[2], lift_ref[...], wall_ref[...]]
    )
    span_held[...] = jnp.zeros_like(span_held)
    below, above = from_below(from_core_ref, from_chip_ref), from_above(from_core_ref, from_chip_ref)
    vector, matrix = [], []

    def add(pair):
        at = place(pair)
        rows, held = mixed.at[pair % 2], own.at[pair % 2]

        def read(f, r0, r1):
            return v_ref[f, r0:r1, at]

        def store(f, value):
            out_ref[f, :, at] = value[0:64].astype(bf16)
            trace = value[64:128]
            out_trace_ref[f, :, at] = trace.astype(bf16)
            pack_field(f, trace, pair, first_span, lane, pitch_ref, span_held)

        vector.append(
            mix_traces(read, pick, held)
            + mix_fluxes(read, coefs, rows)
            + mix_stream(
                read,
                lower_pair(v_ref, below, pair),
                upper_pair(v_ref, above, pair),
                coefs, rows, 192,
            )
            + mix_sides(
                lambda f, r0, r1: held[f, r0:r1].astype(f32),
                lambda f: near_ref[f, :, pair * CELLS : (pair + 1) * CELLS].astype(f32),
                lambda f: far_ref[f].astype(f32),
                [2 * pair, 2 * pair + 1], coefs, rows, 224, first_span, lane,
            )
            + mix_wall(read, lambda: pin_ref[:, at].astype(f32), rows, 288)
        )
        matrix.append(
            staggered([lambda f, _: dot(weights, rows[f]), finish(read, None, smooth), store])
        )

    for pair in range(EX // 2):
        add(pair)
    pipeline(vector, matrix)
    span_ref[...] = span_held[...].astype(bf16)
    store_stream(
        out_ref[:, 48:64, (EX - 1) * CELLS :], out_ref[:, 0:16, 0:CELLS], core_ref, chip_ref
    )


def inner_two_kernel(v_ref, coefs, volume_ref, part_ref, mixed, weights_held):
    weights = fill(weights_held, [volume_ref[d] for d in range(3)])
    vector, matrix = [], []

    def add(pair):
        at = place(pair)
        rows = mixed.at[pair % 2]

        def store(f, value):
            part_ref[f, :, at] = value

        vector.append(mix_fluxes(lambda f, r0, r1: v_ref[f, r0:r1, at], coefs, rows))
        matrix.append(staggered([lambda f, _: dot(weights, rows[f]), store]))

    for pair in range(EX // 2):
        add(pair)
    pipeline(vector, matrix)


def outer_two_kernel(
    v_ref, trace_ref, base_ref, part_ref, mean_ref, amp_ref, plane_ref, from_core_ref, from_chip_ref,
    near_ref, far_ref, pin_ref, coefs, lift_ref, wall_ref, smooth_ref, out_ref, mixed, weights_held,
):
    first_span = lax.axis_index("span") == 0
    first_rans = lax.axis_index("rans") == 0
    lane = lanes()
    weights, smooth = fill(weights_held, [lift_ref[...], wall_ref[...]]), smooth_ref[...]
    below, above = from_below(from_core_ref, from_chip_ref), from_above(from_core_ref, from_chip_ref)
    vector, matrix = [], []

    def edge(f):
        return jnp.where(first_rans, inflow_of(mean_ref, amp_ref, plane_ref)(f), below(f))

    def add(pair):
        at = place(pair)
        rows = mixed.at[pair % 2]

        def read(f, r0, r1):
            return v_ref[f, r0:r1, at]

        def store(f, value):
            out_ref[f, :, at] = value.astype(bf16)

        vector.append(
            mix_stream(
                read, lower_pair(v_ref, edge, pair), upper_pair(v_ref, above, pair), coefs, rows, 0
            )
            + mix_sides(
                lambda f, r0, r1: trace_ref[f, r0:r1, at].astype(f32),
                lambda f: near_ref[f, :, pair * CELLS : (pair + 1) * CELLS].astype(f32),
                lambda f: far_ref[f].astype(f32),
                [2 * pair, 2 * pair + 1], coefs, rows, 32, first_span, lane,
            )
            + mix_wall(read, lambda: pin_ref[:, at].astype(f32), rows, 96)
        )
        matrix.append(
            staggered([
                lambda f, _: dot(weights, rows[f]) + part_ref[f, :, at],
                finish(read, lambda f: base_ref[f, :, at], smooth),
                store,
            ])
        )

    for pair in range(EX // 2):
        add(pair)
    pipeline(vector, matrix)


def inflow_of(mean_ref, amp_ref, plane_ref):
    return lambda f: mean_ref[f] + amp_ref[f] * plane_ref[f]


def inflow_kernel(
    held_ref, held_trace_ref, held_pitch_ref, held_span_ref, v_ref, mean_ref, amp_ref,
    plane_ref, near_ref, far_ref, pin_ref, coefs, volume_ref, lift_ref, wall_ref, filter_ref, out_ref,
    out_trace_ref,
    pitch_ref, span_ref, mixed, own, weights_held,
):
    first_span = lax.axis_index("span") == 0
    first_rans = lax.axis_index("rans") == 0
    lane = lanes()

    @pl.when(first_rans)
    def _():
        pick = trace_selector()
        smooth = with_traces(filter_ref[...], pick)
        weights = fill(
            weights_held, [volume_ref[0], volume_ref[1], volume_ref[2], lift_ref[...], wall_ref[...]]
        )

        def read(f, r0, r1):
            return v_ref[f, r0:r1, 0:CELLS]

        def store(f, value):
            out_ref[f] = value[0:64].astype(bf16)
            t = value[64:128]
            out_trace_ref[f] = t.astype(bf16)
            pitch = jnp.where(lane < 32, t[0:16], pltpu.roll(t[16:32], 96, 1))
            pitch_ref[f] = jnp.where(
                (lane & 63) < 32, pitch, held_pitch_ref[f].astype(f32)
            ).astype(bf16)
            span_ref[f] = pack_span(
                held_span_ref[f].astype(f32), t[32:48], t[48:64], 0, first_span, lane
            ).astype(bf16)

        vector = (
            mix_traces(read, pick, own)
            + mix_stream(
                read,
                inflow_of(mean_ref, amp_ref, plane_ref),
                lambda f: v_ref[f, 0:16, CELLS:PAIR].astype(f32),
                coefs, mixed, 192,
            )
            + mix_sides(
                lambda f, r0, r1: own[f, r0:r1].astype(f32),
                lambda f: near_ref[f].astype(f32),
                lambda f: far_ref[f].astype(f32),
                [0], coefs, mixed, 224, first_span, lane,
            )
            + mix_fluxes(read, coefs, mixed)
            + mix_wall(read, lambda: pin_ref[...].astype(f32), mixed, 288)
        )
        matrix = staggered(
            [lambda f, _: dot(weights, mixed[f]), finish(read, None, smooth), store]
        )
        pipeline([vector], [matrix])

    @pl.when(jnp.logical_not(first_rans))
    def _():
        out_ref[...] = held_ref[...]
        out_trace_ref[...] = held_trace_ref[...]
        pitch_ref[...] = held_pitch_ref[...]
        span_ref[...] = held_span_ref[...]


VMEM = pl.BlockSpec(memory_space=pltpu.VMEM)
SMEM = pl.BlockSpec(memory_space=pltpu.SMEM)
PARAMS = pltpu.CompilerParams(vmem_limit_bytes=40 * 2**20)


def shape_of(*dims, dtype=bf16):
    return jax.ShapeDtypeStruct(dims, dtype)


def front(*dims):
    return pl.BlockSpec(dims, lambda i: (0,) * len(dims))


def cost(us):
    return pl.CostEstimate(flops=int(us * 1e8), bytes_accessed=int(us * 3e6), transcendentals=0)


def body(
    solution, volume_ops, flux_jacobian, lift_matrix, filter_matrix, wall_matrix, pinched_map,
    mode_rows, mode_seeds, mode_shape, mean_inflow, eddy_amplitude,
):
    ranks = lax.axis_size("rans")
    eddies, foot = mode_shape.shape[2:]
    plane_rows = mean_inflow.shape[3]
    faces = shape_of(FIELDS, 16, CELLS)
    def slab(z, y, core):
        return 8 * z + 2 * y + core

    columns = ranks // 8
    root_y = [0] + [1] * (columns - 1)
    first_level = [
        [
            (slab(z, [y for y in range(4) if y != root_y[z]][turn], core), slab(z, root_y[z], core))
            for z in range(columns)
            for core in range(2)
        ]
        for turn in range(3)
    ]
    second_level = [
        [
            (slab(z + up, root_y[z + up], core), slab(z, root_y[z], 0))
            for z in range(0, columns, 2)
        ]
        for up, core in ((0, 1), (1, 0), (1, 1))
    ]
    third_level = [[(slab(z, root_y[z], 0), 0)] for z in (2, 6, 4)]

    def gather_sum(value, level, own=None):
        parts = [lax.ppermute(value, "rans", pairs) for pairs in level]
        value = value if own is None else own
        for part in parts:
            value = value + part
        return value

    jacobian = flux_jacobian.transpose(1, 0, 2)
    pins = pinched_map.reshape(1, -1)
    elements = solution.shape[2]
    traces = shape_of(FIELDS, NODES, elements)
    sends = (faces, faces, shape_of(FIELDS, 16, EX // 2 * CELLS), faces)
    swap = [(0, 1), (1, 0)]
    same_chip = [(i, i ^ 1) for i in range(ranks)]
    next_chip = [(a + 1, b + 1) for a, b in same_chip if max(a, b) + 1 < ranks]

    span_scratch = pltpu.VMEM((FIELDS, 16, CELLS), f32)
    plane = pl.pallas_call(
        functools.partial(
            plane_kernel, normalizer=float((plane_rows / (eddies * ranks * foot)) ** 0.5)
        ),
        out_shape=shape_of(FIELDS, 16, CELLS, dtype=f32),
        in_specs=[pl.BlockSpec(memory_space=pltpu.HBM)] * 3,
        out_specs=VMEM,
        scratch_shapes=[
            pltpu.VMEM((foot, eddies), jnp.int32),
            pltpu.VMEM((1, eddies), jnp.int32),
            pltpu.VMEM((foot, eddies), f32),
            pltpu.SemaphoreType.DMA((3,)),
        ],
        compiler_params=pltpu.CompilerParams(vmem_limit_bytes=60 * 2**20),
        cost_estimate=cost(4),
        name="eddy_plane",
    )(mode_rows[0, 0].T, mode_seeds.reshape(1, eddies), mode_shape[0, 0].T)
    held_plane, core, chip, pitch, span = pl.pallas_call(
        pack_kernel,
        out_shape=(shape_of(FIELDS, 16, CELLS, dtype=f32),) + sends,
        in_specs=[VMEM] * 2,
        out_specs=(VMEM,) * 5,
        scratch_shapes=[span_scratch],
        compiler_params=PARAMS,
        cost_estimate=cost(1),
        name="pack_faces",
    )(plane, solution)
    plane = gather_sum(plane, first_level, held_plane)
    near = lax.ppermute(pitch, "pitch", swap)
    plane, chip, core, span = lax.optimization_barrier((plane, chip, core, span))
    plane = gather_sum(plane, second_level)
    from_chip = lax.ppermute(chip, "rans", next_chip)
    core, span, near = lax.optimization_barrier((core, span, near))
    far = lax.ppermute(span, "span", swap)
    from_core = lax.ppermute(core, "rans", same_chip)
    plane, near, far, from_core = lax.optimization_barrier((plane, near, far, from_core))
    plane = gather_sum(plane, third_level)

    phase_one, trace_one, core, chip, pitch, span = pl.pallas_call(
        phase_one_kernel,
        out_shape=(traces, traces) + sends,
        in_specs=[VMEM] * 6 + [SMEM] + [VMEM] * 4,
        out_specs=(VMEM,) * 6,
        scratch_shapes=[
            pltpu.VMEM((2, FIELDS, MIXED, PAIR), bf16),
            pltpu.VMEM((2, FIELDS, NODES, PAIR), bf16),
            pltpu.VMEM((NODES, MIXED), bf16),
            span_scratch,
        ],
        compiler_params=PARAMS,
        cost_estimate=cost(6),
        name="phase_one",
    )(
        solution, from_core, from_chip, near, far, pins, jacobian, volume_ops, lift_matrix, wall_matrix,
        filter_matrix,
    )
    from_core = lax.ppermute(core, "rans", same_chip)
    from_chip = lax.ppermute(chip, "rans", next_chip)
    plane, from_core = lax.optimization_barrier((plane, from_core))

    mean = mean_inflow.reshape(FIELDS, 16, CELLS)
    amplitude = eddy_amplitude.reshape(FIELDS, 16, CELLS)
    layer = front(FIELDS, NODES, CELLS)
    face = front(FIELDS, 16, CELLS)
    phase_one, trace_one, pitch, span = pl.pallas_call(
        inflow_kernel,
        grid=(1,),
        out_shape=(traces, traces, sends[2], sends[3]),
        in_specs=[layer, layer, face, face, front(FIELDS, NODES, PAIR)]
        + [face] * 5
        + [
            front(1, CELLS), SMEM, front(3, NODES, NODES), front(NODES, 96), front(NODES, NODES),
            front(NODES, NODES),
        ],
        out_specs=(layer, layer, face, face),
        scratch_shapes=[
            pltpu.VMEM((FIELDS, MIXED, CELLS), bf16),
            pltpu.VMEM((FIELDS, NODES, CELLS), bf16),
            pltpu.VMEM((NODES, MIXED), bf16),
        ],
        input_output_aliases={0: 0, 1: 1, 2: 2, 3: 3},
        compiler_params=PARAMS,
        cost_estimate=cost(0.1),
        name="inflow_layer",
    )(
        phase_one, trace_one, pitch, span, solution, mean, amplitude, plane, near, far,
        pins, jacobian, volume_ops, lift_matrix, wall_matrix, filter_matrix,
    )
    near = lax.ppermute(pitch, "pitch", swap)
    far = lax.ppermute(span, "span", swap)
    part = pl.pallas_call(
        inner_two_kernel,
        out_shape=shape_of(FIELDS, NODES, elements, dtype=f32),
        in_specs=[VMEM, SMEM, VMEM],
        out_specs=VMEM,
        scratch_shapes=[
            pltpu.VMEM((2, FIELDS, INNER, PAIR), bf16), pltpu.VMEM((NODES, INNER), bf16)
        ],
        compiler_params=PARAMS,
        cost_estimate=cost(0.1),
        name="inner_two",
    )(phase_one, jacobian, volume_ops)
    return pl.pallas_call(
        outer_two_kernel,
        out_shape=traces,
        in_specs=[VMEM] * 12 + [SMEM] + [VMEM] * 3,
        out_specs=VMEM,
        scratch_shapes=[
            pltpu.VMEM((2, FIELDS, MIXED - INNER, PAIR), bf16),
            pltpu.VMEM((NODES, MIXED - INNER), bf16),
        ],
        compiler_params=PARAMS,
        cost_estimate=cost(4),
        name="outer_two",
    )(
        phase_one, trace_one, solution, part, mean, amplitude, plane, from_core, from_chip, near, far,
        pins, jacobian, lift_matrix, wall_matrix, filter_matrix,
    )


def solution(mesh):
    spread = P(None, None, ("rans", "pitch", "span"))
    in_specs = (
        spread,
        P(),
        P(),
        P(),
        P(),
        P(),
        P(("rans", "pitch", "span")),
        P("pitch", "span", "rans", None),
        P("pitch", "span", "rans"),
        P("pitch", "span", "rans", None),
        P("pitch", "span", None, None),
        P("pitch", "span", None, None),
    )
    return jax.shard_map(body, mesh=mesh, in_specs=in_specs, out_specs=spread, check_vma=False)
```

```python
import functools

import jax
import jax.numpy as jnp
from jax import lax
from jax.experimental import pallas as pl
from jax.experimental.pallas import tpu as pltpu
from jax.sharding import PartitionSpec as P

FIELDS = 5
NODES = 64
EX = 12
CELLS = 128
SPAN_CELLS = 32
PAIR = 2 * CELLS
MIXED = 352
INNER = 192
TIME_STEP = 0.4
f32 = jnp.float32
bf16 = jnp.bfloat16


def trace_selector():
    row = lax.broadcasted_iota(jnp.int32, (64, 64), 0)
    node = lax.broadcasted_iota(jnp.int32, (64, 64), 1)
    face, first, second = row >> 4, (row >> 2) & 3, row & 3
    on_pitch = second + jnp.where(face == 1, 12, 0)
    on_span = 4 * second + jnp.where(face == 3, 3, 0)
    source = 16 * first + jnp.where(face < 2, on_pitch, on_span)
    return jnp.where(node == source, 1.0, 0.0).astype(bf16)


def dot(a, b):
    return jnp.dot(a, b, preferred_element_type=f32)


def lanes():
    return lax.broadcasted_iota(jnp.int32, (16, CELLS), 1)


def sum_eddies(rows_ref, seeds_ref, shape_ref, plane_ref, normalizer):
    seeds = seeds_ref[...]
    signs = [(2 * ((seeds >> f) & 1) - 1).astype(f32) for f in range(FIELDS)]
    signs = [jnp.broadcast_to(s, (32, s.shape[1])).astype(bf16) for s in signs]
    eddies = rows_ref.shape[1]
    high_row = lax.broadcasted_iota(jnp.int32, (16, eddies), 0)
    low_row = lax.broadcasted_iota(jnp.int32, (CELLS, eddies), 0)

    def chunk(i, total):
        start = pl.multiple_of(i * 8, 8)
        rows = rows_ref[pl.ds(start, 8), :]
        shapes = shape_ref[pl.ds(start, 8), :]
        for q in range(8):
            row, shape = rows[q : q + 1], shapes[q : q + 1]
            placed = jnp.where((row >> 7) == high_row, shape, 0.0)
            coarse = placed.astype(bf16)
            fine = (placed - coarse.astype(f32)).astype(bf16)
            both = jnp.concatenate([coarse, fine], axis=0)
            signed = jnp.concatenate([both * s for s in signs], axis=0)
            hot = jnp.where((row & 127) == low_row, 1.0, 0.0).astype(bf16)
            total = total + lax.dot_general(
                signed, hot, (((1,), (1,)), ((), ())), preferred_element_type=f32
            )
        return total

    total = lax.fori_loop(
        0, rows_ref.shape[0] // 8, chunk, jnp.zeros((160, CELLS), f32), unroll=True
    )
    for f in range(FIELDS):
        plane_ref[f] = (total[32 * f : 32 * f + 16] + total[32 * f + 16 : 32 * f + 32]) * normalizer


def pack_pitch(traces, lane):
    (low0, high0), (low1, high1) = traces
    return jnp.where(
        lane < 32,
        low0,
        jnp.where(
            lane < 64,
            pltpu.roll(low1, 32, 1),
            jnp.where(lane < 96, pltpu.roll(high0, 96, 1), high1),
        ),
    )


def pack_span(held, low, high, layer, first_span, lane):
    edge = jnp.where(first_span, high, low)
    shift = lax.rem(layer + jnp.where(first_span, 97, 0), 128)
    return jnp.where((lane & 31) == layer, pltpu.roll(edge, shift, 1), held)


def pack_field(f, trace, pair, first_span, lane, pitch_ref, span_held):
    halves = [trace[:, :CELLS], trace[:, CELLS:]]
    packed = pack_pitch([(h[0:16], h[16:32]) for h in halves], lane)
    pitch_ref[f, :, pair * CELLS : (pair + 1) * CELLS] = packed.astype(bf16)
    held = span_held[f]
    for h in range(2):
        held = pack_span(held, halves[h][32:48], halves[h][48:64], 2 * pair + h, first_span, lane)
    span_held[f] = held


def is_even():
    return (lax.axis_index("rans") & 1) == 0


def store_stream(up, down, near_chip_ref, far_chip_ref):
    even = is_even()
    near_chip_ref[...] = jnp.where(even, up, down)
    far_chip_ref[...] = jnp.where(even, down, up)


def from_below(near_chip_ref, far_chip_ref):
    even = is_even()
    return lambda f: jnp.where(even, far_chip_ref[f].astype(f32), near_chip_ref[f].astype(f32))


def from_above(near_chip_ref, far_chip_ref):
    even = is_even()
    return lambda f: jnp.where(even, near_chip_ref[f].astype(f32), far_chip_ref[f].astype(f32))


def plane_kernel(
    rows_hbm, seeds_hbm, shape_hbm, plane_ref, rows_ref, seeds_ref, shape_ref, sems, *, normalizer
):
    copies = [
        pltpu.make_async_copy(source, target, sems.at[i])
        for i, (source, target) in enumerate([
            (rows_hbm, rows_ref), (seeds_hbm, seeds_ref), (shape_hbm, shape_ref)
        ])
    ]
    for copy in copies:
        copy.start()
    for copy in copies:
        copy.wait()
    sum_eddies(rows_ref, seeds_ref, shape_ref, plane_ref, normalizer)


def pack_kernel(
    plane_ref, v_ref, held_plane_ref, core_ref, chip_ref, pitch_ref, span_ref, span_held
):
    first_span = lax.axis_index("span") == 0
    lane = lanes()
    pick = trace_selector()
    held_plane_ref[...] = plane_ref[...]
    span_held[...] = jnp.zeros_like(span_held)
    for pair in range(EX // 2):
        at = slice(pair * PAIR, (pair + 1) * PAIR)
        for f in range(FIELDS):
            pack_field(
                f, dot(pick, v_ref[f, :, at]), pair, first_span, lane, pitch_ref, span_held
            )
    span_ref[...] = span_held[...].astype(bf16)
    store_stream(
        v_ref[:, 48:64, (EX - 1) * CELLS :], v_ref[:, 0:16, 0:CELLS], core_ref, chip_ref
    )


def mix(row, arrays):
    total = row[0] * arrays[0]
    for g in range(1, FIELDS):
        total = total + row[g] * arrays[g]
    return total


def flux_row(jacobian, d, f):
    return [jacobian[f, d, g] for g in range(FIELDS)]


def face_row(jacobian, t, f):
    half = 0.5 * (1.0 if t % 2 else -1.0)
    row = [half * jacobian[f, t // 2, g] for g in range(FIELDS)]
    row[f] = row[f] - 0.5
    return row


def fill(weights, parts):
    column = 0
    for part in parts:
        weights[:, column : column + part.shape[1]] = part
        column += part.shape[1]
    return weights[...]


def mix_fluxes(read, coefs, mixed):
    def rows_step(r):
        def run():
            rows = [read(f, r, r + 16).astype(f32) for f in range(FIELDS)]
            for d in range(3):
                for f in range(FIELDS):
                    mixed[f, 64 * d + r : 64 * d + r + 16, :] = mix(
                        flux_row(coefs, d, f), rows
                    ).astype(bf16)

        return run

    return [rows_step(r) for r in range(0, NODES, 16)]


def write_jumps(t, jumps, coefs, mixed, first_row):
    for f in range(FIELDS):
        mixed[f, first_row : first_row + 16, :] = mix(face_row(coefs, t, f), jumps).astype(bf16)


def mix_stream(read, lower, upper, coefs, mixed, row):
    def low():
        jumps = [lower(f) - read(f, 0, 16).astype(f32) for f in range(FIELDS)]
        write_jumps(0, jumps, coefs, mixed, row)

    def high():
        jumps = [upper(f) - read(f, 48, 64).astype(f32) for f in range(FIELDS)]
        write_jumps(1, jumps, coefs, mixed, row + 16)

    return [low, high]


def mix_sides(trace, pitch, span, layers, coefs, mixed, row, first_span, lane):
    def halves(f, r):
        own = trace(f, r, r + 16)
        return [own[:, h * CELLS : (h + 1) * CELLS] for h in range(len(layers))]

    def join(parts):
        return parts[0] if len(parts) == 1 else jnp.concatenate(parts, axis=1)

    def pitch_low():
        jumps = []
        for f in range(FIELDS):
            near, low, high = pitch(f), halves(f, 0), halves(f, 16)
            jumps.append(join([
                jnp.where(
                    lane < 32, pltpu.roll(near, 64 if h == 0 else 32, 1), pltpu.roll(high[h], 32, 1)
                ) - low[h]
                for h in range(len(layers))
            ]))
        write_jumps(2, jumps, coefs, mixed, row)

    def pitch_high():
        jumps = []
        for f in range(FIELDS):
            near, low, high = pitch(f), halves(f, 0), halves(f, 16)
            jumps.append(join([
                jnp.where(
                    lane >= 96, pltpu.roll(near, 96 if h == 0 else 64, 1), pltpu.roll(low[h], 96, 1)
                ) - high[h]
                for h in range(len(layers))
            ]))
        write_jumps(3, jumps, coefs, mixed, row + 16)

    def arrived(f, layer):
        return pltpu.roll(span(f), lax.rem(jnp.where(first_span, 31, 128) - layer, 128), 1)

    def span_low():
        jumps = []
        for f in range(FIELDS):
            low, high = halves(f, 32), halves(f, 48)
            jumps.append(join([
                jnp.where(
                    (lane & 31) == 0,
                    jnp.where(first_span, low[h], arrived(f, layer)),
                    pltpu.roll(high[h], 1, 1),
                ) - low[h]
                for h, layer in enumerate(layers)
            ]))
        write_jumps(4, jumps, coefs, mixed, row + 32)

    def span_high():
        jumps = []
        for f in range(FIELDS):
            low, high = halves(f, 32), halves(f, 48)
            jumps.append(join([
                jnp.where(
                    (lane & 31) == 31,
                    jnp.where(first_span, arrived(f, layer), high[h]),
                    pltpu.roll(low[h], 127, 1),
                ) - high[h]
                for h, layer in enumerate(layers)
            ]))
        write_jumps(5, jumps, coefs, mixed, row + 48)

    return [pitch_low, pitch_high, span_low, span_high]


def mix_wall(read, pinned, mixed, row):
    def run():
        for f in range(FIELDS):
            mixed[f, row : row + 64, :] = (read(f, 0, 64).astype(f32) * pinned()).astype(bf16)

    return [run]


def staggered(stages):
    held = [None] * FIELDS
    steps = []

    def step(stage, f):
        def run():
            held[f] = stage(f, held[f])

        return run

    for turn in range(FIELDS + len(stages) - 1):
        for k, stage in enumerate(stages):
            if 0 <= turn - k < FIELDS:
                steps.append(step(stage, turn - k))
    return steps


def interleave(first, second):
    count = max(len(first), len(second))
    for i in range(count):
        for steps in (first, second):
            for step in steps[i * len(steps) // count : (i + 1) * len(steps) // count]:
                step()


def pipeline(vector, matrix):
    for step in vector[0]:
        step()
    for p in range(len(matrix)):
        interleave(matrix[p], vector[p + 1] if p + 1 < len(vector) else [])


def finish(read, base, smooth):
    def trial(f, rate):
        v = read(f, 0, 64).astype(f32)
        if base is None:
            now = v - TIME_STEP * rate
        else:
            now = 0.5 * (base(f).astype(f32) + v - TIME_STEP * rate)
        return dot(smooth, now.astype(bf16))

    return trial


def with_traces(filter_matrix, pick):
    return jnp.concatenate([filter_matrix, dot(pick, filter_matrix).astype(bf16)], axis=0)


def mix_traces(read, pick, own):
    def run():
        for f in range(FIELDS):
            own[f] = dot(pick, read(f, 0, 64)).astype(bf16)

    return [run]


def place(pair):
    return slice(pair * PAIR, (pair + 1) * PAIR)


def lower_pair(v_ref, edge, pair):
    def lower(f):
        if pair:
            return v_ref[f, 48:64, pair * PAIR - CELLS : (pair + 1) * PAIR - CELLS].astype(f32)
        return jnp.concatenate([edge(f), v_ref[f, 48:64, 0:CELLS].astype(f32)], axis=1)

    return lower


def upper_pair(v_ref, above, pair):
    first = pair * PAIR + CELLS
    last_rans = lax.axis_index("rans") == lax.axis_size("rans") - 1

    def upper(f):
        if pair < EX // 2 - 1:
            return v_ref[f, 0:16, first : first + PAIR].astype(f32)
        edge = jnp.where(
            last_rans, v_ref[f, 48:64, first : first + CELLS].astype(f32), above(f)
        )
        return jnp.concatenate([v_ref[f, 0:16, first : first + CELLS].astype(f32), edge], axis=1)

    return upper


def phase_one_kernel(
    v_ref, from_core_ref, from_chip_ref, near_ref, far_ref, pin_ref, coefs, volume_ref, lift_ref,
    wall_ref, filter_ref,
    out_ref, out_trace_ref, core_ref, chip_ref, pitch_ref, span_ref, mixed, own, weights_held,
    span_held,
):
    first_span = lax.axis_index("span") == 0
    lane = lanes()
    pick = trace_selector()
    smooth = with_traces(filter_ref[...], pick)
    weights = fill(
        weights_held, [volume_ref[0], volume_ref[1], volume_ref[2], lift_ref[...], wall_ref[...]]
    )
    span_held[...] = jnp.zeros_like(span_held)
    below, above = from_below(from_core_ref, from_chip_ref), from_above(from_core_ref, from_chip_ref)
    vector, matrix = [], []

    def add(pair):
        at = place(pair)
        rows, held = mixed.at[pair % 2], own.at[pair % 2]

        def read(f, r0, r1):
            return v_ref[f, r0:r1, at]

        def store(f, value):
            out_ref[f, :, at] = value[0:64].astype(bf16)
            trace = value[64:128]
            out_trace_ref[f, :, at] = trace.astype(bf16)
            pack_field(f, trace, pair, first_span, lane, pitch_ref, span_held)

        vector.append(
            mix_traces(read, pick, held)
            + mix_fluxes(read, coefs, rows)
            + mix_stream(
                read,
                lower_pair(v_ref, below, pair),
                upper_pair(v_ref, above, pair),
                coefs, rows, 192,
            )
            + mix_sides(
                lambda f, r0, r1: held[f, r0:r1].astype(f32),
                lambda f: near_ref[f, :, pair * CELLS : (pair + 1) * CELLS].astype(f32),
                lambda f: far_ref[f].astype(f32),
                [2 * pair, 2 * pair + 1], coefs, rows, 224, first_span, lane,
            )
            + mix_wall(read, lambda: pin_ref[:, at].astype(f32), rows, 288)
        )
        matrix.append(
            staggered([lambda f, _: dot(weights, rows[f]), finish(read, None, smooth), store])
        )

    for pair in range(EX // 2):
        add(pair)
    pipeline(vector, matrix)
    span_ref[...] = span_held[...].astype(bf16)
    store_stream(
        out_ref[:, 48:64, (EX - 1) * CELLS :], out_ref[:, 0:16, 0:CELLS], core_ref, chip_ref
    )


def inner_two_kernel(v_ref, coefs, volume_ref, part_ref, mixed, weights_held):
    weights = fill(weights_held, [volume_ref[d] for d in range(3)])
    vector, matrix = [], []

    def add(pair):
        at = place(pair)
        rows = mixed.at[pair % 2]

        def store(f, value):
            part_ref[f, :, at] = value

        vector.append(mix_fluxes(lambda f, r0, r1: v_ref[f, r0:r1, at], coefs, rows))
        matrix.append(staggered([lambda f, _: dot(weights, rows[f]), store]))

    for pair in range(EX // 2):
        add(pair)
    pipeline(vector, matrix)


def outer_two_kernel(
    v_ref, trace_ref, base_ref, part_ref, mean_ref, amp_ref, plane_ref, from_core_ref, from_chip_ref,
    near_ref, far_ref, pin_ref, coefs, lift_ref, wall_ref, smooth_ref, out_ref, mixed, weights_held,
):
    first_span = lax.axis_index("span") == 0
    first_rans = lax.axis_index("rans") == 0
    lane = lanes()
    weights, smooth = fill(weights_held, [lift_ref[...], wall_ref[...]]), smooth_ref[...]
    below, above = from_below(from_core_ref, from_chip_ref), from_above(from_core_ref, from_chip_ref)
    vector, matrix = [], []

    def edge(f):
        return jnp.where(first_rans, inflow_of(mean_ref, amp_ref, plane_ref)(f), below(f))

    def add(pair):
        at = place(pair)
        rows = mixed.at[pair % 2]

        def read(f, r0, r1):
            return v_ref[f, r0:r1, at]

        def store(f, value):
            out_ref[f, :, at] = value.astype(bf16)

        vector.append(
            mix_stream(
                read, lower_pair(v_ref, edge, pair), upper_pair(v_ref, above, pair), coefs, rows, 0
            )
            + mix_sides(
                lambda f, r0, r1: trace_ref[f, r0:r1, at].astype(f32),
                lambda f: near_ref[f, :, pair * CELLS : (pair + 1) * CELLS].astype(f32),
                lambda f: far_ref[f].astype(f32),
                [2 * pair, 2 * pair + 1], coefs, rows, 32, first_span, lane,
            )
            + mix_wall(read, lambda: pin_ref[:, at].astype(f32), rows, 96)
        )
        matrix.append(
            staggered([
                lambda f, _: dot(weights, rows[f]) + part_ref[f, :, at],
                finish(read, lambda f: base_ref[f, :, at], smooth),
                store,
            ])
        )

    for pair in range(EX // 2):
        add(pair)
    pipeline(vector, matrix)


def inflow_of(mean_ref, amp_ref, plane_ref):
    return lambda f: mean_ref[f] + amp_ref[f] * plane_ref[f]


def inflow_kernel(
    held_any, held_trace_any, held_pitch_any, held_span_any, v_ref, mean_ref, amp_ref, plane_ref,
    near_ref, far_ref, pin_ref, coefs, volume_ref, lift_ref, wall_ref, filter_ref, out_any,
    out_trace_any, pitch_any, span_any, mixed, own, weights_held, edge, edge_trace, edge_pitch,
    edge_span, sems,
):
    first_span = lax.axis_index("span") == 0
    lane = lanes()
    layer = slice(0, CELLS)

    @pl.when(lax.axis_index("rans") == 0)
    def _():
        loads = [
            pltpu.make_async_copy(held_pitch_any.at[:, :, layer], edge_pitch, sems.at[0]),
            pltpu.make_async_copy(held_span_any, edge_span, sems.at[1]),
        ]
        for copy in loads:
            copy.start()
        pick = trace_selector()
        smooth = with_traces(filter_ref[...], pick)
        weights = fill(
            weights_held, [volume_ref[0], volume_ref[1], volume_ref[2], lift_ref[...], wall_ref[...]]
        )

        def read(f, r0, r1):
            return v_ref[f, r0:r1, layer]

        def store(f, value):
            edge[f] = value[0:64].astype(bf16)
            t = value[64:128]
            edge_trace[f] = t.astype(bf16)
            pitch = jnp.where(lane < 32, t[0:16], pltpu.roll(t[16:32], 96, 1))
            edge_pitch[f] = jnp.where(
                (lane & 63) < 32, pitch, edge_pitch[f].astype(f32)
            ).astype(bf16)
            edge_span[f] = pack_span(
                edge_span[f].astype(f32), t[32:48], t[48:64], 0, first_span, lane
            ).astype(bf16)

        vector = (
            mix_traces(read, pick, own)
            + mix_stream(
                read,
                inflow_of(mean_ref, amp_ref, plane_ref),
                lambda f: v_ref[f, 0:16, CELLS:PAIR].astype(f32),
                coefs, mixed, 192,
            )
            + mix_sides(
                lambda f, r0, r1: own[f, r0:r1].astype(f32),
                lambda f: near_ref[f, :, layer].astype(f32),
                lambda f: far_ref[f].astype(f32),
                [0], coefs, mixed, 224, first_span, lane,
            )
            + mix_fluxes(read, coefs, mixed)
            + mix_wall(read, lambda: pin_ref[:, layer].astype(f32), mixed, 288)
        )
        for step in vector:
            step()
        for copy in loads:
            copy.wait()
        for step in staggered(
            [lambda f, _: dot(weights, mixed[f]), finish(read, None, smooth), store]
        ):
            step()
        stores = [
            pltpu.make_async_copy(edge, out_any.at[:, :, layer], sems.at[2]),
            pltpu.make_async_copy(edge_trace, out_trace_any.at[:, :, layer], sems.at[3]),
            pltpu.make_async_copy(edge_pitch, pitch_any.at[:, :, layer], sems.at[4]),
            pltpu.make_async_copy(edge_span, span_any, sems.at[5]),
        ]
        for copy in stores:
            copy.start()
        for copy in stores:
            copy.wait()


VMEM = pl.BlockSpec(memory_space=pltpu.VMEM)
SMEM = pl.BlockSpec(memory_space=pltpu.SMEM)
PARAMS = pltpu.CompilerParams(vmem_limit_bytes=40 * 2**20)


def shape_of(*dims, dtype=bf16):
    return jax.ShapeDtypeStruct(dims, dtype)


def cost(us):
    return pl.CostEstimate(flops=int(us * 1e8), bytes_accessed=int(us * 3e6), transcendentals=0)


def body(
    solution, volume_ops, flux_jacobian, lift_matrix, filter_matrix, wall_matrix, pinched_map,
    mode_rows, mode_seeds, mode_shape, mean_inflow, eddy_amplitude,
):
    ranks = lax.axis_size("rans")
    eddies, foot = mode_shape.shape[2:]
    plane_rows = mean_inflow.shape[3]
    faces = shape_of(FIELDS, 16, CELLS)
    def slab(z, y, core):
        return 8 * z + 2 * y + core

    columns = ranks // 8
    root_y = [0] + [1] * (columns - 1)
    first_level = [
        [
            (slab(z, [y for y in range(4) if y != root_y[z]][turn], core), slab(z, root_y[z], core))
            for z in range(columns)
            for core in range(2)
        ]
        for turn in range(3)
    ]
    second_level = [
        [
            (slab(z + up, root_y[z + up], core), slab(z, root_y[z], 0))
            for z in range(0, columns, 2)
        ]
        for up, core in ((0, 1), (1, 0), (1, 1))
    ]
    third_level = [[(slab(z, root_y[z], 0), 0)] for z in (2, 6, 4)]

    def gather_sum(value, level, own=None):
        parts = [lax.ppermute(value, "rans", pairs) for pairs in level]
        value = value if own is None else own
        for part in parts:
            value = value + part
        return value

    jacobian = flux_jacobian.transpose(1, 0, 2)
    pins = pinched_map.reshape(1, -1)
    elements = solution.shape[2]
    traces = shape_of(FIELDS, NODES, elements)
    sends = (faces, faces, shape_of(FIELDS, 16, EX // 2 * CELLS), faces)
    swap = [(0, 1), (1, 0)]
    same_chip = [(i, i ^ 1) for i in range(ranks)]
    next_chip = [(a + 1, b + 1) for a, b in same_chip if max(a, b) + 1 < ranks]

    span_scratch = pltpu.VMEM((FIELDS, 16, CELLS), f32)
    plane = pl.pallas_call(
        functools.partial(
            plane_kernel, normalizer=float((plane_rows / (eddies * ranks * foot)) ** 0.5)
        ),
        out_shape=shape_of(FIELDS, 16, CELLS, dtype=f32),
        in_specs=[pl.BlockSpec(memory_space=pltpu.HBM)] * 3,
        out_specs=VMEM,
        scratch_shapes=[
            pltpu.VMEM((foot, eddies), jnp.int32),
            pltpu.VMEM((1, eddies), jnp.int32),
            pltpu.VMEM((foot, eddies), f32),
            pltpu.SemaphoreType.DMA((3,)),
        ],
        compiler_params=pltpu.CompilerParams(vmem_limit_bytes=60 * 2**20),
        cost_estimate=cost(4),
        name="eddy_plane",
    )(mode_rows[0, 0].T, mode_seeds.reshape(1, eddies), mode_shape[0, 0].T)
    held_plane, core, chip, pitch, span = pl.pallas_call(
        pack_kernel,
        out_shape=(shape_of(FIELDS, 16, CELLS, dtype=f32),) + sends,
        in_specs=[VMEM] * 2,
        out_specs=(VMEM,) * 5,
        scratch_shapes=[span_scratch],
        compiler_params=PARAMS,
        cost_estimate=cost(1),
        name="pack_faces",
    )(plane, solution)
    plane = gather_sum(plane, first_level, held_plane)
    near = lax.ppermute(pitch, "pitch", swap)
    plane, chip, core, span = lax.optimization_barrier((plane, chip, core, span))
    plane = gather_sum(plane, second_level)
    from_chip = lax.ppermute(chip, "rans", next_chip)
    core, span, near = lax.optimization_barrier((core, span, near))
    far = lax.ppermute(span, "span", swap)
    from_core = lax.ppermute(core, "rans", same_chip)
    plane, near, far, from_core = lax.optimization_barrier((plane, near, far, from_core))
    plane = gather_sum(plane, third_level)

    phase_one, trace_one, core, chip, pitch, span = pl.pallas_call(
        phase_one_kernel,
        out_shape=(traces, traces) + sends,
        in_specs=[VMEM] * 6 + [SMEM] + [VMEM] * 4,
        out_specs=(VMEM,) * 6,
        scratch_shapes=[
            pltpu.VMEM((2, FIELDS, MIXED, PAIR), bf16),
            pltpu.VMEM((2, FIELDS, NODES, PAIR), bf16),
            pltpu.VMEM((NODES, MIXED), bf16),
            span_scratch,
        ],
        compiler_params=PARAMS,
        cost_estimate=cost(6),
        name="phase_one",
    )(
        solution, from_core, from_chip, near, far, pins, jacobian, volume_ops, lift_matrix, wall_matrix,
        filter_matrix,
    )
    from_core = lax.ppermute(core, "rans", same_chip)
    from_chip = lax.ppermute(chip, "rans", next_chip)
    plane, from_core = lax.optimization_barrier((plane, from_core))

    mean = mean_inflow.reshape(FIELDS, 16, CELLS)
    amplitude = eddy_amplitude.reshape(FIELDS, 16, CELLS)
    anywhere = pl.BlockSpec(memory_space=pl.ANY)
    phase_one, trace_one, pitch, span = pl.pallas_call(
        inflow_kernel,
        out_shape=(traces, traces, sends[2], sends[3]),
        in_specs=[anywhere] * 4 + [VMEM] * 7 + [SMEM] + [VMEM] * 4,
        out_specs=(anywhere,) * 4,
        scratch_shapes=[
            pltpu.VMEM((FIELDS, MIXED, CELLS), bf16),
            pltpu.VMEM((FIELDS, NODES, CELLS), bf16),
            pltpu.VMEM((NODES, MIXED), bf16),
            pltpu.VMEM((FIELDS, NODES, CELLS), bf16),
            pltpu.VMEM((FIELDS, NODES, CELLS), bf16),
            pltpu.VMEM((FIELDS, 16, CELLS), bf16),
            pltpu.VMEM((FIELDS, 16, CELLS), bf16),
            pltpu.SemaphoreType.DMA((6,)),
        ],
        input_output_aliases={0: 0, 1: 1, 2: 2, 3: 3},
        compiler_params=PARAMS,
        cost_estimate=cost(0.1),
        name="inflow_layer",
    )(
        phase_one, trace_one, pitch, span, solution, mean, amplitude, plane, near, far, pins,
        jacobian, volume_ops, lift_matrix, wall_matrix, filter_matrix,
    )
    near = lax.ppermute(pitch, "pitch", swap)
    far = lax.ppermute(span, "span", swap)
    part = pl.pallas_call(
        inner_two_kernel,
        out_shape=shape_of(FIELDS, NODES, elements, dtype=f32),
        in_specs=[VMEM, SMEM, VMEM],
        out_specs=VMEM,
        scratch_shapes=[
            pltpu.VMEM((2, FIELDS, INNER, PAIR), bf16), pltpu.VMEM((NODES, INNER), bf16)
        ],
        compiler_params=PARAMS,
        cost_estimate=cost(0.1),
        name="inner_two",
    )(phase_one, jacobian, volume_ops)
    return pl.pallas_call(
        outer_two_kernel,
        out_shape=traces,
        in_specs=[VMEM] * 12 + [SMEM] + [VMEM] * 3,
        out_specs=VMEM,
        scratch_shapes=[
            pltpu.VMEM((2, FIELDS, MIXED - INNER, PAIR), bf16),
            pltpu.VMEM((NODES, MIXED - INNER), bf16),
        ],
        compiler_params=PARAMS,
        cost_estimate=cost(4),
        name="outer_two",
    )(
        phase_one, trace_one, solution, part, mean, amplitude, plane, from_core, from_chip, near, far,
        pins, jacobian, lift_matrix, wall_matrix, filter_matrix,
    )


def solution(mesh):
    spread = P(None, None, ("rans", "pitch", "span"))
    in_specs = (
        spread,
        P(),
        P(),
        P(),
        P(),
        P(),
        P(("rans", "pitch", "span")),
        P("pitch", "span", "rans", None),
        P("pitch", "span", "rans"),
        P("pitch", "span", "rans", None),
        P("pitch", "span", None, None),
        P("pitch", "span", None, None),
    )
    return jax.shard_map(body, mesh=mesh, in_specs=in_specs, out_specs=spread, check_vma=False)
```

```python
import functools

import jax
import jax.numpy as jnp
from jax import lax
from jax.experimental import pallas as pl
from jax.experimental.pallas import tpu as pltpu
from jax.sharding import PartitionSpec as P

FIELDS = 5
NODES = 64
EX = 12
CELLS = 128
SPAN_CELLS = 32
PAIR = 2 * CELLS
MIXED = 352
INNER = 192
TIME_STEP = 0.4
f32 = jnp.float32
bf16 = jnp.bfloat16


def trace_selector():
    row = lax.broadcasted_iota(jnp.int32, (64, 64), 0)
    node = lax.broadcasted_iota(jnp.int32, (64, 64), 1)
    face, first, second = row >> 4, (row >> 2) & 3, row & 3
    on_pitch = second + jnp.where(face == 1, 12, 0)
    on_span = 4 * second + jnp.where(face == 3, 3, 0)
    source = 16 * first + jnp.where(face < 2, on_pitch, on_span)
    return jnp.where(node == source, 1.0, 0.0).astype(bf16)


def dot(a, b):
    return jnp.dot(a, b, preferred_element_type=f32)


def lanes():
    return lax.broadcasted_iota(jnp.int32, (16, CELLS), 1)


def sum_eddies(rows_ref, seeds_ref, shape_ref, plane_ref, normalizer):
    seeds = seeds_ref[...]
    signs = [(2 * ((seeds >> f) & 1) - 1).astype(f32) for f in range(FIELDS)]
    signs = [jnp.broadcast_to(s, (32, s.shape[1])).astype(bf16) for s in signs]
    eddies = rows_ref.shape[1]
    high_row = lax.broadcasted_iota(jnp.int32, (16, eddies), 0)
    low_row = lax.broadcasted_iota(jnp.int32, (CELLS, eddies), 0)

    def chunk(i, total):
        start = pl.multiple_of(i * 8, 8)
        rows = rows_ref[pl.ds(start, 8), :]
        shapes = shape_ref[pl.ds(start, 8), :]
        for q in range(8):
            row, shape = rows[q : q + 1], shapes[q : q + 1]
            placed = jnp.where((row >> 7) == high_row, shape, 0.0)
            coarse = placed.astype(bf16)
            fine = (placed - coarse.astype(f32)).astype(bf16)
            both = jnp.concatenate([coarse, fine], axis=0)
            signed = jnp.concatenate([both * s for s in signs], axis=0)
            hot = jnp.where((row & 127) == low_row, 1.0, 0.0).astype(bf16)
            total = total + lax.dot_general(
                signed, hot, (((1,), (1,)), ((), ())), preferred_element_type=f32
            )
        return total

    total = lax.fori_loop(
        0, rows_ref.shape[0] // 8, chunk, jnp.zeros((160, CELLS), f32), unroll=True
    )
    for f in range(FIELDS):
        plane_ref[f] = (total[32 * f : 32 * f + 16] + total[32 * f + 16 : 32 * f + 32]) * normalizer


def pack_pitch(traces, lane):
    (low0, high0), (low1, high1) = traces
    return jnp.where(
        lane < 32,
        low0,
        jnp.where(
            lane < 64,
            pltpu.roll(low1, 32, 1),
            jnp.where(lane < 96, pltpu.roll(high0, 96, 1), high1),
        ),
    )


def pack_span(held, low, high, layer, first_span, lane):
    edge = jnp.where(first_span, high, low)
    shift = lax.rem(layer + jnp.where(first_span, 97, 0), 128)
    return jnp.where((lane & 31) == layer, pltpu.roll(edge, shift, 1), held)


def pack_field(f, trace, pair, first_span, lane, pitch_ref, span_held):
    halves = [trace[:, :CELLS], trace[:, CELLS:]]
    packed = pack_pitch([(h[0:16], h[16:32]) for h in halves], lane)
    pitch_ref[f, :, pair * CELLS : (pair + 1) * CELLS] = packed.astype(bf16)
    held = span_held[f]
    for h in range(2):
        held = pack_span(held, halves[h][32:48], halves[h][48:64], 2 * pair + h, first_span, lane)
    span_held[f] = held


def is_even():
    return (lax.axis_index("rans") & 1) == 0


def store_stream(up, down, near_chip_ref, far_chip_ref):
    even = is_even()
    near_chip_ref[...] = jnp.where(even, up, down)
    far_chip_ref[...] = jnp.where(even, down, up)


def from_below(near_chip_ref, far_chip_ref):
    even = is_even()
    return lambda f: jnp.where(even, far_chip_ref[f].astype(f32), near_chip_ref[f].astype(f32))


def from_above(near_chip_ref, far_chip_ref):
    even = is_even()
    return lambda f: jnp.where(even, near_chip_ref[f].astype(f32), far_chip_ref[f].astype(f32))


def plane_kernel(
    rows_hbm, seeds_hbm, shape_hbm, plane_ref, rows_ref, seeds_ref, shape_ref, sems, *, normalizer
):
    copies = [
        pltpu.make_async_copy(source, target, sems.at[i])
        for i, (source, target) in enumerate([
            (rows_hbm, rows_ref), (seeds_hbm, seeds_ref), (shape_hbm, shape_ref)
        ])
    ]
    for copy in copies:
        copy.start()
    for copy in copies:
        copy.wait()
    sum_eddies(rows_ref, seeds_ref, shape_ref, plane_ref, normalizer)


def pack_kernel(
    plane_ref, v_ref, held_plane_ref, core_ref, chip_ref, pitch_ref, span_ref, span_held
):
    first_span = lax.axis_index("span") == 0
    lane = lanes()
    pick = trace_selector()
    held_plane_ref[...] = plane_ref[...]
    span_held[...] = jnp.zeros_like(span_held)
    for pair in range(EX // 2):
        at = slice(pair * PAIR, (pair + 1) * PAIR)
        for f in range(FIELDS):
            pack_field(
                f, dot(pick, v_ref[f, :, at]), pair, first_span, lane, pitch_ref, span_held
            )
    span_ref[...] = span_held[...].astype(bf16)
    store_stream(
        v_ref[:, 48:64, (EX - 1) * CELLS :], v_ref[:, 0:16, 0:CELLS], core_ref, chip_ref
    )


def mix(row, arrays):
    total = row[0] * arrays[0]
    for g in range(1, FIELDS):
        total = total + row[g] * arrays[g]
    return total


def flux_row(jacobian, d, f):
    return [jacobian[f, d, g] for g in range(FIELDS)]


def face_row(jacobian, t, f):
    half = 0.5 * (1.0 if t % 2 else -1.0)
    row = [half * jacobian[f, t // 2, g] for g in range(FIELDS)]
    row[f] = row[f] - 0.5
    return row


def fill(weights, parts):
    column = 0
    for part in parts:
        weights[:, column : column + part.shape[1]] = part
        column += part.shape[1]
    return weights[...]


def mix_fluxes(read, coefs, mixed):
    def rows_step(r):
        def run():
            rows = [read(f, r, r + 16).astype(f32) for f in range(FIELDS)]
            for d in range(3):
                for f in range(FIELDS):
                    mixed[f, 64 * d + r : 64 * d + r + 16, :] = mix(
                        flux_row(coefs, d, f), rows
                    ).astype(bf16)

        return run

    return [rows_step(r) for r in range(0, NODES, 16)]


def write_jumps(t, jumps, coefs, mixed, first_row):
    for f in range(FIELDS):
        mixed[f, first_row : first_row + 16, :] = mix(face_row(coefs, t, f), jumps).astype(bf16)


def mix_stream(read, lower, upper, coefs, mixed, row):
    def low():
        jumps = [lower(f) - read(f, 0, 16).astype(f32) for f in range(FIELDS)]
        write_jumps(0, jumps, coefs, mixed, row)

    def high():
        jumps = [upper(f) - read(f, 48, 64).astype(f32) for f in range(FIELDS)]
        write_jumps(1, jumps, coefs, mixed, row + 16)

    return [low, high]


def mix_sides(trace, pitch, span, layers, coefs, mixed, row, first_span, lane):
    def halves(f, r):
        own = trace(f, r, r + 16)
        return [own[:, h * CELLS : (h + 1) * CELLS] for h in range(len(layers))]

    def join(parts):
        return parts[0] if len(parts) == 1 else jnp.concatenate(parts, axis=1)

    def pitch_low():
        jumps = []
        for f in range(FIELDS):
            near, low, high = pitch(f), halves(f, 0), halves(f, 16)
            jumps.append(join([
                jnp.where(
                    lane < 32, pltpu.roll(near, 64 if h == 0 else 32, 1), pltpu.roll(high[h], 32, 1)
                ) - low[h]
                for h in range(len(layers))
            ]))
        write_jumps(2, jumps, coefs, mixed, row)

    def pitch_high():
        jumps = []
        for f in range(FIELDS):
            near, low, high = pitch(f), halves(f, 0), halves(f, 16)
            jumps.append(join([
                jnp.where(
                    lane >= 96, pltpu.roll(near, 96 if h == 0 else 64, 1), pltpu.roll(low[h], 96, 1)
                ) - high[h]
                for h in range(len(layers))
            ]))
        write_jumps(3, jumps, coefs, mixed, row + 16)

    def arrived(f, layer):
        return pltpu.roll(span(f), lax.rem(jnp.where(first_span, 31, 128) - layer, 128), 1)

    def span_low():
        jumps = []
        for f in range(FIELDS):
            low, high = halves(f, 32), halves(f, 48)
            jumps.append(join([
                jnp.where(
                    (lane & 31) == 0,
                    jnp.where(first_span, low[h], arrived(f, layer)),
                    pltpu.roll(high[h], 1, 1),
                ) - low[h]
                for h, layer in enumerate(layers)
            ]))
        write_jumps(4, jumps, coefs, mixed, row + 32)

    def span_high():
        jumps = []
        for f in range(FIELDS):
            low, high = halves(f, 32), halves(f, 48)
            jumps.append(join([
                jnp.where(
                    (lane & 31) == 31,
                    jnp.where(first_span, arrived(f, layer), high[h]),
                    pltpu.roll(low[h], 127, 1),
                ) - high[h]
                for h, layer in enumerate(layers)
            ]))
        write_jumps(5, jumps, coefs, mixed, row + 48)

    return [pitch_low, pitch_high, span_low, span_high]


def mix_wall(read, pinned, mixed, row):
    def run():
        for f in range(FIELDS):
            mixed[f, row : row + 64, :] = (read(f, 0, 64).astype(f32) * pinned()).astype(bf16)

    return [run]


def staggered(stages):
    held = [None] * FIELDS
    steps = []

    def step(stage, f):
        def run():
            held[f] = stage(f, held[f])

        return run

    for turn in range(FIELDS + len(stages) - 1):
        for k, stage in enumerate(stages):
            if 0 <= turn - k < FIELDS:
                steps.append(step(stage, turn - k))
    return steps


def interleave(first, second):
    count = max(len(first), len(second))
    for i in range(count):
        for steps in (first, second):
            for step in steps[i * len(steps) // count : (i + 1) * len(steps) // count]:
                step()


def pipeline(vector, matrix):
    for step in vector[0]:
        step()
    for p in range(len(matrix)):
        interleave(matrix[p], vector[p + 1] if p + 1 < len(vector) else [])


def finish(read, base, smooth):
    def trial(f, rate):
        v = read(f, 0, 64).astype(f32)
        if base is None:
            now = v - TIME_STEP * rate
        else:
            now = 0.5 * (base(f).astype(f32) + v - TIME_STEP * rate)
        return dot(smooth, now.astype(bf16))

    return trial


def with_traces(filter_matrix, pick):
    return jnp.concatenate([filter_matrix, dot(pick, filter_matrix).astype(bf16)], axis=0)


def mix_traces(read, pick, own):
    def run():
        for f in range(FIELDS):
            own[f] = dot(pick, read(f, 0, 64)).astype(bf16)

    return [run]


def place(pair):
    return slice(pair * PAIR, (pair + 1) * PAIR)


def lower_pair(v_ref, edge, pair):
    def lower(f):
        if pair:
            return v_ref[f, 48:64, pair * PAIR - CELLS : (pair + 1) * PAIR - CELLS].astype(f32)
        return jnp.concatenate([edge(f), v_ref[f, 48:64, 0:CELLS].astype(f32)], axis=1)

    return lower


def upper_pair(v_ref, above, pair):
    first = pair * PAIR + CELLS
    last_rans = lax.axis_index("rans") == lax.axis_size("rans") - 1

    def upper(f):
        if pair < EX // 2 - 1:
            return v_ref[f, 0:16, first : first + PAIR].astype(f32)
        edge = jnp.where(
            last_rans, v_ref[f, 48:64, first : first + CELLS].astype(f32), above(f)
        )
        return jnp.concatenate([v_ref[f, 0:16, first : first + CELLS].astype(f32), edge], axis=1)

    return upper


def phase_one_kernel(
    v_ref, from_core_ref, from_chip_ref, near_ref, far_ref, pin_ref, jacobian_any, volume_ref, lift_ref,
    wall_ref, filter_ref,
    out_ref, out_trace_ref, core_ref, chip_ref, pitch_ref, span_ref, mixed, own, weights_held,
    span_held, coefs, sem,
):
    load = pltpu.make_async_copy(jacobian_any, coefs, sem)
    load.start()
    first_span = lax.axis_index("span") == 0
    lane = lanes()
    pick = trace_selector()
    smooth = with_traces(filter_ref[...], pick)
    weights = fill(
        weights_held, [volume_ref[0], volume_ref[1], volume_ref[2], lift_ref[...], wall_ref[...]]
    )
    span_held[...] = jnp.zeros_like(span_held)
    below, above = from_below(from_core_ref, from_chip_ref), from_above(from_core_ref, from_chip_ref)
    vector, matrix = [], []

    def add(pair):
        at = place(pair)
        rows, held = mixed.at[pair % 2], own.at[pair % 2]

        def read(f, r0, r1):
            return v_ref[f, r0:r1, at]

        def store(f, value):
            out_ref[f, :, at] = value[0:64].astype(bf16)
            trace = value[64:128]
            out_trace_ref[f, :, at] = trace.astype(bf16)
            pack_field(f, trace, pair, first_span, lane, pitch_ref, span_held)

        vector.append(
            mix_traces(read, pick, held)
            + mix_fluxes(read, coefs, rows)
            + mix_stream(
                read,
                lower_pair(v_ref, below, pair),
                upper_pair(v_ref, above, pair),
                coefs, rows, 192,
            )
            + mix_sides(
                lambda f, r0, r1: held[f, r0:r1].astype(f32),
                lambda f: near_ref[f, :, pair * CELLS : (pair + 1) * CELLS].astype(f32),
                lambda f: far_ref[f].astype(f32),
                [2 * pair, 2 * pair + 1], coefs, rows, 224, first_span, lane,
            )
            + mix_wall(read, lambda: pin_ref[:, at].astype(f32), rows, 288)
        )
        matrix.append(
            staggered([lambda f, _: dot(weights, rows[f]), finish(read, None, smooth), store])
        )

    for pair in range(EX // 2):
        add(pair)
    load.wait()
    pipeline(vector, matrix)
    span_ref[...] = span_held[...].astype(bf16)
    store_stream(
        out_ref[:, 48:64, (EX - 1) * CELLS :], out_ref[:, 0:16, 0:CELLS], core_ref, chip_ref
    )


def inner_two_kernel(
    v_ref, jacobian_any, volume_ref, part_ref, mixed, weights_held, coefs, sem
):
    load = pltpu.make_async_copy(jacobian_any, coefs, sem)
    load.start()
    weights = fill(weights_held, [volume_ref[d] for d in range(3)])
    vector, matrix = [], []

    def add(pair):
        at = place(pair)
        rows = mixed.at[pair % 2]

        def store(f, value):
            part_ref[f, :, at] = value

        vector.append(mix_fluxes(lambda f, r0, r1: v_ref[f, r0:r1, at], coefs, rows))
        matrix.append(staggered([lambda f, _: dot(weights, rows[f]), store]))

    for pair in range(EX // 2):
        add(pair)
    load.wait()
    pipeline(vector, matrix)


def outer_two_kernel(
    v_ref, trace_ref, base_ref, part_ref, mean_ref, amp_ref, plane_ref, from_core_ref, from_chip_ref,
    near_ref, far_ref, pin_ref, jacobian_any, lift_ref, wall_ref, smooth_ref, out_ref, mixed,
    weights_held, coefs, sem,
):
    load = pltpu.make_async_copy(jacobian_any, coefs, sem)
    load.start()
    first_span = lax.axis_index("span") == 0
    first_rans = lax.axis_index("rans") == 0
    lane = lanes()
    weights, smooth = fill(weights_held, [lift_ref[...], wall_ref[...]]), smooth_ref[...]
    below, above = from_below(from_core_ref, from_chip_ref), from_above(from_core_ref, from_chip_ref)
    vector, matrix = [], []

    def edge(f):
        return jnp.where(first_rans, inflow_of(mean_ref, amp_ref, plane_ref)(f), below(f))

    def add(pair):
        at = place(pair)
        rows = mixed.at[pair % 2]

        def read(f, r0, r1):
            return v_ref[f, r0:r1, at]

        def store(f, value):
            out_ref[f, :, at] = value.astype(bf16)

        vector.append(
            mix_stream(
                read, lower_pair(v_ref, edge, pair), upper_pair(v_ref, above, pair), coefs, rows, 0
            )
            + mix_sides(
                lambda f, r0, r1: trace_ref[f, r0:r1, at].astype(f32),
                lambda f: near_ref[f, :, pair * CELLS : (pair + 1) * CELLS].astype(f32),
                lambda f: far_ref[f].astype(f32),
                [2 * pair, 2 * pair + 1], coefs, rows, 32, first_span, lane,
            )
            + mix_wall(read, lambda: pin_ref[:, at].astype(f32), rows, 96)
        )
        matrix.append(
            staggered([
                lambda f, _: dot(weights, rows[f]) + part_ref[f, :, at],
                finish(read, lambda f: base_ref[f, :, at], smooth),
                store,
            ])
        )

    for pair in range(EX // 2):
        add(pair)
    load.wait()
    pipeline(vector, matrix)


def inflow_of(mean_ref, amp_ref, plane_ref):
    return lambda f: mean_ref[f] + amp_ref[f] * plane_ref[f]


def inflow_kernel(
    held_any, held_trace_any, held_pitch_any, held_span_any, v_ref, mean_ref, amp_ref, plane_ref,
    near_ref, far_ref, pin_ref, jacobian_any, volume_ref, lift_ref, wall_ref, filter_ref, out_any,
    out_trace_any, pitch_any, span_any, mixed, own, weights_held, edge, edge_trace, edge_pitch,
    edge_span, coefs, sems,
):
    first_span = lax.axis_index("span") == 0
    lane = lanes()
    layer = slice(0, CELLS)

    @pl.when(lax.axis_index("rans") == 0)
    def _():
        loads = [
            pltpu.make_async_copy(held_pitch_any.at[:, :, layer], edge_pitch, sems.at[0]),
            pltpu.make_async_copy(held_span_any, edge_span, sems.at[1]),
            pltpu.make_async_copy(jacobian_any, coefs, sems.at[6]),
        ]
        for copy in loads:
            copy.start()
        pick = trace_selector()
        smooth = with_traces(filter_ref[...], pick)
        weights = fill(
            weights_held, [volume_ref[0], volume_ref[1], volume_ref[2], lift_ref[...], wall_ref[...]]
        )

        def read(f, r0, r1):
            return v_ref[f, r0:r1, layer]

        def store(f, value):
            edge[f] = value[0:64].astype(bf16)
            t = value[64:128]
            edge_trace[f] = t.astype(bf16)
            pitch = jnp.where(lane < 32, t[0:16], pltpu.roll(t[16:32], 96, 1))
            edge_pitch[f] = jnp.where(
                (lane & 63) < 32, pitch, edge_pitch[f].astype(f32)
            ).astype(bf16)
            edge_span[f] = pack_span(
                edge_span[f].astype(f32), t[32:48], t[48:64], 0, first_span, lane
            ).astype(bf16)

        vector = (
            mix_traces(read, pick, own)
            + mix_stream(
                read,
                inflow_of(mean_ref, amp_ref, plane_ref),
                lambda f: v_ref[f, 0:16, CELLS:PAIR].astype(f32),
                coefs, mixed, 192,
            )
            + mix_sides(
                lambda f, r0, r1: own[f, r0:r1].astype(f32),
                lambda f: near_ref[f, :, layer].astype(f32),
                lambda f: far_ref[f].astype(f32),
                [0], coefs, mixed, 224, first_span, lane,
            )
            + mix_fluxes(read, coefs, mixed)
            + mix_wall(read, lambda: pin_ref[:, layer].astype(f32), mixed, 288)
        )
        for copy in loads:
            copy.wait()
        for step in vector:
            step()
        for step in staggered(
            [lambda f, _: dot(weights, mixed[f]), finish(read, None, smooth), store]
        ):
            step()
        stores = [
            pltpu.make_async_copy(edge, out_any.at[:, :, layer], sems.at[2]),
            pltpu.make_async_copy(edge_trace, out_trace_any.at[:, :, layer], sems.at[3]),
            pltpu.make_async_copy(edge_pitch, pitch_any.at[:, :, layer], sems.at[4]),
            pltpu.make_async_copy(edge_span, span_any, sems.at[5]),
        ]
        for copy in stores:
            copy.start()
        for copy in stores:
            copy.wait()


VMEM = pl.BlockSpec(memory_space=pltpu.VMEM)
ANY = pl.BlockSpec(memory_space=pl.ANY)
PARAMS = pltpu.CompilerParams(vmem_limit_bytes=40 * 2**20)


def shape_of(*dims, dtype=bf16):
    return jax.ShapeDtypeStruct(dims, dtype)


def cost(us):
    return pl.CostEstimate(flops=int(us * 1e8), bytes_accessed=int(us * 3e6), transcendentals=0)


def body(
    solution, volume_ops, flux_jacobian, lift_matrix, filter_matrix, wall_matrix, pinched_map,
    mode_rows, mode_seeds, mode_shape, mean_inflow, eddy_amplitude,
):
    ranks = lax.axis_size("rans")
    eddies, foot = mode_shape.shape[2:]
    plane_rows = mean_inflow.shape[3]
    faces = shape_of(FIELDS, 16, CELLS)
    def slab(z, y, core):
        return 8 * z + 2 * y + core

    columns = ranks // 8
    root_y = [0] + [1] * (columns - 1)
    first_level = [
        [
            (slab(z, [y for y in range(4) if y != root_y[z]][turn], core), slab(z, root_y[z], core))
            for z in range(columns)
            for core in range(2)
        ]
        for turn in range(3)
    ]
    second_level = [
        [
            (slab(z + up, root_y[z + up], core), slab(z, root_y[z], 0))
            for z in range(0, columns, 2)
        ]
        for up, core in ((0, 1), (1, 0), (1, 1))
    ]
    third_level = [[(slab(z, root_y[z], 0), 0)] for z in (2, 6, 4)]

    def gather_sum(value, level, own=None):
        parts = [lax.ppermute(value, "rans", pairs) for pairs in level]
        value = value if own is None else own
        for part in parts:
            value = value + part
        return value

    jacobian = flux_jacobian.transpose(1, 0, 2)
    jacobian_scratch = [pltpu.SMEM(jacobian.shape, f32), pltpu.SemaphoreType.DMA(())]
    pins = pinched_map.reshape(1, -1)
    elements = solution.shape[2]
    traces = shape_of(FIELDS, NODES, elements)
    sends = (faces, faces, shape_of(FIELDS, 16, EX // 2 * CELLS), faces)
    swap = [(0, 1), (1, 0)]
    same_chip = [(i, i ^ 1) for i in range(ranks)]
    next_chip = [(a + 1, b + 1) for a, b in same_chip if max(a, b) + 1 < ranks]

    span_scratch = pltpu.VMEM((FIELDS, 16, CELLS), f32)
    plane = pl.pallas_call(
        functools.partial(
            plane_kernel, normalizer=float((plane_rows / (eddies * ranks * foot)) ** 0.5)
        ),
        out_shape=shape_of(FIELDS, 16, CELLS, dtype=f32),
        in_specs=[pl.BlockSpec(memory_space=pltpu.HBM)] * 3,
        out_specs=VMEM,
        scratch_shapes=[
            pltpu.VMEM((foot, eddies), jnp.int32),
            pltpu.VMEM((1, eddies), jnp.int32),
            pltpu.VMEM((foot, eddies), f32),
            pltpu.SemaphoreType.DMA((3,)),
        ],
        compiler_params=pltpu.CompilerParams(vmem_limit_bytes=60 * 2**20),
        cost_estimate=cost(4),
        name="eddy_plane",
    )(mode_rows[0, 0].T, mode_seeds.reshape(1, eddies), mode_shape[0, 0].T)
    held_plane, core, chip, pitch, span = pl.pallas_call(
        pack_kernel,
        out_shape=(shape_of(FIELDS, 16, CELLS, dtype=f32),) + sends,
        in_specs=[VMEM] * 2,
        out_specs=(VMEM,) * 5,
        scratch_shapes=[span_scratch],
        compiler_params=PARAMS,
        cost_estimate=cost(1),
        name="pack_faces",
    )(plane, solution)
    plane = gather_sum(plane, first_level, held_plane)
    near = lax.ppermute(pitch, "pitch", swap)
    plane, chip, core, span = lax.optimization_barrier((plane, chip, core, span))
    plane = gather_sum(plane, second_level)
    from_chip = lax.ppermute(chip, "rans", next_chip)
    core, span, near = lax.optimization_barrier((core, span, near))
    far = lax.ppermute(span, "span", swap)
    from_core = lax.ppermute(core, "rans", same_chip)
    plane, near, far, from_core = lax.optimization_barrier((plane, near, far, from_core))
    plane = gather_sum(plane, third_level)

    phase_one, trace_one, core, chip, pitch, span = pl.pallas_call(
        phase_one_kernel,
        out_shape=(traces, traces) + sends,
        in_specs=[VMEM] * 6 + [ANY] + [VMEM] * 4,
        out_specs=(VMEM,) * 6,
        scratch_shapes=[
            pltpu.VMEM((2, FIELDS, MIXED, PAIR), bf16),
            pltpu.VMEM((2, FIELDS, NODES, PAIR), bf16),
            pltpu.VMEM((NODES, MIXED), bf16),
            span_scratch,
            *jacobian_scratch,
        ],
        compiler_params=PARAMS,
        cost_estimate=cost(6),
        name="phase_one",
    )(
        solution, from_core, from_chip, near, far, pins, jacobian, volume_ops, lift_matrix, wall_matrix,
        filter_matrix,
    )
    from_core = lax.ppermute(core, "rans", same_chip)
    from_chip = lax.ppermute(chip, "rans", next_chip)
    plane, from_core = lax.optimization_barrier((plane, from_core))

    mean = mean_inflow.reshape(FIELDS, 16, CELLS)
    amplitude = eddy_amplitude.reshape(FIELDS, 16, CELLS)
    phase_one, trace_one, pitch, span = pl.pallas_call(
        inflow_kernel,
        out_shape=(traces, traces, sends[2], sends[3]),
        in_specs=[ANY] * 4 + [VMEM] * 7 + [ANY] + [VMEM] * 4,
        out_specs=(ANY,) * 4,
        scratch_shapes=[
            pltpu.VMEM((FIELDS, MIXED, CELLS), bf16),
            pltpu.VMEM((FIELDS, NODES, CELLS), bf16),
            pltpu.VMEM((NODES, MIXED), bf16),
            pltpu.VMEM((FIELDS, NODES, CELLS), bf16),
            pltpu.VMEM((FIELDS, NODES, CELLS), bf16),
            pltpu.VMEM((FIELDS, 16, CELLS), bf16),
            pltpu.VMEM((FIELDS, 16, CELLS), bf16),
            jacobian_scratch[0],
            pltpu.SemaphoreType.DMA((7,)),
        ],
        input_output_aliases={0: 0, 1: 1, 2: 2, 3: 3},
        compiler_params=PARAMS,
        cost_estimate=cost(0.1),
        name="inflow_layer",
    )(
        phase_one, trace_one, pitch, span, solution, mean, amplitude, plane, near, far, pins,
        jacobian, volume_ops, lift_matrix, wall_matrix, filter_matrix,
    )
    near = lax.ppermute(pitch, "pitch", swap)
    far = lax.ppermute(span, "span", swap)
    part = pl.pallas_call(
        inner_two_kernel,
        out_shape=shape_of(FIELDS, NODES, elements, dtype=f32),
        in_specs=[VMEM, ANY, VMEM],
        out_specs=VMEM,
        scratch_shapes=[
            pltpu.VMEM((2, FIELDS, INNER, PAIR), bf16), pltpu.VMEM((NODES, INNER), bf16),
            *jacobian_scratch,
        ],
        compiler_params=PARAMS,
        cost_estimate=cost(0.1),
        name="inner_two",
    )(phase_one, jacobian, volume_ops)
    return pl.pallas_call(
        outer_two_kernel,
        out_shape=traces,
        in_specs=[VMEM] * 12 + [ANY] + [VMEM] * 3,
        out_specs=VMEM,
        scratch_shapes=[
            pltpu.VMEM((2, FIELDS, MIXED - INNER, PAIR), bf16),
            pltpu.VMEM((NODES, MIXED - INNER), bf16),
            *jacobian_scratch,
        ],
        compiler_params=PARAMS,
        cost_estimate=cost(4),
        name="outer_two",
    )(
        phase_one, trace_one, solution, part, mean, amplitude, plane, from_core, from_chip, near, far,
        pins, jacobian, lift_matrix, wall_matrix, filter_matrix,
    )


def solution(mesh):
    spread = P(None, None, ("rans", "pitch", "span"))
    in_specs = (
        spread,
        P(),
        P(),
        P(),
        P(),
        P(),
        P(("rans", "pitch", "span")),
        P("pitch", "span", "rans", None),
        P("pitch", "span", "rans"),
        P("pitch", "span", "rans", None),
        P("pitch", "span", None, None),
        P("pitch", "span", None, None),
    )
    return jax.shard_map(body, mesh=mesh, in_specs=in_specs, out_specs=spread, check_vma=False)
```
